32 devices in a mesh: section: 2 (over core), dp: 16 (over z, y, x).
Axes of the slice: x: 2, y: 2, z: 4, core: 2. Of those that a mesh axis runs over, the one named last changes fastest.
Arguments:
- inputs: bfloat16 [32768, 768], P('dp'), may hold values from -6 to 6
- out_grad: bfloat16 [32768, 768], P('dp'), may hold values from -6 to 6
- picks: int32 [32, 128], P('dp'), may hold values from 0 to 1023, as said below
- valid: int32 [32, 128], P('dp'), may hold values from 0 to 1, as said below
- router: float32 [768], replicated, may hold values from -0.21875 to 0.21875
- gain_attn: float32 [2, 768], P('section'), may hold values from 0.1 to 1.9
- w_qkv: bfloat16 [2, 768, 2304], P('section'), may hold values from -0.21875 to 0.21875
- w_out: bfloat16 [2, 768, 768], P('section'), may hold values from -0.875 to 0.875
- gain_mlp: float32 [2, 768], P('section'), may hold values from 0.1 to 1.9
- w_in: bfloat16 [2, 768, 3072], P('section'), may hold values from -0.21875 to 0.21875
- w_back: bfloat16 [2, 3072, 768], P('section'), may hold values from -0.109375 to 0.109375
Outputs:
- block_ends: bfloat16 [2, 32768, 768], P('section', 'dp')
- router_grad: float32 [768], replicated
- gain_attn_grad: float32 [2, 768], P('section', 'dp')
- w_qkv_grad: float32 [2, 768, 2304], P('section', 'dp')
- w_out_grad: float32 [2, 768, 768], P('section', 'dp')
- gain_mlp_grad: float32 [2, 768], P('section', 'dp')
- w_in_grad: float32 [2, 768, 3072], P('section', 'dp')
- w_back_grad: float32 [2, 3072, 768], P('section', 'dp')
The draws below stay inside these ranges and needn't reach their ends.
Inputs may be any that keep to these rules, and one draw needn't show every extreme that they name: `picks`: each row holds 128 different positions of its sequence, in increasing order. `valid`: each row has between 32 and 128 slots equal to 1; some row has all 128.
All inputs are finite; a program needn't handle non-finite values.
Results may differ from the reference program's by a relative error of at most 0.02.
Values may be sent and summed in bfloat16 or wider, within the bound.
No kernel may reach another device: no remote copies, remote signals or barrier semaphores. Data moves between devices by JAX's collectives and lax.ppermute only.
A program may use at most 384 MiB of HBM per device.

```python
import jax
import jax.numpy as jnp
from jax import lax

D = 768
FF = 3072
HEADS = 12
HEAD_DIM = 64
SEQ_LEN = 1024
CAP = 128
TOKENS = 32768


def draw_picks(key, part):
    key = jax.random.fold_in(key, 11)
    seq_keys = jax.random.split(key, TOKENS // SEQ_LEN)

    def one_sequence(seq_key):
        return jnp.sort(jax.random.permutation(seq_key, SEQ_LEN)[:CAP])
    return jax.vmap(one_sequence)(seq_keys).astype(jnp.int32)


def draw_valid(key, part):
    key = jax.random.fold_in(key, 23)
    count_key, rank_key = jax.random.split(key)
    seq_count = TOKENS // SEQ_LEN
    spread_draw = jax.random.randint(count_key, (seq_count,), 0, CAP)
    counts = CAP - 3 * spread_draw * spread_draw // (4 * CAP)
    counts = counts.at[0].set(CAP)
    slot_ranks = jax.vmap(lambda rank_seed: jax.random.permutation(rank_seed, CAP))(jax.random.split(rank_key, seq_count))
    return (slot_ranks < counts[:, None]).astype(jnp.int32)


def block_levels(key, dims, shards, low, largest):
    factor_of = 1.0
    for position, parts in shards:
        draws = jax.random.uniform(jax.random.fold_in(jax.random.fold_in(key, 6), position), (parts,), jnp.float32, low / len(shards), largest / len(shards))
        factor_of = factor_of * jnp.repeat(jnp.exp(draws), dims[position] // parts).reshape((-1,) + (1,) * (len(dims) - 1 - position))
    return factor_of


def centred(own_key, dims, width, reach, shards=(), dtype=jnp.bfloat16):
    values = width * jax.random.normal(own_key, dims, jnp.float32)
    if shards:
        values = values * block_levels(own_key, dims, shards, -0.22, 0.18)
    return jnp.clip(values, -reach, reach).astype(dtype)


def setup_inputs(seed: int = 0) -> dict:
    streams_of = jax.random.split(jax.random.key(seed), 12)
    inputs = centred(streams_of[0], (TOKENS, D), 1.0, 6.0, ((0, 16),))
    out_grad = centred(streams_of[1], (TOKENS, D), 1.0, 6.0, ((0, 16),))
    picks = draw_picks(jax.random.fold_in(streams_of[11], 71), 0)
    valid = draw_valid(jax.random.fold_in(streams_of[11], 71), 0)
    router = centred(streams_of[4], (D,), D ** -0.5, 0.21875, (), jnp.float32)
    gain_attn = jnp.clip(1.0 + 0.18 * jax.random.normal(streams_of[5], (2, D), jnp.float32), 0.1, 1.9)
    w_qkv = centred(streams_of[6], (2, D, 3 * D), D ** -0.5, 0.21875, ((0, 2),))
    w_out = centred(streams_of[7], (2, D, D), (D // 16) ** -0.5, 0.875, ((0, 2),))
    gain_mlp = jnp.clip(1.0 + 0.18 * jax.random.normal(streams_of[8], (2, D), jnp.float32), 0.1, 1.9)
    w_in = centred(streams_of[9], (2, D, FF), D ** -0.5, 0.21875, ((0, 2),))
    w_back = centred(streams_of[10], (2, FF, D), FF ** -0.5, 0.109375, ((0, 2),))
    return {"inputs": inputs, "out_grad": out_grad, "picks": picks, "valid": valid, "router": router, "gain_attn": gain_attn, "w_qkv": w_qkv, "w_out": w_out, "gain_mlp": gain_mlp, "w_in": w_in, "w_back": w_back}


highest = lax.Precision.HIGHEST
eps = 1e-06

@jax.custom_vjp
def low(v):
    return lax.optimization_barrier(v.astype(jnp.bfloat16)).astype(jnp.float32)

@jax.custom_vjp
def low_back(v):
    return v

def low_keep(v):
    return (low(v), None)

def low_pass(kept, grad):
    return (grad,)

def back_keep(v):
    return (v, None)

def back_low(kept, grad):
    return (low(grad),)
low.defvjp(low_keep, low_pass)
low_back.defvjp(back_keep, back_low)

def norm_rows(row_data, gain):
    return row_data * lax.rsqrt(lax.optimization_barrier(jnp.mean(row_data * row_data, axis=-1, keepdims=True)) + eps) * gain

def attention(normed, w_qkv, w_out, allowed):
    row_count = normed.shape[0]
    packed = low(low_back(jnp.dot(low(normed), w_qkv, precision=highest)))
    packed = packed.reshape(row_count, 3, HEADS, HEAD_DIM)
    scores = jnp.einsum('qhd,khd->hqk', packed[:, 0], packed[:, 1], precision=highest) * HEAD_DIM ** (-0.5)
    scores = jnp.where(allowed[None], low_back(scores), -1e+30)
    attn_probs = jax.nn.softmax(scores, axis=-1)
    mixed_heads = jnp.einsum('hqk,khd->qhd', low(attn_probs), packed[:, 2], precision=highest)
    mixed_heads = low(low_back(mixed_heads.reshape(row_count, HEADS * HEAD_DIM)))
    return low_back(jnp.dot(mixed_heads, w_out, precision=highest))

def feed_forward(normed_mid, w_in, w_back):
    hidden_pre = low_back(jnp.dot(low(normed_mid), w_in, precision=highest))
    hidden_act = low(jax.nn.gelu(hidden_pre))
    return low_back(jnp.dot(hidden_act, w_back, precision=highest))

def block(row_data, layer, allowed):
    gain_attn, w_qkv, w_out, gain_mlp, w_in, w_back = layer
    attn_out = attention(norm_rows(row_data, gain_attn), w_qkv, w_out, allowed)
    middle_rows = row_data + attn_out
    return attn_out + feed_forward(norm_rows(middle_rows, gain_mlp), w_in, w_back)

def forward(seq_rows, seq_picks, seq_valid, params):
    router, gain_attn, w_qkv, w_out, gain_mlp, w_in, w_back = params
    first = (gain_attn[0], w_qkv[0], w_out[0], gain_mlp[0], w_in[0], w_back[0])
    second = (gain_attn[1], w_qkv[1], w_out[1], gain_mlp[1], w_in[1], w_back[1])
    chosen = seq_rows[seq_picks]
    slot_ids = jnp.arange(CAP)
    usable = (seq_valid[None, :] > 0) | (slot_ids[None, :] == slot_ids[:, None])
    allowed = (seq_picks[None, :] <= seq_picks[:, None]) & usable
    gates = jax.nn.sigmoid(jnp.dot(chosen, router, precision=highest))
    slot_mask = seq_valid.astype(jnp.float32)
    delta = low((gates * slot_mask)[:, None] * block(chosen, first, allowed))
    middle = low_back(seq_rows.at[seq_picks].add(delta))
    places = jnp.arange(SEQ_LEN)
    return middle + block(middle, second, places[None, :] <= places[:, None])

def reference(inputs, out_grad, picks, valid, router, gain_attn, w_qkv, w_out, gain_mlp, w_in, w_back):
    params = (router.astype(jnp.float32), gain_attn.astype(jnp.float32), w_qkv.astype(jnp.float32), w_out.astype(jnp.float32), gain_mlp.astype(jnp.float32), w_in.astype(jnp.float32), w_back.astype(jnp.float32))
    seq_count = inputs.shape[0] // SEQ_LEN
    seq_inputs = inputs.astype(jnp.float32).reshape(seq_count, SEQ_LEN, D)
    seq_cots = out_grad.astype(jnp.float32).reshape(seq_count, SEQ_LEN, D)

    def per_sequence(totals, item):
        seq_rows, seq_cot, seq_picks, seq_valid = item

        def run(row_data, weights):
            return forward(row_data, seq_picks, seq_valid, weights)
        result, pull = jax.vjp(run, seq_rows, params)
        grad_rows, grad_params = pull(seq_cot)
        totals = jax.tree.map(jnp.add, totals, grad_params)
        return (totals, (result, grad_rows))
    start_totals = jax.tree.map(jnp.zeros_like, params)
    totals, outputs = lax.scan(per_sequence, start_totals, (seq_inputs, seq_cots, picks, valid))
    results, grad_rows = outputs
    block_ends = jnp.stack([grad_rows.reshape(-1, D), results.reshape(-1, D)]).astype(jnp.bfloat16)
    return (block_ends, totals[0], totals[1], totals[2], totals[3], totals[4], totals[5], totals[6])
```

```python
import functools

import jax
import jax.numpy as jnp
from jax import lax
from jax.experimental import pallas as pl
from jax.experimental.pallas import tpu as pltpu
from jax.sharding import PartitionSpec as P

HEADS = 12
HEAD_DIM = 64
LANES = 128
PAIRS = HEADS * HEAD_DIM // LANES
EPS = 1e-06
FACTOR = HEAD_DIM ** (-0.5)
PIECES = 16
STAGES = 4
TILE = 256
VMEM_BYTES = 56 * 1024 * 1024
BF16 = jnp.bfloat16
F32 = jnp.float32


def nn(a, b):
    return lax.dot_general(a, b, (((1,), (0,)), ((), ())), preferred_element_type=F32)


def nt(a, b):
    return lax.dot_general(a, b, (((1,), (1,)), ((), ())), preferred_element_type=F32)


def tn(a, b):
    return lax.dot_general(a, b, (((0,), (0,)), ((), ())), preferred_element_type=F32)


def shape(dims, dtype):
    return jax.ShapeDtypeStruct(dims, dtype)


def whole(dims):
    zeros = (0,) * len(dims)
    return pl.BlockSpec(dims, lambda *_: zeros)


ANY = pl.BlockSpec(memory_space=pl.ANY)


def run(body, info, ins, outs, grid, scratch=(), flops=0, moved=0):
    arrays, in_specs = zip(*ins)
    shapes, out_specs = zip(*outs)
    return pl.pallas_call(
        body,
        out_shape=shapes,
        grid_spec=pltpu.PrefetchScalarGridSpec(
            num_scalar_prefetch=1,
            grid=grid,
            in_specs=in_specs,
            out_specs=out_specs,
            scratch_shapes=scratch,
        ),
        compiler_params=pltpu.CompilerParams(
            vmem_limit_bytes=VMEM_BYTES, dimension_semantics=("arbitrary",) * len(grid)
        ),
        cost_estimate=pl.CostEstimate(flops=flops, bytes_accessed=moved, transcendentals=0),
    )(info, *arrays)


def lane_head(rows, which):
    lane = lax.broadcasted_iota(jnp.int32, (rows, LANES), 1)
    return (lane < HEAD_DIM) if which == 0 else (lane >= HEAD_DIM)


def head_only(value, which):
    return jnp.where(lane_head(value.shape[0], which), value, jnp.zeros_like(value))


def mean_square_scale(rows):
    return lax.rsqrt(jnp.mean(rows * rows, axis=-1, keepdims=True) + EPS)


def norm_back(grad, rows, scale, gain):
    hat = rows * scale
    scaled = grad * gain
    back = scale * (scaled - hat * jnp.mean(scaled * hat, axis=-1, keepdims=True))
    return back, jnp.sum(grad * hat, axis=0, keepdims=True)


def gelu_parts(pre):
    root = 0.7978845608028654
    square = pre * pre
    bent = jnp.tanh(root * pre * (1.0 + 0.044715 * square))
    half = 0.5 * (1.0 + bent)
    slope = half + 0.5 * pre * (1.0 - bent * bent) * (root * (1.0 + 0.134145 * square))
    return pre * half, slope


def fetch(info, local, remote, buf, sem):
    @pl.when(info[0] == 1)
    def _():
        pltpu.make_async_copy(local, buf, sem).start()

    @pl.when(info[0] == 0)
    def _():
        pltpu.make_async_copy(remote, buf, sem).start()


def arrived(source, buf, sem):
    pltpu.make_async_copy(source, buf, sem).wait()


def small_attention(packed, seq, pair, allowed):
    cap = allowed.shape[0]
    rows = slice(seq * cap, (seq + 1) * cap)
    width = HEADS * HEAD_DIM
    first = pair * LANES
    queries = packed[rows, first : first + LANES] * BF16(FACTOR)
    keys = packed[rows, width + first : width + first + LANES]
    values = packed[rows, 2 * width + first : 2 * width + first + LANES]
    probs = []
    for head in range(2):
        scores = nt(head_only(queries, head), keys)
        scores = jnp.where(allowed, scores, -1e30)
        top = jnp.max(scores, axis=-1, keepdims=True)
        grown = jnp.exp(scores - top)
        probs.append(grown / jnp.sum(grown, axis=-1, keepdims=True))
    return queries, keys, values, probs


def slot_rule(valid_row, cap):
    query = lax.broadcasted_iota(jnp.int32, (cap, cap), 0)
    key = lax.broadcasted_iota(jnp.int32, (cap, cap), 1)
    return (key <= query) & ((valid_row > 0) | (key == query))


def routed_forward_body(
    info, x, pick_col, valid_row, valid_col, router, gain_attn, gain_mlp, w_qkv, w_out, w_in, w_back,
    chosen_o, normed_o, packed_o, mixed_o, rows_o, mid_o, act_o, slope_o, branch_o, gate_o, delta_o,
    b_qkv, b_out, b_in, b_back, sems,
):
    @pl.when(info[0] == 0)
    def _():
        copies = [
            pltpu.make_async_copy(source, buf, sems.at[n])
            for n, (source, buf) in enumerate(
                ((w_qkv, b_qkv), (w_out, b_out), (w_in, b_in), (w_back, b_back))
            )
        ]
        for copy in copies:
            copy.start()
        seqs, cap = valid_row.shape
        seq_len = x.shape[0] // seqs
        parts = []
        for seq in range(seqs):
            place = lax.broadcasted_iota(jnp.int32, (cap, seq_len), 1)
            hot = (pick_col[seq * cap : (seq + 1) * cap, :] == place).astype(BF16)
            parts.append(nn(hot, x[seq * seq_len : (seq + 1) * seq_len, :]))
        chosen = jnp.concatenate(parts, axis=0)
        chosen_o[...] = chosen.astype(BF16)
        gates = jax.nn.sigmoid(jnp.sum(chosen * router[...], axis=-1, keepdims=True))
        gate_o[...] = jnp.broadcast_to(gates, gate_o.shape)
        normed = (chosen * mean_square_scale(chosen) * gain_attn[...]).astype(BF16)
        normed_o[...] = normed
        copies[0].wait()
        packed_o[...] = nn(normed, b_qkv[...]).astype(BF16)
        for seq in range(seqs):
            allowed = slot_rule(valid_row[seq : seq + 1, :], cap)
            for pair in range(PAIRS):
                _, _, values, probs = small_attention(packed_o, seq, pair, allowed)
                mixed = sum(nn(probs[h].astype(BF16), head_only(values, h)) for h in range(2))
                mixed_o[seq * cap : (seq + 1) * cap, pair * LANES : (pair + 1) * LANES] = (
                    mixed.astype(BF16)
                )
        copies[1].wait()
        attn_out = nn(mixed_o[...], b_out[...])
        rows = chosen + attn_out
        rows_o[...] = rows
        normed_mid = (rows * mean_square_scale(rows) * gain_mlp[...]).astype(BF16)
        mid_o[...] = normed_mid
        copies[2].wait()
        copies[3].wait()
        hidden = b_in.shape[1]
        step = 768
        for first in range(0, hidden, step):
            cols = slice(first, first + step)
            act, slope = gelu_parts(nn(normed_mid, b_in[:, cols]))
            act = act.astype(BF16)
            act_o[:, cols] = act
            slope_o[:, cols] = slope.astype(BF16)
        branch = attn_out + nn(act_o[...], b_back[...])
        branch_o[...] = branch
        delta_o[...] = (gates * valid_col[...].astype(F32) * branch).astype(BF16)


def routed_backward_body(
    info, g_sel, chosen_i, packed, rows_i, slope, branch, gate, valid_row, valid_col, router, gain_attn, gain_mlp,
    w_qkv, w_out, w_in, w_back,
    ffn_o, hidden_o, attn_o, packed_o, chosen_o, small_o,
    b_qkv, b_out, b_in, b_back, sems,
):
    @pl.when(info[0] == 0)
    def _():
        copies = [
            pltpu.make_async_copy(source, buf, sems.at[n])
            for n, (source, buf) in enumerate(
                ((w_qkv, b_qkv), (w_out, b_out), (w_in, b_in), (w_back, b_back))
            )
        ]
        for n in (3, 2, 1, 0):
            copies[n].start()
        seqs, cap = valid_row.shape
        chosen = chosen_i[...].astype(F32)
        grad_sel = g_sel[...].astype(F32)
        gates = gate[:, 0:1]
        mask = valid_col[...].astype(F32)
        logit = jnp.sum(grad_sel * branch[...], axis=-1, keepdims=True) * mask * gates * (1.0 - gates)
        grad = grad_sel * (gates * mask)
        grad_ffn = grad.astype(BF16)
        ffn_o[...] = grad_ffn
        copies[3].wait()
        copies[2].wait()
        step = 768
        for first in range(0, b_in.shape[1], step):
            cols = slice(first, first + step)
            hidden = (nt(grad_ffn, b_back[cols, :]) * slope[:, cols].astype(F32)).astype(BF16)
            hidden_o[:, cols] = hidden
        grad_mid = nt(hidden_o[...], b_in[...])
        rows = rows_i[...]
        grad_rows, gain_mlp_sum = norm_back(grad_mid, rows, mean_square_scale(rows), gain_mlp[...])
        grad_attn = (grad + grad_rows).astype(BF16)
        attn_o[...] = grad_attn
        copies[1].wait()
        grad_mixed = nt(grad_attn, b_out[...]).astype(BF16)
        for seq in range(seqs):
            at = slice(seq * cap, (seq + 1) * cap)
            allowed = slot_rule(valid_row[seq : seq + 1, :], cap)
            for pair in range(PAIRS):
                cols = slice(pair * LANES, (pair + 1) * LANES)
                queries, keys, values, probs = small_attention(packed, seq, pair, allowed)
                grads = grad_mixed[at, cols]
                dq = dk = dv = 0.0
                for head in range(2):
                    grad_head = head_only(grads, head)
                    grad_probs = nt(grad_head, values)
                    prob = probs[head]
                    inner = jnp.sum(prob * grad_probs, axis=-1, keepdims=True)
                    low = (prob * (grad_probs - inner)).astype(BF16)
                    dq = dq + nn(low, head_only(keys, head))
                    dk = dk + tn(low, head_only(queries, head))
                    dv = dv + tn(prob.astype(BF16), grad_head)
                packed_o[0, at, cols] = (dq * FACTOR).astype(BF16)
                packed_o[1, at, cols] = dk.astype(BF16)
                packed_o[2, at, cols] = dv.astype(BF16)
        copies[0].wait()
        width = chosen.shape[1]
        grad_normed = sum(
            nt(packed_o[n], b_qkv[:, n * width : (n + 1) * width]) for n in range(3)
        )
        back, gain_attn_sum = norm_back(grad_normed, chosen, mean_square_scale(chosen), gain_attn[...])
        chosen_o[...] = grad_rows + back + logit * router[...]
        small_o[...] = jnp.zeros(small_o.shape, F32)
        small_o[0:1, :] = jnp.sum(logit * chosen, axis=0, keepdims=True)
        small_o[1:2, :] = gain_mlp_sum
        small_o[2:3, :] = gain_attn_sum


def dense_in_body(info, x, delta, pick_row, gain, w_local, w_far, middle_o, normed_o, packed_o, b_qkv, sem):
    step = pl.program_id(0)

    @pl.when(step == 0)
    def _():
        fetch(info, w_local, w_far, b_qkv, sem)

    rows, width = x.shape
    cap = delta.shape[0]
    place = step * rows + lax.broadcasted_iota(jnp.int32, (rows, cap), 0)
    hot = (pick_row[...] == place).astype(BF16)
    middle = x[...].astype(F32) + nn(hot, delta[...])
    middle_o[...] = middle
    normed = (middle * mean_square_scale(middle) * gain[...]).astype(BF16)
    normed_o[...] = normed

    @pl.when(step == 0)
    def _():
        arrived(w_local, b_qkv, sem)

    for n in range(3):
        packed_o[n] = nn(normed, b_qkv[:, n * width : (n + 1) * width]).astype(BF16)


def attend_forward_body(info, packed, mixed_o, logsum_o):
    seq_len = packed.shape[1]
    queries = packed[0] * BF16(FACTOR)
    keys = packed[1]
    values = [head_only(packed[2], h) for h in range(2)]
    below = lax.broadcasted_iota(jnp.int32, (TILE, TILE), 1) <= lax.broadcasted_iota(
        jnp.int32, (TILE, TILE), 0
    )
    for block in range(seq_len // TILE):
        at = slice(block * TILE, (block + 1) * TILE)
        upto = (block + 1) * TILE
        total = 0.0
        sums = []
        for head in range(2):
            query = head_only(queries[at], head)
            last = jnp.where(below, nt(query, keys[at]), -1e30)
            scores = last
            if block:
                scores = jnp.concatenate([nt(query, keys[: block * TILE]), last], axis=1)
            top = jnp.max(scores, axis=-1, keepdims=True)
            grown = jnp.exp(scores - top)
            row_sum = jnp.sum(grown, axis=-1, keepdims=True)
            total = total + nn(grown.astype(BF16), values[head][:upto]) * (1.0 / row_sum)
            sums.append(top + jnp.log(row_sum))
        mixed_o[at, :] = total.astype(BF16)
        both = jnp.where(lane_head(TILE, 0), sums[0], sums[1])
        turned = jnp.transpose(both)
        logsum_o[0, 0:1, at] = turned[0:1]
        logsum_o[0, 1:2, at] = turned[HEAD_DIM : HEAD_DIM + 1]


def attend_backward_body(info, packed, grad, mixed, logsum, out, grad_q):
    seq_len = packed.shape[1]
    blocks = seq_len // TILE
    queries = packed[0] * BF16(FACTOR)
    queries = [head_only(queries, h) for h in range(2)]
    key_heads = [head_only(packed[1], h) for h in range(2)]
    grads = [head_only(grad[...], h) for h in range(2)]
    product = grad[...].astype(F32) * mixed[...].astype(F32)
    pick_row = lax.broadcasted_iota(jnp.int32, (8, LANES), 0)
    pick_lane = lax.broadcasted_iota(jnp.int32, (8, LANES), 1)
    pick = (pick_row == pick_lane // HEAD_DIM).astype(F32)
    inner = lax.dot_general(
        pick, product, (((1,), (1,)), ((), ())), precision=lax.Precision.HIGHEST, preferred_element_type=F32
    )
    above = lax.broadcasted_iota(jnp.int32, (TILE, TILE), 0) <= lax.broadcasted_iota(
        jnp.int32, (TILE, TILE), 1
    )
    grad_q[...] = jnp.zeros(grad_q.shape, F32)
    for j in range(blocks):
        kat = slice(j * TILE, (j + 1) * TILE)
        keys = packed[1, kat, :]
        values = packed[2, kat, :]
        dk = dv = 0.0
        for i in range(j, blocks):
            qat = slice(i * TILE, (i + 1) * TILE)
            dq = 0.0
            for head in range(2):
                query = queries[head][qat]
                grad_head = grads[head][qat]
                probs = jnp.exp(nt(keys, query) - logsum[0, head : head + 1, qat])
                if i == j:
                    probs = jnp.where(above, probs, 0.0)
                grad_probs = nt(values, grad_head)
                low = (probs * (grad_probs - inner[head : head + 1, qat])).astype(BF16)
                dv = dv + nn(probs.astype(BF16), grad_head)
                dk = dk + nn(low, query)
                dq = dq + tn(low, key_heads[head][kat])
            grad_q[qat, :] += dq
        out[1, kat, :] = dk.astype(BF16)
        out[2, kat, :] = dv.astype(BF16)
    out[0] = (grad_q[...] * FACTOR).astype(BF16)


def feed_body(
    info, mixed, middle, out_grad, gain, wo_l, wo_f, wi_l, wi_f, wb_l, wb_f,
    result_o, act_o, hidden_o, mid_o, carry_o, attn_o, mixed_o, gain_o,
    b_out, b_in, b_back, sems,
):
    step = pl.program_id(0)

    @pl.when(step == 0)
    def _():
        fetch(info, wo_l, wo_f, b_out, sems.at[0])
        fetch(info, wi_l, wi_f, b_in, sems.at[1])
        fetch(info, wb_l, wb_f, b_back, sems.at[2])
        arrived(wo_l, b_out, sems.at[0])

    rows = middle[...] + nn(mixed[...], b_out[...])
    scale = mean_square_scale(rows)
    normed_mid = (rows * scale * gain[...]).astype(BF16)
    mid_o[...] = normed_mid

    @pl.when(step == 0)
    def _():
        arrived(wi_l, b_in, sems.at[1])
        arrived(wb_l, b_back, sems.at[2])

    grad_ffn = out_grad[...]
    width = 768
    for first in range(0, b_in.shape[1], width):
        cols = slice(first, first + width)
        act, slope = gelu_parts(nn(normed_mid, b_in[:, cols]))
        act = act.astype(BF16)
        act_o[:, cols] = act
        hidden = (nt(grad_ffn, b_back[cols, :]) * slope).astype(BF16)
        hidden_o[:, cols] = hidden
    result_o[...] = (rows + nn(act_o[...], b_back[...])).astype(BF16)
    grad_mid = nt(hidden_o[...], b_in[...])
    back, gain_sum = norm_back(grad_mid, rows, scale, gain[...])
    carry = grad_ffn.astype(F32) + back
    carry_o[...] = carry
    grad_attn = carry.astype(BF16)
    attn_o[...] = grad_attn
    mixed_o[...] = nt(grad_attn, b_out[...]).astype(BF16)

    @pl.when(step == 0)
    def _():
        gain_o[...] = jnp.zeros(gain_o.shape, F32)

    gain_o[0:1, :] += gain_sum


def dense_out_body(info, packed, carry, middle, gain, pick_col, w_local, w_far, grad_o, sel_o, gain_o, b_qkv, sem):
    step = pl.program_id(0)

    @pl.when(step == 0)
    def _():
        fetch(info, w_local, w_far, b_qkv, sem)
        gain_o[...] = jnp.zeros(gain_o.shape, F32)
        sel_o[...] = jnp.zeros(sel_o.shape, F32)
        arrived(w_local, b_qkv, sem)

    count, width = middle.shape
    grad_normed = sum(nt(packed[n], b_qkv[:, n * width : (n + 1) * width]) for n in range(3))
    rows = middle[...]
    back, gain_sum = norm_back(grad_normed, rows, mean_square_scale(rows), gain[...])
    gain_o[0:1, :] += gain_sum
    grad = (carry[...] + back).astype(BF16)
    grad_o[...] = grad
    cap = pick_col.shape[0]
    place = step * count + lax.broadcasted_iota(jnp.int32, (cap, count), 1)
    sel_o[...] += nn((pick_col[...] == place).astype(BF16), grad)


def ends_body(info, own, far, grad_chosen, pick_row, out):
    seq = pl.program_id(0)
    step = pl.program_id(1)

    @pl.when(seq == info[0])
    def _():
        out[...] = own[...]

    @pl.when(seq != info[0])
    def _():
        out[...] = far[...]

    @pl.when(info[0] == 0)
    def _():
        rows = out.shape[0]
        cap = grad_chosen.shape[0]
        place = step * rows + lax.broadcasted_iota(jnp.int32, (rows, cap), 0)
        hot = (pick_row[0] == place).astype(F32)
        added = lax.dot_general(
            hot, grad_chosen[...], (((1,), (0,)), ((), ())),
            precision=lax.Precision.HIGHEST, preferred_element_type=F32,
        )
        out[...] = (out[...].astype(F32) + added).astype(BF16)


def position(info, dest):
    relative = info[1] ^ dest
    place = 0
    for stage in range(STAGES):
        place = place * 2 + ((relative >> info[2 + stage]) & 1)
    return place


def chosen_ref(info, refs):
    if len(refs) == 1:
        return refs[0][...]
    return jnp.where(info[0] == 0, refs[0][...], refs[1][...])


def wide_body(count, info, *refs):
    lefts, rights, out, turned = refs[:count], refs[count : 2 * count], refs[-2], refs[-1]

    @pl.when(pl.program_id(0) == 0)
    def _():
        turned[...] = jnp.transpose(chosen_ref(info, lefts))

    right = chosen_ref(info, rights)
    product = nn(turned[...], right.reshape(right.shape[-2:])).astype(BF16)
    piece = out.shape[1]
    for dest in range(PIECES):
        out[position(info, dest)] = product[dest * piece : (dest + 1) * piece, :]


def tall_body(count, info, *refs):
    lefts, rights, out = refs[:count], refs[count : 2 * count], refs[-1]
    step = pl.program_id(0)
    product = tn(chosen_ref(info, lefts), chosen_ref(info, rights)).astype(BF16)
    piece = out.shape[1]
    per_step = product.shape[0] // piece
    for n in range(per_step):
        out[position(info, step * per_step + n)] = product[n * piece : (n + 1) * piece, :]


def wide_product(info, lefts, rights, own, tile):
    depth, rows = lefts[0].shape
    cols = rights[0].shape[-1] * (rights[0].shape[0] if rights[0].ndim == 3 else 1) // 2
    steps = cols // tile

    def half(info_ref):
        return info_ref[0] if own else 1 - info_ref[0]

    if rights[0].ndim == 3:
        fold = rights[0].shape[-1] // tile

        def at(t, info_ref):
            tile_index = t + half(info_ref) * steps
            return (tile_index // fold, 0, tile_index % fold)

        right_spec = pl.BlockSpec((1, depth, tile), at)
    else:
        right_spec = pl.BlockSpec((depth, tile), lambda t, info_ref: (0, t + half(info_ref) * steps))
    return run(
        functools.partial(wide_body, len(lefts)),
        info,
        [(left, whole((depth, rows))) for left in lefts] + [(right, right_spec) for right in rights],
        [
            (
                shape((PIECES, rows // PIECES, cols), BF16),
                pl.BlockSpec((PIECES, rows // PIECES, tile), lambda t, info_ref: (0, 0, t)),
            )
        ],
        (steps,),
        [pltpu.VMEM((rows, depth), BF16)],
        flops=2 * depth * rows * cols,
        moved=2 * (depth * rows + depth * cols + rows * cols),
    )[0]


def tall_product(info, lefts, rights, own):
    depth, rows = lefts[0].shape
    cols = rights[0].shape[1] // 2
    tile = 384
    steps = rows // tile

    def half(info_ref):
        return info_ref[0] if own else 1 - info_ref[0]

    out_dims = (PIECES, rows // PIECES, cols)
    return run(
        functools.partial(tall_body, len(lefts)),
        info,
        [(left, pl.BlockSpec((depth, tile), lambda t, info_ref: (0, t))) for left in lefts]
        + [
            (right, pl.BlockSpec((depth, cols), lambda t, info_ref: (0, half(info_ref))))
            for right in rights
        ],
        [(shape(out_dims, BF16), whole(out_dims))],
        (steps,),
        flops=2 * depth * rows * cols,
        moved=2 * (depth * rows + depth * cols + rows * cols),
    )[0]


def to_section(value, source):
    return lax.ppermute(value, "section", [(source, 1 - source)])


def swap_section(value):
    return lax.ppermute(value, "section", [(0, 1), (1, 0)])


def added_up(parts):
    total = parts[0].astype(F32)
    for part in parts[1:]:
        total = total + part.astype(F32)
    return total


def cross(value, orders, stage, count, low):
    pairs = []
    for section, order in enumerate(orders):
        base = section * count
        flip = low << order[stage]
        pairs += [(base + n, base + (n ^ flip)) for n in range(count)]
    return lax.ppermute(value, ("section", "dp"), pairs)


def scatter_sum(parts, orders):
    count = lax.axis_size("dp")
    low = count // PIECES
    for stage in range(STAGES):
        half = parts[0].shape[0] // 2
        send = added_up([part[half:] for part in parts]).astype(BF16)
        parts = [part[:half] for part in parts] + [cross(send, orders, stage, count, low)]
    own = added_up(parts)[0]
    if low > 1:
        rows, cols = own.shape
        place = lax.axis_index("dp") % low
        pieces = jnp.take(own.reshape(low, rows // low, cols), jnp.arange(low) ^ place, axis=0)
        while pieces.shape[0] > 1:
            half = pieces.shape[0] // 2
            far = lax.ppermute(pieces[half:], "dp", [(n, n ^ half) for n in range(count)])
            pieces = pieces[:half] + far
        own = pieces[0]
    return own


def sum_all(value):
    value = value + swap_section(value)
    count = lax.axis_size("dp")
    flip = 1
    while flip < count:
        value = value + lax.ppermute(value, "dp", [(n, n ^ flip) for n in range(count)])
        flip *= 2
    return value


ORDER_X = (0, 1, 2, 3)
ORDER_Y = (1, 0, 2, 3)
ORDER_Z = (2, 0, 1, 3)
ORDER_W = (2, 1, 0, 3)


def shards(inputs, out_grad, picks, valid, router, gain_attn, w_qkv, w_out, gain_mlp, w_in, w_back):
    w_qkv, w_out, w_in, w_back = w_qkv[0], w_out[0], w_in[0], w_back[0]
    seqs, cap = picks.shape
    seq_len = inputs.shape[0] // seqs
    width = inputs.shape[1]
    hidden = w_in.shape[1]
    rows = seqs * cap
    tiles = seq_len // TILE
    section = lax.axis_index("section")
    low = lax.axis_size("dp") // PIECES
    spot = lax.axis_index("dp") // low
    first = section == 0

    def facts(orders):
        order = jnp.where(first, jnp.array(orders[0]), jnp.array(orders[1]))
        return jnp.concatenate([jnp.stack([section, spot]), order]).astype(jnp.int32)

    info = facts((ORDER_X, ORDER_X))
    far_qkv = to_section(w_qkv, 1)
    far_out = to_section(w_out, 1)
    far_in = to_section(w_in, 1)
    far_back = to_section(w_back, 1)
    pick_col = picks.reshape(rows, 1)
    valid_col = valid.reshape(rows, 1)
    router_row = router.reshape(1, width)

    weight_bufs = [
        pltpu.VMEM(w_qkv.shape, BF16),
        pltpu.VMEM(w_out.shape, BF16),
        pltpu.VMEM(w_in.shape, BF16),
        pltpu.VMEM(w_back.shape, BF16),
        pltpu.SemaphoreType.DMA((4,)),
    ]
    weight_ins = [(w_qkv, ANY), (w_out, ANY), (w_in, ANY), (w_back, ANY)]

    def full(array):
        return (array, whole(array.shape))

    def made(dims, dtype):
        return (shape(dims, dtype), whole(dims))

    routed_flops = 2 * rows * (4 * width * width + 2 * width * hidden)
    weight_bytes = 2 * (4 * width * width + 2 * width * hidden)
    chosen, normed0, packed0, mixed0, rows0, mid0, act0, slope0, branch0, gate0, delta = run(
        routed_forward_body,
        info,
        [full(v) for v in (inputs, pick_col, valid, valid_col, router_row, gain_attn, gain_mlp)] + weight_ins,
        [
            made((rows, width), BF16),
            made((rows, width), BF16),
            made((rows, 3 * width), BF16),
            made((rows, width), BF16),
            made((rows, width), F32),
            made((rows, width), BF16),
            made((rows, hidden), BF16),
            made((rows, hidden), BF16),
            made((rows, width), F32),
            made((rows, LANES), F32),
            made((rows, width), BF16),
        ],
        (1,),
        weight_bufs,
        flops=routed_flops,
        moved=weight_bytes,
    )
    far_delta = to_section(delta[cap:], 0)
    own_delta = jnp.where(first, delta[:cap], far_delta)
    own_picks = jnp.where(first, picks[0], picks[1])
    own_row = own_picks.reshape(1, cap)
    own_col = own_picks.reshape(cap, 1)

    gain_attn1 = jnp.where(first, swap_section(gain_attn), gain_attn)
    gain_mlp1 = jnp.where(first, swap_section(gain_mlp), gain_mlp)

    def row_tile(dims):
        return pl.BlockSpec(dims, lambda i, info_ref: (i, 0))

    def seq_tile():
        return pl.BlockSpec((TILE, width), lambda i, info_ref: (info_ref[0] * tiles + i, 0))

    def tiled(cols, dtype):
        return (shape((seq_len, cols), dtype), row_tile((TILE, cols)))

    three_tile = pl.BlockSpec((3, TILE, width), lambda i, info_ref: (0, i, 0))
    three = shape((3, seq_len, width), BF16)
    qkv_buf = [pltpu.VMEM(w_qkv.shape, BF16), pltpu.SemaphoreType.DMA]

    middle, normed1, packed1 = run(
        dense_in_body,
        info,
        [
            (inputs, seq_tile()),
            full(own_delta),
            full(own_row),
            full(gain_attn1),
            (w_qkv, ANY),
            (far_qkv, ANY),
        ],
        [tiled(width, F32), tiled(width, BF16), (three, three_tile)],
        (tiles,),
        qkv_buf,
        flops=6 * seq_len * width * width,
        moved=seq_len * width * 12 + 6 * width * width,
    )

    pair_spec = pl.BlockSpec((3, seq_len, LANES), lambda h, info_ref: (0, 0, h))
    column_spec = pl.BlockSpec((seq_len, LANES), lambda h, info_ref: (0, h))
    logsum_spec = pl.BlockSpec((1, 8, seq_len), lambda h, info_ref: (h, 0, 0))
    attend_flops = 2 * HEADS * seq_len * seq_len * TILE
    mixed1, logsum1 = run(
        attend_forward_body,
        info,
        [(packed1, pair_spec)],
        [
            (shape((seq_len, width), BF16), column_spec),
            (shape((PAIRS, 8, seq_len), F32), logsum_spec),
        ],
        (PAIRS,),
        flops=attend_flops,
        moved=8 * seq_len * width,
    )

    result, act1, hidden1, mid1, carry, attn1, grad_mixed1, gain_mlp_sum = run(
        feed_body,
        info,
        [
            (mixed1, row_tile((TILE, width))),
            (middle, row_tile((TILE, width))),
            (out_grad, seq_tile()),
            full(gain_mlp1),
            (w_out, ANY),
            (far_out, ANY),
            (w_in, ANY),
            (far_in, ANY),
            (w_back, ANY),
            (far_back, ANY),
        ],
        [
            tiled(width, BF16),
            tiled(hidden, BF16),
            tiled(hidden, BF16),
            tiled(width, BF16),
            tiled(width, F32),
            tiled(width, BF16),
            tiled(width, BF16),
            made((8, width), F32),
        ],
        (tiles,),
        [
            pltpu.VMEM(w_out.shape, BF16),
            pltpu.VMEM(w_in.shape, BF16),
            pltpu.VMEM(w_back.shape, BF16),
            pltpu.SemaphoreType.DMA((3,)),
        ],
        flops=2 * seq_len * width * (2 * width + 4 * hidden),
        moved=seq_len * (20 * width + 4 * hidden) + 2 * width * (width + 2 * hidden),
    )

    out_grad1 = jnp.where(first, out_grad[:seq_len], out_grad[seq_len:])

    def dense_sum(product, orders):
        away = product(facts(orders[::-1]), False)
        return scatter_sum([product(facts(orders), True), swap_section(away)], orders)

    def routed_sum(product, orders):
        return scatter_sum([product(facts(orders), True)], orders)

    sum_in1 = dense_sum(lambda f, own: wide_product(f, [mid1], [hidden1], own, 512), (ORDER_X, ORDER_Y))
    sum_back1 = dense_sum(lambda f, own: tall_product(f, [act1], [out_grad1], own), (ORDER_Z, ORDER_X))

    packed_grad1 = run(
        attend_backward_body,
        info,
        [(packed1, pair_spec), (grad_mixed1, column_spec), (mixed1, column_spec), (logsum1, logsum_spec)],
        [(three, pair_spec)],
        (PAIRS,),
        [pltpu.VMEM((seq_len, LANES), F32)],
        flops=5 * attend_flops // 2,
        moved=16 * seq_len * width,
    )[0]

    sum_out1 = dense_sum(lambda f, own: wide_product(f, [mixed1], [attn1], own, 384), (ORDER_Y, ORDER_W))

    grad_middle, grad_sel, gain_attn_sum = run(
        dense_out_body,
        info,
        [
            (packed_grad1, three_tile),
            (carry, row_tile((TILE, width))),
            (middle, row_tile((TILE, width))),
            full(gain_attn1),
            full(own_col),
            (w_qkv, ANY),
            (far_qkv, ANY),
        ],
        [tiled(width, BF16), made((cap, width), F32), made((8, width), F32)],
        (tiles,),
        qkv_buf,
        flops=6 * seq_len * width * width,
        moved=seq_len * width * 16 + 6 * width * width,
    )
    grad_sel = grad_sel.astype(BF16)
    both_sel = jnp.concatenate([grad_sel, to_section(grad_sel, 1)], axis=0)
    sum_qkv1 = dense_sum(lambda f, own: wide_product(f, [normed1], [packed_grad1], own, 384), (ORDER_Y, ORDER_W))

    ffn0, hidden0, attn0, packed_grad0, grad_chosen, small0 = run(
        routed_backward_body,
        info,
        [
            full(v)
            for v in (
                both_sel, chosen, packed0, rows0, slope0, branch0, gate0, valid, valid_col,
                router_row, gain_attn, gain_mlp,
            )
        ]
        + weight_ins,
        [
            made((rows, width), BF16),
            made((rows, hidden), BF16),
            made((rows, width), BF16),
            made((3, rows, width), BF16),
            made((rows, width), F32),
            made((8, width), F32),
        ],
        (1,),
        weight_bufs,
        flops=routed_flops,
        moved=weight_bytes,
    )

    def both(value):
        return [value, to_section(value, 0)]

    sum_in0 = routed_sum(lambda f, own: wide_product(f, both(mid0), both(hidden0), own, 512), (ORDER_X, ORDER_Y))
    sum_back0 = routed_sum(lambda f, own: tall_product(f, both(act0), both(ffn0), own), (ORDER_Z, ORDER_X))
    sum_out0 = routed_sum(lambda f, own: wide_product(f, both(mixed0), both(attn0), own, 384), (ORDER_Y, ORDER_W))
    sum_qkv0 = routed_sum(
        lambda f, own: wide_product(f, both(normed0), both(packed_grad0), own, 384), (ORDER_Y, ORDER_W)
    )

    far_end = swap_section(jnp.where(first, result, grad_middle))
    own_end = jnp.where(first, grad_middle, result)
    end_spec = pl.BlockSpec((TILE, width), lambda s, i, info_ref: (i, 0))
    ends = run(
        ends_body,
        info,
        [
            (own_end, end_spec),
            (far_end, end_spec),
            (grad_chosen, pl.BlockSpec((cap, width), lambda s, i, info_ref: (s, 0))),
            (picks.reshape(seqs, 1, cap), pl.BlockSpec((1, 1, cap), lambda s, i, info_ref: (s, 0, 0))),
        ],
        [
            (
                shape((seqs * seq_len, width), BF16),
                pl.BlockSpec((TILE, width), lambda s, i, info_ref: (s * tiles + i, 0)),
            )
        ],
        (seqs, tiles),
        flops=4 * seqs * seq_len * cap * width,
        moved=8 * seqs * seq_len * width,
    )[0]

    small = jnp.where(first, small0, 0.0)
    small = jnp.concatenate([small[0:3], gain_mlp_sum[0:1], gain_attn_sum[0:1], small[3:6]], axis=0)
    small = sum_all(small)
    share = width // lax.axis_size("dp")

    def gain_share(routed_row, dense_row):
        row = jnp.where(first, small[routed_row], small[dense_row])
        return lax.dynamic_slice_in_dim(row, lax.axis_index("dp") * share, share)[None]

    def joined(routed, dense):
        far = swap_section(jnp.where(first, dense, routed))
        return jnp.where(
            first,
            jnp.concatenate([routed, far], axis=1),
            jnp.concatenate([far, dense], axis=1),
        )[None]

    return (
        ends[None],
        small[0],
        gain_share(2, 4),
        joined(sum_qkv0, sum_qkv1),
        joined(sum_out0, sum_out1),
        gain_share(1, 3),
        joined(sum_in0, sum_in1),
        joined(sum_back0, sum_back1),
    )


def solution(mesh):
    placed = (
        P("dp", None),
        P("dp", None),
        P("dp", None),
        P("dp", None),
        P(),
        P("section", None),
        P("section", None, None),
        P("section", None, None),
        P("section", None),
        P("section", None, None),
        P("section", None, None),
    )
    return jax.shard_map(
        shards,
        mesh=mesh,
        in_specs=placed,
        out_specs=(
            P("section", "dp", None),
            P(),
            P("section", "dp"),
            P("section", "dp", None),
            P("section", "dp", None),
            P("section", "dp"),
            P("section", "dp", None),
            P("section", "dp", None),
        ),
        check_vma=False,
    )
```

```python
import functools

import jax
import jax.numpy as jnp
from jax import lax
from jax.experimental import pallas as pl
from jax.experimental.pallas import tpu as pltpu
from jax.sharding import PartitionSpec as P

HEADS = 12
HEAD_DIM = 64
LANES = 128
PAIRS = HEADS * HEAD_DIM // LANES
EPS = 1e-06
FACTOR = HEAD_DIM ** (-0.5)
PIECES = 16
STAGES = 4
QUAD = 4
TILE = 256
VMEM_BYTES = 56 * 1024 * 1024
BF16 = jnp.bfloat16
F32 = jnp.float32


def nn(a, b):
    return lax.dot_general(a, b, (((1,), (0,)), ((), ())), preferred_element_type=F32)


def nt(a, b):
    return lax.dot_general(a, b, (((1,), (1,)), ((), ())), preferred_element_type=F32)


def tn(a, b):
    return lax.dot_general(a, b, (((0,), (0,)), ((), ())), preferred_element_type=F32)


def shape(dims, dtype):
    return jax.ShapeDtypeStruct(dims, dtype)


def whole(dims):
    zeros = (0,) * len(dims)
    return pl.BlockSpec(dims, lambda *_: zeros)


ANY = pl.BlockSpec(memory_space=pl.ANY)


def run(body, info, ins, outs, grid, scratch=(), flops=0, moved=0):
    arrays, in_specs = zip(*ins)
    shapes, out_specs = zip(*outs)
    return pl.pallas_call(
        body,
        out_shape=shapes,
        grid_spec=pltpu.PrefetchScalarGridSpec(
            num_scalar_prefetch=1,
            grid=grid,
            in_specs=in_specs,
            out_specs=out_specs,
            scratch_shapes=scratch,
        ),
        compiler_params=pltpu.CompilerParams(
            vmem_limit_bytes=VMEM_BYTES, dimension_semantics=("arbitrary",) * len(grid)
        ),
        cost_estimate=pl.CostEstimate(flops=flops, bytes_accessed=moved, transcendentals=0),
    )(info, *arrays)


def top_lanes(rows):
    return lax.broadcasted_iota(jnp.int32, (rows, LANES), 1) < HEAD_DIM


def lane_head(rows, which):
    lane = lax.broadcasted_iota(jnp.int32, (rows, LANES), 1)
    return (lane < HEAD_DIM) if which == 0 else (lane >= HEAD_DIM)


def head_only(value, which):
    return jnp.where(lane_head(value.shape[0], which), value, jnp.zeros_like(value))


def mean_square_scale(rows):
    return lax.rsqrt(jnp.mean(rows * rows, axis=-1, keepdims=True) + EPS)


def norm_back(grad, rows, scale, gain):
    hat = rows * scale
    scaled = grad * gain
    back = scale * (scaled - hat * jnp.mean(scaled * hat, axis=-1, keepdims=True))
    return back, jnp.sum(grad * hat, axis=0, keepdims=True)


def gelu_parts(pre):
    root = 0.7978845608028654
    square = pre * pre
    bent = jnp.tanh(root * pre * (1.0 + 0.044715 * square))
    half = 0.5 * (1.0 + bent)
    slope = half + 0.5 * pre * (1.0 - bent * bent) * (root * (1.0 + 0.134145 * square))
    return pre * half, slope


def fetch(info, local, remote, buf, sem):
    @pl.when(info[0] == 1)
    def _():
        pltpu.make_async_copy(local, buf, sem).start()

    @pl.when(info[0] == 0)
    def _():
        pltpu.make_async_copy(remote, buf, sem).start()


def arrived(source, buf, sem):
    pltpu.make_async_copy(source, buf, sem).wait()


def stacked(value):
    return jnp.concatenate([head_only(value, h) for h in range(2)], axis=0)


def unstacked(value):
    half = value.shape[0] // 2
    return jnp.where(top_lanes(half), value[:half], value[half:])


def slot_pieces(packed, seq, pair, cap):
    rows = slice(seq * cap, (seq + 1) * cap)
    width = HEADS * HEAD_DIM
    first = pair * LANES
    queries = stacked(packed[rows, first : first + LANES] * BF16(FACTOR))
    keys = packed[rows, width + first : width + first + LANES]
    values = packed[rows, 2 * width + first : 2 * width + first + LANES]
    return queries, keys, values


def slot_rule(valid_row, cap):
    query = lax.broadcasted_iota(jnp.int32, (cap, cap), 0)
    key = lax.broadcasted_iota(jnp.int32, (cap, cap), 1)
    rule = (key <= query) & ((valid_row > 0) | (key == query))
    return jnp.concatenate([rule, rule], axis=0)


def column_of(row):
    return jnp.transpose(jnp.broadcast_to(row, (row.shape[1], row.shape[1])))


def slot_mask(valid):
    seqs = valid.shape[0]
    return jnp.concatenate([column_of(valid[s : s + 1, :].astype(F32)) for s in range(seqs)], axis=0)[:, 0:1]


def weight_copies(sources, bufs, sems):
    return [pltpu.make_async_copy(a, b, sems.at[n]) for n, (a, b) in enumerate(zip(sources, bufs))]


def routed_forward_body(
    info, x, picks, valid, consts, w_qkv, w_out, w_in, w_back,
    chosen_o, normed_o, packed_o, mixed_o, rows_o, stay_o, over_x_o, over_y_o, slope_o, branch_o, gate_o, open_o,
    near_o, away_o,
    b_qkv, b_out, b_in, b_back, act_b, sems,
):
    @pl.when(info[0] == 0)
    def _():
        copies = weight_copies((w_qkv, w_out, w_in, w_back), (b_qkv, b_out, b_in, b_back), sems)
        for copy in copies:
            copy.start()
        seqs, cap = valid.shape
        seq_len = x.shape[0] // seqs
        parts = []
        for seq in range(seqs):
            place = lax.broadcasted_iota(jnp.int32, (seq_len, cap), 0)
            hot = (picks[seq : seq + 1, :] == place).astype(BF16)
            parts.append(tn(hot, x[seq * seq_len : (seq + 1) * seq_len, :]))
        chosen = jnp.concatenate(parts, axis=0)
        chosen_o[...] = chosen.astype(BF16)
        gates = jax.nn.sigmoid(jnp.sum(chosen * consts[2:3, :], axis=-1, keepdims=True))
        gate_o[...] = jnp.broadcast_to(gates, gate_o.shape)
        normed = (chosen * mean_square_scale(chosen) * consts[0:1, :]).astype(BF16)
        normed_o[...] = jnp.transpose(normed)
        copies[0].wait()
        packed_o[...] = nn(normed, b_qkv[...]).astype(BF16)
        work = [(seq, pair) for seq in range(seqs) for pair in range(PAIRS)]
        allowed = [slot_rule(valid[seq : seq + 1, :], cap) for seq in range(seqs)]
        pieces = [slot_pieces(packed_o, seq, pair, cap) for seq, pair in work]
        scores = [jnp.where(allowed[w[0]], nt(p[0], p[1]), -1e30) for w, p in zip(work, pieces)]
        grown = [jnp.exp(v - jnp.max(v, axis=-1, keepdims=True)).astype(BF16) for v in scores]
        ones = jnp.ones((cap, LANES), BF16)
        outs = [nn(g, jnp.concatenate([p[2], ones], axis=1)) for g, p in zip(grown, pieces)]
        outs = [unstacked(o[:, :LANES] / o[:, LANES:]).astype(BF16) for o in outs]
        mixed = jnp.concatenate(
            [jnp.concatenate(outs[s * PAIRS : (s + 1) * PAIRS], axis=1) for s in range(seqs)], axis=0
        )
        mixed_o[...] = jnp.transpose(mixed)
        copies[1].wait()
        attn_out = nn(mixed, b_out[...])
        rows = chosen + attn_out
        rows_o[...] = rows
        normed_mid = (rows * mean_square_scale(rows) * consts[1:2, :]).astype(BF16)
        mid_turned = jnp.transpose(normed_mid)
        stay_o[2] = mid_turned
        over_x_o[4] = mid_turned
        over_y_o[2] = mid_turned
        copies[2].wait()
        hidden = b_in.shape[1]
        step = 768
        piece = hidden // PIECES
        member = info[1] & 3
        for first in range(0, hidden, step):
            cols = slice(first, first + step)
            act, slope = gelu_parts(nn(normed_mid, b_in[:, cols]))
            act = act.astype(BF16)
            slope = slope.astype(BF16)
            act_b[:, cols] = act
            slope_o[:, cols] = slope
            for n, turned in enumerate((jnp.transpose(act), jnp.transpose(slope))):
                at = pl.ds(first // step * piece, piece)
                for owner in range(QUAD):
                    part = turned[owner * piece : (owner + 1) * piece, :]
                    relative = owner ^ member

                    @pl.when(relative == 0)
                    def _():
                        stay_o[n, at, :] = part

                    @pl.when(relative == 2)
                    def _():
                        over_y_o[n, at, :] = part

                    @pl.when((relative & 1) == 1)
                    def _():
                        over_x_o[n + (relative & 2), at, :] = part

        copies[3].wait()
        branch = attn_out + nn(act_b[...], b_back[...])
        branch_o[...] = branch
        opened = gates * slot_mask(valid)
        open_o[...] = jnp.broadcast_to(opened, open_o.shape)
        delta = (opened * branch).astype(BF16)
        near_o[...] = delta[:cap]
        away_o[...] = delta[cap:]


def routed_backward_body(
    info, near, far, chosen_i, packed, rows_i, slope, branch, gate, valid, consts, w_qkv, w_out, w_in, w_back,
    attn_o, packed_o, chosen_o, small_o,
    b_qkv, b_out, b_in, b_back, hidden_b, sems,
):
    @pl.when(info[0] == 0)
    def _():
        copies = weight_copies((w_qkv, w_out, w_in, w_back), (b_qkv, b_out, b_in, b_back), sems)
        for n in (3, 2, 1, 0):
            copies[n].start()
        seqs, cap = valid.shape
        chosen = chosen_i[...].astype(F32)
        grad_sel = jnp.concatenate([near[...], far[...]], axis=0).astype(F32)
        gates = gate[:, 0:1]
        mask = slot_mask(valid)
        logit = jnp.sum(grad_sel * branch[...], axis=-1, keepdims=True) * mask * gates * (1.0 - gates)
        grad = grad_sel * (gates * mask)
        grad_ffn = grad.astype(BF16)
        copies[3].wait()
        copies[2].wait()
        step = 768
        for first in range(0, b_in.shape[1], step):
            cols = slice(first, first + step)
            hidden = (nt(grad_ffn, b_back[cols, :]) * slope[:, cols].astype(F32)).astype(BF16)
            hidden_b[:, cols] = hidden
        grad_mid = nt(hidden_b[...], b_in[...])
        rows = rows_i[...]
        grad_rows, gain_mlp_sum = norm_back(grad_mid, rows, mean_square_scale(rows), consts[1:2, :])
        grad_attn = (grad + grad_rows).astype(BF16)
        attn_o[...] = grad_attn
        copies[1].wait()
        grad_mixed = nt(grad_attn, b_out[...]).astype(BF16)
        work = [(seq, pair) for seq in range(seqs) for pair in range(PAIRS)]
        allowed = [slot_rule(valid[seq : seq + 1, :], cap) for seq in range(seqs)]
        pieces = [slot_pieces(packed, seq, pair, cap) for seq, pair in work]
        grads = [
            stacked(grad_mixed[seq * cap : (seq + 1) * cap, pair * LANES : (pair + 1) * LANES])
            for seq, pair in work
        ]
        scores = [jnp.where(allowed[w[0]], nt(p[0], p[1]), -1e30) for w, p in zip(work, pieces)]
        grad_probs = [nt(g, p[2]) for g, p in zip(grads, pieces)]
        grown = [jnp.exp(v - jnp.max(v, axis=-1, keepdims=True)) for v in scores]
        probs = [v / jnp.sum(v, axis=-1, keepdims=True) for v in grown]
        lows = [
            (p * (g - jnp.sum(p * g, axis=-1, keepdims=True))).astype(BF16) for p, g in zip(probs, grad_probs)
        ]
        for (seq, pair), piece, grad_head, prob, low in zip(work, pieces, grads, probs, lows):
            at = slice(seq * cap, (seq + 1) * cap)
            cols = slice(pair * LANES, (pair + 1) * LANES)
            packed_o[0, at, cols] = (unstacked(nn(low, piece[1])) * FACTOR).astype(BF16)
            packed_o[1, at, cols] = tn(low, piece[0]).astype(BF16)
            packed_o[2, at, cols] = tn(prob.astype(BF16), grad_head).astype(BF16)
        copies[0].wait()
        width = chosen.shape[1]
        grad_normed = sum(nt(packed_o[n], b_qkv[:, n * width : (n + 1) * width]) for n in range(3))
        back, gain_attn_sum = norm_back(grad_normed, chosen, mean_square_scale(chosen), consts[0:1, :])
        chosen_o[...] = grad_rows + back + logit * consts[2:3, :]
        small_o[...] = jnp.zeros(small_o.shape, F32)
        small_o[0:1, :] = jnp.sum(logit * chosen, axis=0, keepdims=True)
        small_o[1:2, :] = gain_mlp_sum
        small_o[2:3, :] = gain_attn_sum


def dense_gain(info, local, far, row):
    return jnp.where(info[0] == 1, local[row : row + 1, :], far[row : row + 1, :])


def dense_in_body(
    info, x, near, away, picks, consts, consts_far, w_local, w_far, middle_o, normed_o, packed_o, b_qkv, sem
):
    step = pl.program_id(0)

    @pl.when(step == 0)
    def _():
        fetch(info, w_local, w_far, b_qkv, sem)

    rows, width = x.shape
    cap = near.shape[0]
    delta = jnp.where(info[0] == 0, near[...], away[...])
    place = step * rows + lax.broadcasted_iota(jnp.int32, (rows, cap), 0)
    hot = (picks[pl.ds(info[0], 1), :] == place).astype(BF16)
    middle = x[...].astype(F32) + nn(hot, delta)
    middle_o[...] = middle
    normed = (middle * mean_square_scale(middle) * dense_gain(info, consts, consts_far, 0)).astype(BF16)
    normed_o[...] = jnp.transpose(normed)

    @pl.when(step == 0)
    def _():
        arrived(w_local, b_qkv, sem)

    for n in range(3):
        packed_o[n] = nn(normed, b_qkv[:, n * width : (n + 1) * width]).astype(BF16)


def attend_forward_body(info, packed, mixed_o, logsum_o):
    seq_len = packed.shape[1]
    tile = 2 * TILE
    queries = packed[0] * BF16(FACTOR)
    keys = packed[1]
    ones = jnp.ones((seq_len, LANES), BF16)
    values = [jnp.concatenate([head_only(packed[2], h), ones], axis=1) for h in range(2)]
    below = lax.broadcasted_iota(jnp.int32, (tile, tile), 1) <= lax.broadcasted_iota(jnp.int32, (tile, tile), 0)
    for first in range(0, seq_len, tile):
        upto = first + tile
        at = slice(first, upto)
        scores = []
        for head in range(2):
            score = nt(head_only(queries[at], head), keys[:upto])
            last = jnp.where(below, score[:, first:], -1e30)
            scores.append(jnp.concatenate([score[:, :first], last], axis=1) if first else last)
        tops = [jnp.max(score, axis=-1, keepdims=True) for score in scores]
        grown = [jnp.exp(score - top).astype(BF16) for score, top in zip(scores, tops)]
        outs = [nn(g, value[:upto]) for g, value in zip(grown, values)]
        mixed = sum(out[:, :LANES] * (1.0 / out[:, LANES:]) for out in outs)
        mixed_o[at, :] = mixed.astype(BF16)
        sums = [top + jnp.log(out[:, LANES:]) for top, out in zip(tops, outs)]
        turned = jnp.transpose(jnp.where(top_lanes(tile), sums[0], sums[1]))
        logsum_o[0, 0:1, at] = turned[0:1]
        logsum_o[0, 1:2, at] = turned[HEAD_DIM : HEAD_DIM + 1]


def attend_backward_body(info, packed, grad, mixed, logsum, out, grad_q):
    seq_len = packed.shape[1]
    queries = packed[0] * BF16(FACTOR)
    queries = [head_only(queries, h) for h in range(2)]
    key_heads = [head_only(packed[1], h) for h in range(2)]
    grads = [head_only(grad[...], h) for h in range(2)]
    product = grad[...].astype(F32) * mixed[...].astype(F32)
    pick_row = lax.broadcasted_iota(jnp.int32, (8, LANES), 0)
    pick_lane = lax.broadcasted_iota(jnp.int32, (8, LANES), 1)
    pick = (pick_row == pick_lane // HEAD_DIM).astype(F32)
    inner = lax.dot_general(
        pick, product, (((1,), (1,)), ((), ())), precision=lax.Precision.HIGHEST, preferred_element_type=F32
    )
    above = lax.broadcasted_iota(jnp.int32, (TILE, TILE), 0) <= lax.broadcasted_iota(
        jnp.int32, (TILE, TILE), 1
    )
    for first in range(0, seq_len, TILE):
        kat = slice(first, first + TILE)
        keys = packed[1, kat, :]
        values = packed[2, kat, :]
        dks, dvs, dqs = [], [], []
        for head in range(2):
            query = queries[head][first:]
            grad_head = grads[head][first:]
            probs = jnp.exp(nt(keys, query) - logsum[0, head : head + 1, first:])
            edge = jnp.where(above, probs[:, :TILE], 0.0)
            probs = jnp.concatenate([edge, probs[:, TILE:]], axis=1) if first + TILE < seq_len else edge
            grad_probs = nt(values, grad_head)
            low = (probs * (grad_probs - inner[head : head + 1, first:])).astype(BF16)
            dvs.append(nn(probs.astype(BF16), grad_head))
            dks.append(nn(low, query))
            dqs.append(tn(low, key_heads[head][kat]))
        if first == 0:
            grad_q[...] = dqs[0] + dqs[1]
        else:
            grad_q[first:, :] += dqs[0] + dqs[1]
        out[1, kat, :] = (dks[0] + dks[1]).astype(BF16)
        out[2, kat, :] = (dvs[0] + dvs[1]).astype(BF16)
    out[0] = (grad_q[...] * FACTOR).astype(BF16)


def feed_body(
    info, mixed, middle, out_grad, consts, consts_far, wo_l, wo_f, wi_l, wi_f, wb_l, wb_f,
    result_o, act_o, hidden_o, mid_o, turned_o, carry_o, attn_o, mixed_o, gain_o,
    b_out, b_in, b_back, sems,
):
    step = pl.program_id(0)

    @pl.when(step == 0)
    def _():
        fetch(info, wo_l, wo_f, b_out, sems.at[0])
        fetch(info, wi_l, wi_f, b_in, sems.at[1])
        fetch(info, wb_l, wb_f, b_back, sems.at[2])
        gain_o[...] = jnp.zeros(gain_o.shape, F32)
        arrived(wo_l, b_out, sems.at[0])

    gain = dense_gain(info, consts, consts_far, 1)
    turned_o[...] = jnp.transpose(mixed[...])
    rows = middle[...] + nn(mixed[...], b_out[...])
    scale = mean_square_scale(rows)
    normed_mid = (rows * scale * gain).astype(BF16)
    mid_o[...] = jnp.transpose(normed_mid)

    @pl.when(step == 0)
    def _():
        arrived(wi_l, b_in, sems.at[1])
        arrived(wb_l, b_back, sems.at[2])

    grad_ffn = out_grad[...]
    width = 768
    for first in range(0, b_in.shape[1], width):
        cols = slice(first, first + width)
        act, slope = gelu_parts(nn(normed_mid, b_in[:, cols]))
        act_o[:, cols] = act.astype(BF16)
        hidden_o[:, cols] = (nt(grad_ffn, b_back[cols, :]) * slope).astype(BF16)
    result_o[...] = (rows + nn(act_o[...], b_back[...])).astype(BF16)
    grad_mid = nt(hidden_o[...], b_in[...])
    back, gain_sum = norm_back(grad_mid, rows, scale, gain)
    carry = grad_ffn.astype(F32) + back
    carry_o[...] = carry
    grad_attn = carry.astype(BF16)
    attn_o[...] = grad_attn
    mixed_o[...] = nt(grad_attn, b_out[...]).astype(BF16)
    gain_o[3:4, :] += gain_sum


def dense_out_body(
    info, packed, carry, middle, consts, consts_far, picks, w_local, w_far, grad_o, sel_o, gain_o, b_qkv, total, sem
):
    step = pl.program_id(0)

    @pl.when(step == 0)
    def _():
        fetch(info, w_local, w_far, b_qkv, sem)
        gain_o[...] = jnp.zeros(gain_o.shape, F32)
        total[...] = jnp.zeros(total.shape, F32)
        arrived(w_local, b_qkv, sem)

    count, width = middle.shape
    grad_normed = sum(nt(packed[n], b_qkv[:, n * width : (n + 1) * width]) for n in range(3))
    rows = middle[...]
    gain = dense_gain(info, consts, consts_far, 0)
    back, gain_sum = norm_back(grad_normed, rows, mean_square_scale(rows), gain)
    gain_o[4:5, :] += gain_sum
    grad = (carry[...] + back).astype(BF16)
    grad_o[...] = grad
    cap = total.shape[0]
    place = step * count + lax.broadcasted_iota(jnp.int32, (count, cap), 0)
    total[...] += tn((picks[pl.ds(info[0], 1), :] == place).astype(BF16), grad)

    @pl.when(step == pl.num_programs(0) - 1)
    def _():
        sel_o[...] = total[...].astype(BF16)


def ends_body(info, result, grad, far_result, far_grad, grad_chosen, picks, out):
    seq = pl.program_id(0)
    step = pl.program_id(1)

    @pl.when(info[0] == 1)
    def _():
        out[...] = jnp.where(seq == 1, result[...], far_result[...])

    @pl.when(info[0] == 0)
    def _():
        base = jnp.where(seq == 0, grad[...], far_grad[...]).astype(F32)
        rows = out.shape[0]
        cap = grad_chosen.shape[0]
        place = step * rows + lax.broadcasted_iota(jnp.int32, (rows, cap), 0)
        hot = (picks[pl.ds(seq, 1), :] == place).astype(BF16)
        high = grad_chosen[...].astype(BF16)
        low = (grad_chosen[...] - high.astype(F32)).astype(BF16)
        out[...] = (base + (nn(hot, high) + nn(hot, low))).astype(BF16)


def position(info, base, dest):
    relative = info[1] ^ dest
    place = 0
    for stage in range(STAGES):
        place = place * 2 + ((relative >> info[base + stage]) & 1)
    return place


def picked(info, refs):
    if len(refs) == 1:
        return refs[0][...]
    return jnp.where(info[0] == 0, refs[0][...], refs[1][...])


def put_block(info, base, out, product, slot):
    piece = product.shape[0] // PIECES
    for dest in range(PIECES):
        out[position(info, base, dest), slot * piece : (slot + 1) * piece, :] = product[
            dest * piece : (dest + 1) * piece, :
        ]


def feed_grad_body(base, send, info, mid, hidden, act, ffn, out):
    step = pl.program_id(0)
    inward = (info[0] == 0) if send else (info[0] == 1)

    @pl.when(inward)
    def _():
        product = nn(mid[...], hidden[...]).astype(BF16)
        piece = product.shape[0] // PIECES
        for dest in range(PIECES):
            out[position(info, base, dest), pl.ds(pl.multiple_of(step * piece, piece), piece), :] = product[
                dest * piece : (dest + 1) * piece, :
            ]

    @pl.when(jnp.logical_not(inward))
    def _():
        product = tn(act[...], ffn[...]).astype(BF16)
        piece = out.shape[1]
        count = product.shape[0] // piece
        for n in range(count):
            out[position(info, base, step * count + n)] = product[n * piece : (n + 1) * piece, :]


def origin(info, base, place):
    relative = 0
    for stage in range(STAGES):
        if place >> (STAGES - 1 - stage) & 1:
            relative = relative | (1 << info[base + stage])
    return info[1] ^ relative


def put_block(info, base, outs, product, slot, buf):
    piece = product.shape[0] // PIECES
    buf[...] = product.astype(BF16)
    at = slice(slot * piece, (slot + 1) * piece)
    for place in range(PIECES):
        dest = origin(info, base, place)
        rows = pl.ds(pl.multiple_of(dest * piece, piece), piece)
        outs[0 if place < PIECES // 2 else 1][place % (PIECES // 2), at, :] = buf[rows, :]


def side_grad_body(
    info, normed0, packed0, mixed0, attn0,
    n_near, n_far, p_near, p_far, m_near, m_far, a_near, a_far,
    qk_stay, qk_go, v_stay, v_go, o_stay, o_go,
    n_buf, p_buf, m_buf, a_buf, buf, sems,
):
    targets = (
        (SIDE_QK, (qk_stay, qk_go), 0),
        (SIDE_QK, (qk_stay, qk_go), 1),
        (SIDE_V, (v_stay, v_go), 0),
        (SIDE_O, (o_stay, o_go), 0),
    )

    @pl.when(info[0] == 0)
    def _():
        for n in range(3):
            put_block(info, targets[n][0], targets[n][1], nn(normed0[...], packed0[n]), targets[n][2], buf)
        put_block(info, targets[3][0], targets[3][1], nn(mixed0[...], attn0[...]), targets[3][2], buf)

    @pl.when(info[0] == 1)
    def _():
        sources = [(m_near, m_buf, 0), (m_far, m_buf, 1), (a_near, a_buf, 0), (a_far, a_buf, 1)]
        sources += [(n_near, n_buf, 0), (n_far, n_buf, 1)]
        copies = [
            pltpu.make_async_copy(source, target.at[n], sems.at[k])
            for k, (source, target, n) in enumerate(sources)
        ]
        blocks = [
            pltpu.make_async_copy(source.at[which], p_buf.at[n, which], sems.at[6 + 2 * which + n])
            for which in range(3)
            for n, source in enumerate((p_near, p_far))
        ]
        for copy in copies + blocks:
            copy.start()
        for copy in copies[:4]:
            copy.wait()
        put_block(
            info, targets[3][0], targets[3][1], nn(m_buf[0], a_buf[0]) + nn(m_buf[1], a_buf[1]), targets[3][2], buf
        )
        for copy in copies[4:]:
            copy.wait()
        for which in range(3):
            blocks[2 * which].wait()
            blocks[2 * which + 1].wait()
            product = nn(n_buf[0], p_buf[0, which]) + nn(n_buf[1], p_buf[1, which])
            put_block(info, targets[which][0], targets[which][1], product, targets[which][2], buf)


def quad_grad_body(
    info, stay, from_x, from_y, from_xy, g_own, g_x, g_y, g_xy, w_back, go_o, stay_o,
    b_back, acts, slopes, mids, grads, hidden, buf, sems,
):
    @pl.when(info[0] == 0)
    def _():
        rows = g_own.shape[0]
        piece = b_back.shape[0] // QUAD
        member = info[1] & 3
        copies = []
        for z in range(QUAD):
            at = pl.ds(pl.multiple_of((z * QUAD + member) * piece, piece), piece)
            copies.append(pltpu.make_async_copy(w_back.at[at], b_back.at[pl.ds(z * piece, piece)], sems.at[z]))
        for copy in copies:
            copy.start()
        for n, (source, offset) in enumerate(((stay, 2), (from_x, 4), (from_y, 2), (from_xy, 2))):
            at = slice(n * rows, (n + 1) * rows)
            acts[:, at] = source[0]
            slopes[:, at] = source[1]
            mids[:, at] = source[offset]
        for n, source in enumerate((g_own, g_x, g_y, g_xy)):
            grads[n * rows : (n + 1) * rows, :] = source[...]
        for copy in copies:
            copy.wait()
        hidden[...] = (nt(b_back[...], grads[...]) * slopes[...].astype(F32)).astype(BF16)
        layer = info[1] >> 2
        for part, product in enumerate((nn(acts[...], grads[...]), nt(mids[...], hidden[...]))):
            buf[...] = product.astype(BF16)
            for place in range(QUAD):
                z = layer ^ ((place >> 1) | ((place & 1) << 1))
                at = pl.ds(pl.multiple_of(z * piece, piece), piece)
                target = stay_o if place < 2 else go_o
                target[place % 2, part * piece : (part + 1) * piece, :] = buf[at, :]


def feed_grad(info, base, mid, hidden, act, ffn, send, ffn_block):
    width, depth = mid.shape
    steps = hidden.shape[1] // width
    dims = (PIECES, steps * width // PIECES, width)

    def inward(t, info_ref):
        here = 1 - info_ref[0] if send else info_ref[0]
        return (0, t * here)

    def backward(t, info_ref):
        here = info_ref[0] if send else 1 - info_ref[0]
        return (0, t * here)

    return run(
        functools.partial(feed_grad_body, base, send),
        info,
        [
            (mid, whole((width, depth))),
            (hidden, pl.BlockSpec((depth, width), inward)),
            (act, pl.BlockSpec((depth, width), backward)),
            (ffn, pl.BlockSpec((depth, width), ffn_block)),
        ],
        [(shape(dims, BF16), whole(dims))],
        (steps,),
        flops=2 * depth * steps * width * width,
        moved=2 * (depth + depth * steps + PIECES * dims[1]) * width,
    )[0]


def side_grad(info, routed, dense):
    width, depth = dense[0].shape
    rows = routed[0].shape[1]
    half = PIECES // 2
    piece = width // PIECES

    def made(blocks):
        dims = (half, blocks * piece, width)
        return (shape(dims, BF16), whole(dims))

    return run(
        side_grad_body,
        info,
        [(v, whole(v.shape)) for v in routed] + [(v, ANY) for v in dense],
        [made(2), made(2), made(1), made(1), made(1), made(1)],
        (1,),
        [
            pltpu.VMEM((2, width, depth), BF16),
            pltpu.VMEM((2, 3, depth, width), BF16),
            pltpu.VMEM((2, width, depth), BF16),
            pltpu.VMEM((2, depth, width), BF16),
            pltpu.VMEM((width, width), BF16),
            pltpu.SemaphoreType.DMA((12,)),
        ],
        flops=16 * depth * width * width,
        moved=24 * depth * width,
    )


def quad_grad(info, parts, grads, w_back):
    _, sub, rows = parts[0].shape
    width = w_back.shape[1]
    made = (shape((2, 2 * sub // QUAD, width), BF16), whole((2, 2 * sub // QUAD, width)))
    total = QUAD * rows
    return run(
        quad_grad_body,
        info,
        [(v, whole(v.shape)) for v in parts + grads] + [(w_back, ANY)],
        [made, made],
        (1,),
        [
            pltpu.VMEM((sub, width), BF16),
            pltpu.VMEM((sub, total), BF16),
            pltpu.VMEM((sub, total), BF16),
            pltpu.VMEM((width, total), BF16),
            pltpu.VMEM((total, width), BF16),
            pltpu.VMEM((sub, total), BF16),
            pltpu.VMEM((width, width), BF16),
            pltpu.SemaphoreType.DMA((QUAD,)),
        ],
        flops=6 * sub * total * width,
        moved=10 * sub * total,
    )


def to_section(value, source):
    return lax.ppermute(value, "section", [(source, 1 - source)])


def swap_section(value):
    return lax.ppermute(value, "section", [(0, 1), (1, 0)])


def after(value, *earlier):
    return lax.optimization_barrier((value, *earlier))[0]


def added_up(parts):
    total = parts[0].astype(F32)
    for part in parts[1:]:
        total = total + part.astype(F32)
    return total


def cross(value, orders, stage):
    count = lax.axis_size("dp")
    low = count // PIECES
    pairs = []
    for section, order in enumerate(orders):
        base = section * count
        flip = low << order[stage]
        pairs += [(base + n, base + (n ^ flip)) for n in range(count)]
    return lax.ppermute(value, ("section", "dp"), pairs)


def cross_first(value, axis):
    count = lax.axis_size("dp")
    flip = (count // PIECES) << axis
    return lax.ppermute(value, ("section", "dp"), [(n, n ^ flip) for n in range(count)])


class Exchange:
    def __init__(self, stay, go, swap, stages):
        self.stay, self.go, self.swap = stay, go, swap
        self.stages, self.stage, self.flying = stages, 0, None

    def start(self, info):
        if self.stage:
            half = self.stay[0].shape[0] // 2
            self.go = [part[half:] for part in self.stay]
            self.stay = [part[:half] for part in self.stay]
        send = added_up(self.go).astype(BF16) if len(self.go) > 1 else self.go[0]
        info, send = lax.optimization_barrier((info, send))
        self.flying = self.swap(send, self.stage)
        self.stage += 1
        return info

    def total(self):
        assert self.stage == self.stages
        return added_up(self.stay)[0]


def settle(info, *values):
    arrays = [value.flying if isinstance(value, Exchange) else value for value in values]
    info, *arrays = lax.optimization_barrier((info, *arrays))
    plain = []
    for value, array in zip(values, arrays):
        if isinstance(value, Exchange):
            value.stay = value.stay + [array]
        else:
            plain.append(array)
    return (info, *plain)


def share_out(piece):
    count = lax.axis_size("dp")
    low = count // PIECES
    if low > 1:
        rows, cols = piece.shape
        place = lax.axis_index("dp") % low
        parts = jnp.take(piece.reshape(low, rows // low, cols), jnp.arange(low) ^ place, axis=0)
        while parts.shape[0] > 1:
            half = parts.shape[0] // 2
            far = lax.ppermute(parts[half:], "dp", [(n, n ^ half) for n in range(count)])
            parts = parts[:half] + far
        piece = parts[0]
    return piece[None]


def across(value, flip):
    return lax.ppermute(value, "dp", [(n, n ^ flip) for n in range(lax.axis_size("dp"))])


X, Y, Z, ZZ = 0, 1, 2, 3
FEED_ORDERS = ((X, Z, Y, ZZ), (Y, X, Z, ZZ))
QK_ORDERS = ((X, Y, Z, ZZ), (Y, X, Z, ZZ))
V_ORDERS = ((Z, X, Y, ZZ), (Z, Y, X, ZZ))
O_ORDERS = ((Y, Z, X, ZZ), (X, Z, Y, ZZ))
FEED_KEEP, FEED_SEND, SIDE_QK, SIDE_V, SIDE_O = 2, 6, 10, 14, 18


def shards(inputs, out_grad, picks, valid, router, gain_attn, w_qkv, w_out, gain_mlp, w_in, w_back):
    w_qkv, w_out, w_in, w_back = w_qkv[0], w_out[0], w_in[0], w_back[0]
    seqs, cap = picks.shape
    seq_len = inputs.shape[0] // seqs
    width = inputs.shape[1]
    hidden = w_in.shape[1]
    rows = seqs * cap
    tiles = seq_len // TILE
    section = lax.axis_index("section")
    spot = lax.axis_index("dp") // (lax.axis_size("dp") // PIECES)
    first = section == 0

    table = []
    for mine in (0, 1):
        table.append(
            FEED_ORDERS[mine] + FEED_ORDERS[1 - mine] + QK_ORDERS[mine] + V_ORDERS[mine] + O_ORDERS[mine]
        )
    orders = jnp.where(first, jnp.array(table[0]), jnp.array(table[1]))
    info = jnp.concatenate([jnp.stack([section, spot]), orders]).astype(jnp.int32)
    consts = jnp.concatenate([gain_attn, gain_mlp, router[None]], axis=0)

    consts_far = swap_section(consts)
    far_qkv = to_section(w_qkv, 1)

    weight_bufs = [pltpu.VMEM(w.shape, BF16) for w in (w_qkv, w_out, w_in, w_back)]
    weight_bufs.append(pltpu.SemaphoreType.DMA((4,)))
    weight_ins = [(w_qkv, ANY), (w_out, ANY), (w_in, ANY), (w_back, ANY)]

    def full(array):
        return (array, whole(array.shape))

    def made(dims, dtype):
        return (shape(dims, dtype), whole(dims))

    routed_flops = 2 * rows * (4 * width * width + 2 * width * hidden)
    weight_bytes = 2 * (4 * width * width + 2 * width * hidden)
    sub = hidden // QUAD
    (
        chosen, normed0, packed0, mixed0, rows0, stay0, over_x, over_y, slope0, branch0, gate0, open0, near, away,
    ) = run(
        routed_forward_body,
        info,
        [full(v) for v in (inputs, picks, valid, consts)] + weight_ins,
        [
            made((rows, width), BF16),
            made((width, rows), BF16),
            made((rows, 3 * width), BF16),
            made((width, rows), BF16),
            made((rows, width), F32),
            made((3, sub, rows), BF16),
            made((5, sub, rows), BF16),
            made((3, sub, rows), BF16),
            made((rows, hidden), BF16),
            made((rows, width), F32),
            made((rows, LANES), F32),
            made((rows, LANES), F32),
            made((cap, width), BF16),
            made((cap, width), BF16),
        ],
        (1,),
        weight_bufs[:4] + [pltpu.VMEM((rows, hidden), BF16)] + weight_bufs[4:],
        flops=routed_flops,
        moved=weight_bytes,
    )
    info, consts_far, far_qkv, near, away, over_x, over_y, normed0, w_in_now = settle(
        info, consts_far, far_qkv, near, away, over_x, over_y, normed0, w_in
    )
    away = to_section(away, 0)
    far_in = to_section(w_in_now, 1)
    from_x = cross_first(over_x, X)

    def row_tile(dims):
        return pl.BlockSpec(dims, lambda i, info_ref: (i, 0))

    def seq_tile():
        return pl.BlockSpec((TILE, width), lambda i, info_ref: (info_ref[0] * tiles + i, 0))

    def tiled(cols, dtype):
        return (shape((seq_len, cols), dtype), row_tile((TILE, cols)))

    def turned(dtype=BF16):
        return (shape((width, seq_len), dtype), pl.BlockSpec((width, TILE), lambda i, info_ref: (0, i)))

    three_tile = pl.BlockSpec((3, TILE, width), lambda i, info_ref: (0, i, 0))
    three = shape((3, seq_len, width), BF16)

    middle, normed1, packed1 = run(
        dense_in_body,
        info,
        [
            (inputs, seq_tile()),
            full(near),
            full(away),
            full(picks),
            full(consts),
            full(consts_far),
            (w_qkv, ANY),
            (far_qkv, ANY),
        ],
        [tiled(width, F32), turned(), (three, three_tile)],
        (tiles,),
        [pltpu.VMEM(w_qkv.shape, BF16), pltpu.SemaphoreType.DMA],
        flops=6 * seq_len * width * width,
        moved=seq_len * width * 12 + 6 * width * width,
    )

    info, far_in, packed1, normed1, over_y, w_back_now, w_out_now = settle(
        info, far_in, packed1, normed1, over_y, w_back, w_out
    )
    from_y = cross_first(over_y, Y)
    far_back = to_section(w_back_now, 1)
    far_out = to_section(w_out_now, 1)

    pair_spec = pl.BlockSpec((3, seq_len, LANES), lambda h, info_ref: (0, 0, h))
    column_spec = pl.BlockSpec((seq_len, LANES), lambda h, info_ref: (0, h))
    logsum_spec = pl.BlockSpec((1, 8, seq_len), lambda h, info_ref: (h, 0, 0))
    attend_flops = 2 * HEADS * seq_len * seq_len * TILE
    mixed1, logsum1 = run(
        attend_forward_body,
        info,
        [(packed1, pair_spec)],
        [
            (shape((seq_len, width), BF16), column_spec),
            (shape((PAIRS, 8, seq_len), F32), logsum_spec),
        ],
        (PAIRS,),
        flops=attend_flops,
        moved=8 * seq_len * width,
    )

    info, mixed1, from_x, from_y, far_back, far_out, normed1 = settle(
        info, mixed1, from_x, from_y, far_back, far_out, normed1
    )
    from_xy = cross_first(from_x[2:], Y)
    far_normed = to_section(normed1, 0)
    result, act1, hidden1, mid1, turned1, carry, attn1, grad_mixed1, gain_mlp_sum = run(
        feed_body,
        info,
        [
            (mixed1, row_tile((TILE, width))),
            (middle, row_tile((TILE, width))),
            (out_grad, seq_tile()),
            full(consts),
            full(consts_far),
            (w_out, ANY),
            (far_out, ANY),
            (w_in, ANY),
            (far_in, ANY),
            (w_back, ANY),
            (far_back, ANY),
        ],
        [
            tiled(width, BF16),
            tiled(hidden, BF16),
            tiled(hidden, BF16),
            turned(),
            turned(),
            tiled(width, F32),
            tiled(width, BF16),
            tiled(width, BF16),
            made((8, width), F32),
        ],
        (tiles,),
        [
            pltpu.VMEM(w_out.shape, BF16),
            pltpu.VMEM(w_in.shape, BF16),
            pltpu.VMEM(w_back.shape, BF16),
            pltpu.SemaphoreType.DMA((3,)),
        ],
        flops=2 * seq_len * width * (2 * width + 4 * hidden),
        moved=seq_len * (20 * width + 4 * hidden) + 2 * width * (width + 2 * hidden),
    )
    info, mid1, from_xy, far_normed, result, turned1, attn1 = settle(
        info, mid1, from_xy, far_normed, result, turned1, attn1
    )
    far_result = to_section(result, 0)
    far_mixed = to_section(turned1, 0)
    far_attn = to_section(attn1, 0)

    def own_seq(t, info_ref):
        return (info_ref[0], 0)

    feed_args = (mid1, hidden1, act1, out_grad)
    feed_send = feed_grad(info, FEED_SEND, *feed_args, True, own_seq)
    info, feed_send, far_result, far_mixed, far_attn = settle(info, feed_send, far_result, far_mixed, far_attn)
    feed_far = swap_section(feed_send)
    feed_keep = feed_grad(info, FEED_KEEP, *feed_args, False, own_seq)
    info, feed_keep, feed_far = settle(info, feed_keep, feed_far)
    half = PIECES // 2
    feed = Exchange(
        [feed_keep[:half], feed_far[:half]],
        [feed_keep[half:], feed_far[half:]],
        lambda value, stage: cross(value, FEED_ORDERS, stage),
        STAGES,
    )
    info = feed.start(info)

    packed_grad1 = run(
        attend_backward_body,
        info,
        [(packed1, pair_spec), (grad_mixed1, column_spec), (mixed1, column_spec), (logsum1, logsum_spec)],
        [(three, pair_spec)],
        (PAIRS,),
        [pltpu.VMEM((seq_len, LANES), F32)],
        flops=5 * attend_flops // 2,
        moved=16 * seq_len * width,
    )[0]
    info, packed_grad1 = settle(info, packed_grad1, feed)
    info = feed.start(info)
    far_packed = to_section(packed_grad1, 0)

    grad_middle, near_sel, gain_attn_sum = run(
        dense_out_body,
        info,
        [
            (packed_grad1, three_tile),
            (carry, row_tile((TILE, width))),
            (middle, row_tile((TILE, width))),
            full(consts),
            full(consts_far),
            full(picks),
            (w_qkv, ANY),
            (far_qkv, ANY),
        ],
        [tiled(width, BF16), made((cap, width), BF16), made((8, width), F32)],
        (tiles,),
        [pltpu.VMEM(w_qkv.shape, BF16), pltpu.VMEM((cap, width), F32), pltpu.SemaphoreType.DMA],
        flops=6 * seq_len * width * width,
        moved=seq_len * width * 16 + 6 * width * width,
    )
    info, near_sel, grad_middle, far_packed = settle(info, near_sel, grad_middle, far_packed, feed)
    far_sel = to_section(near_sel, 1)
    info = feed.start(info)
    far_grad = to_section(grad_middle, 1)
    sel = jnp.concatenate([near_sel, far_sel], axis=0)
    g_own = (sel.astype(F32) * open0[:, 0:1]).astype(BF16)
    g_x = cross_first(g_own, X)
    g_y = cross_first(g_own, Y)
    attn0, packed_grad0, grad_chosen, small0 = run(
        routed_backward_body,
        info,
        [full(v) for v in (near_sel, far_sel, chosen, packed0, rows0, slope0, branch0, gate0, valid, consts)]
        + weight_ins,
        [
            made((rows, width), BF16),
            made((3, rows, width), BF16),
            made((rows, width), F32),
            made((8, width), F32),
        ],
        (1,),
        weight_bufs[:4] + [pltpu.VMEM((rows, hidden), BF16)] + weight_bufs[4:],
        flops=routed_flops,
        moved=weight_bytes,
    )
    info, small0, packed_grad0, far_grad, g_x, g_y = settle(info, small0, packed_grad0, far_grad, g_x, g_y, feed)
    info = feed.start(info)
    g_xy = cross_first(g_x, Y)
    small = jnp.where(first, small0, 0.0) + gain_mlp_sum + gain_attn_sum
    small_far = swap_section(small)

    qk_stay, qk_go, v_stay, v_go, o_stay, o_go = side_grad(
        info,
        [normed0, packed_grad0, mixed0, attn0],
        [normed1, far_normed, packed_grad1, far_packed, turned1, far_mixed, attn1, far_attn],
    )
    side = [
        Exchange([stay], [go], functools.partial(lambda orders, value, stage: cross(value, orders, stage), orders), STAGES)
        for stay, go, orders in ((qk_stay, qk_go, QK_ORDERS), (v_stay, v_go, V_ORDERS), (o_stay, o_go, O_ORDERS))
    ]
    info, g_xy, *gone, small_far = settle(info, g_xy, qk_go, v_go, o_go, small_far, feed)
    small = small + small_far
    small_far = across(small, 1)
    for chain, go in zip(side, gone):
        chain.go = [go]
        info = chain.start(info)

    quad_go, quad_stay = quad_grad(info, [stay0, from_x, from_y, from_xy], [g_own, g_x, g_y, g_xy], w_back)
    info, quad_go, small_far = settle(info, quad_go, small_far)
    small = small + small_far
    small_far = across(small, 2)
    quad = Exchange([quad_stay], [quad_go], lambda value, stage: cross_first(value, (Z, ZZ)[stage]), 2)
    info = quad.start(info)

    end_spec = pl.BlockSpec((TILE, width), lambda s, i, info_ref: (i, 0))
    ends = run(
        ends_body,
        info,
        [
            (result, end_spec),
            (grad_middle, end_spec),
            (far_result, end_spec),
            (far_grad, end_spec),
            (grad_chosen, pl.BlockSpec((cap, width), lambda s, i, info_ref: (s, 0))),
            (picks, pl.BlockSpec((seqs, cap), lambda s, i, info_ref: (0, 0))),
        ],
        [
            (
                shape((seqs * seq_len, width), BF16),
                pl.BlockSpec((TILE, width), lambda s, i, info_ref: (s * tiles + i, 0)),
            )
        ],
        (seqs, tiles),
        flops=4 * seqs * seq_len * cap * width,
        moved=8 * seqs * seq_len * width,
    )[0]

    info, ends, small_far = settle(info, ends, small_far, *side)
    small = small + small_far
    small_far = across(small, 4)
    for chain in side:
        info = chain.start(info)
    info, small_far = settle(info, small_far, quad)
    info = quad.start(info)
    small = small + small_far
    small_far = across(small, 8)
    info, = settle(info, *side)
    for chain in side:
        info = chain.start(info)
    info, small_far = settle(info, small_far, *side)
    small = small + small_far
    for step in range(PIECES, lax.axis_size("dp"), PIECES):
        small = small + across(small, step)
    for chain in side:
        info = chain.start(info)
    settle(info, quad, *side)
    share = width // lax.axis_size("dp")

    def gain_share(routed_row, dense_row):
        row = jnp.where(first, small[routed_row], small[dense_row])
        return lax.dynamic_slice_in_dim(row, lax.axis_index("dp") * share, share)[None]

    piece = width // PIECES
    member = spot & 3
    quad_sum = quad.total()
    back0, in0 = quad_sum[: hidden // PIECES], quad_sum[hidden // PIECES :]
    in0 = jnp.take(in0.reshape(QUAD, piece, width), jnp.array([0, 2, 1, 3]) ^ member, axis=0)
    in0 = jnp.concatenate([in0[:2], cross_first(in0[2:], X)], axis=0)
    in0 = jnp.concatenate([in0[0::2], cross_first(in0[1::2], Y)], axis=0)
    in0 = jnp.take(in0, jnp.arange(QUAD) ^ member, axis=0)
    in0 = in0.reshape(QUAD, piece, QUAD, hidden // PIECES).transpose(1, 2, 0, 3).reshape(piece, hidden)

    feed1 = feed.total()
    in1 = feed1.reshape(QUAD, piece, width).transpose(1, 0, 2).reshape(piece, hidden)
    back1 = to_section(feed1, 0)
    qk, v, out = [chain.total() for chain in side]
    return (
        ends[None],
        small[0],
        gain_share(2, 4),
        share_out(jnp.concatenate([qk[:piece], qk[piece:], v], axis=1)),
        share_out(out),
        gain_share(1, 3),
        share_out(jnp.where(first, in0, in1)),
        share_out(jnp.where(first, back0, back1)),
    )


def solution(mesh):
    placed = (
        P("dp", None),
        P("dp", None),
        P("dp", None),
        P("dp", None),
        P(),
        P("section", None),
        P("section", None, None),
        P("section", None, None),
        P("section", None),
        P("section", None, None),
        P("section", None, None),
    )
    return jax.shard_map(
        shards,
        mesh=mesh,
        in_specs=placed,
        out_specs=(
            P("section", "dp", None),
            P(),
            P("section", "dp"),
            P("section", "dp", None),
            P("section", "dp", None),
            P("section", "dp"),
            P("section", "dp", None),
            P("section", "dp", None),
        ),
        check_vma=False,
    )
```

```python
import functools

import jax
import jax.numpy as jnp
from jax import lax
from jax.experimental import pallas as pl
from jax.experimental.pallas import tpu as pltpu
from jax.sharding import PartitionSpec as P

HEADS = 12
HEAD_DIM = 64
LANES = 128
PAIRS = HEADS * HEAD_DIM // LANES
EPS = 1e-06
FACTOR = HEAD_DIM ** (-0.5)
PIECES = 16
STAGES = 4
QUAD = 4
EXTRA = 16
TILE = 256
VMEM_BYTES = 56 * 1024 * 1024
BF16 = jnp.bfloat16
F32 = jnp.float32


def nn(a, b):
    return lax.dot_general(a, b, (((1,), (0,)), ((), ())), preferred_element_type=F32)


def nt(a, b):
    return lax.dot_general(a, b, (((1,), (1,)), ((), ())), preferred_element_type=F32)


def tn(a, b):
    return lax.dot_general(a, b, (((0,), (0,)), ((), ())), preferred_element_type=F32)


def shape(dims, dtype):
    return jax.ShapeDtypeStruct(dims, dtype)


def whole(dims):
    zeros = (0,) * len(dims)
    return pl.BlockSpec(dims, lambda *_: zeros)


ANY = pl.BlockSpec(memory_space=pl.ANY)


def run(body, info, ins, outs, grid, scratch=(), flops=0, moved=0, aliases=()):
    arrays, in_specs = zip(*ins)
    shapes, out_specs = zip(*outs)
    return pl.pallas_call(
        body,
        out_shape=shapes,
        input_output_aliases=dict(aliases),
        grid_spec=pltpu.PrefetchScalarGridSpec(
            num_scalar_prefetch=1,
            grid=grid,
            in_specs=in_specs,
            out_specs=out_specs,
            scratch_shapes=scratch,
        ),
        compiler_params=pltpu.CompilerParams(
            vmem_limit_bytes=VMEM_BYTES, dimension_semantics=("arbitrary",) * len(grid)
        ),
        cost_estimate=pl.CostEstimate(flops=flops // 4, bytes_accessed=moved // 4, transcendentals=0),
    )(info, *arrays)


def top_lanes(rows):
    return lax.broadcasted_iota(jnp.int32, (rows, LANES), 1) < HEAD_DIM


def lane_head(rows, which):
    lane = lax.broadcasted_iota(jnp.int32, (rows, LANES), 1)
    return (lane < HEAD_DIM) if which == 0 else (lane >= HEAD_DIM)


def head_only(value, which):
    return jnp.where(lane_head(value.shape[0], which), value, jnp.zeros_like(value))


def mean_square_scale(rows):
    return lax.rsqrt(jnp.mean(rows * rows, axis=-1, keepdims=True) + EPS)


def norm_back(grad, rows, scale, gain):
    hat = rows * scale
    scaled = grad * gain
    back = scale * (scaled - hat * jnp.mean(scaled * hat, axis=-1, keepdims=True))
    return back, jnp.sum(grad * hat, axis=0, keepdims=True)


def gelu_parts(pre):
    root = 0.7978845608028654
    square = pre * pre
    bent = jnp.tanh(root * pre * (1.0 + 0.044715 * square))
    half = 0.5 * (1.0 + bent)
    slope = half + 0.5 * pre * (1.0 - bent * bent) * (root * (1.0 + 0.134145 * square))
    return pre * half, slope


def fetch(info, local, remote, buf, sem):
    @pl.when(info[0] == 1)
    def _():
        pltpu.make_async_copy(local, buf, sem).start()

    @pl.when(info[0] == 0)
    def _():
        pltpu.make_async_copy(remote, buf, sem).start()


def arrived(source, buf, sem):
    pltpu.make_async_copy(source, buf, sem).wait()


def stacked(value):
    return jnp.concatenate([head_only(value, h) for h in range(2)], axis=0)


def unstacked(value):
    half = value.shape[0] // 2
    return jnp.where(top_lanes(half), value[:half], value[half:])


def slot_pieces(packed, seq, pair, cap):
    rows = slice(seq * cap, (seq + 1) * cap)
    width = HEADS * HEAD_DIM
    first = pair * LANES
    queries = stacked(packed[rows, first : first + LANES] * BF16(FACTOR))
    keys = packed[rows, width + first : width + first + LANES]
    values = packed[rows, 2 * width + first : 2 * width + first + LANES]
    return queries, keys, values


def slot_rule(valid_row, cap):
    query = lax.broadcasted_iota(jnp.int32, (cap, cap), 0)
    key = lax.broadcasted_iota(jnp.int32, (cap, cap), 1)
    rule = (key <= query) & ((valid_row > 0) | (key == query))
    return jnp.concatenate([rule, rule], axis=0)


def column_of(row):
    return jnp.transpose(jnp.broadcast_to(row, (row.shape[1], row.shape[1])))


def slot_mask(valid):
    seqs = valid.shape[0]
    return jnp.concatenate([column_of(valid[s : s + 1, :].astype(F32)) for s in range(seqs)], axis=0)[:, 0:1]


def weight_copies(sources, bufs, sems):
    return [pltpu.make_async_copy(a, b, sems.at[n]) for n, (a, b) in enumerate(zip(sources, bufs))]


def routed_forward_body(
    info, x, picks, valid, gain_attn, gain_mlp, router, w_qkv, w_out, w_in, w_back,
    chosen_o, normed_o, packed_o, mixed_o, rows_o, slope_o, branch_o, gate_o, open_o, near_o, away_o,
    stay_o, over_x_o, over_y_o, over_xy_o,
    b_qkv, b_out, b_in, b_back, act_b, shares, sems, out_sems,
):
    @pl.when(info[0] == 1)
    def _():
        rest = jnp.concatenate([gain_attn[...], gain_mlp[...]], axis=0)
        count = away_o.shape[0] - EXTRA
        for part in range(3):
            rounded = rest.astype(BF16)
            away_o[count + 2 * part : count + 2 * part + 2, :] = rounded
            rest = rest - rounded.astype(F32)

    @pl.when(info[0] == 0)
    def _():
        copies = weight_copies((w_qkv, w_out, w_in, w_back), (b_qkv, b_out, b_in, b_back), sems)
        for copy in copies:
            copy.start()
        seqs, cap = valid.shape
        seq_len = x.shape[0] // seqs
        parts = []
        for seq in range(seqs):
            place = lax.broadcasted_iota(jnp.int32, (seq_len, cap), 0)
            hot = (picks[seq : seq + 1, :] == place).astype(BF16)
            parts.append(tn(hot, x[seq * seq_len : (seq + 1) * seq_len, :]))
        chosen = jnp.concatenate(parts, axis=0)
        chosen_o[...] = chosen.astype(BF16)
        gates = jax.nn.sigmoid(jnp.sum(chosen * router[...], axis=-1, keepdims=True))
        gate_o[...] = jnp.broadcast_to(gates, gate_o.shape)
        normed = (chosen * mean_square_scale(chosen) * gain_attn[...]).astype(BF16)
        normed_o[...] = normed
        copies[0].wait()
        packed_o[...] = nn(normed, b_qkv[...]).astype(BF16)
        work = [(seq, pair) for seq in range(seqs) for pair in range(PAIRS)]
        allowed = [slot_rule(valid[seq : seq + 1, :], cap) for seq in range(seqs)]
        pieces = [slot_pieces(packed_o, seq, pair, cap) for seq, pair in work]
        scores = [jnp.where(allowed[w[0]], nt(p[0], p[1]), -1e30) for w, p in zip(work, pieces)]
        grown = [jnp.exp(v - jnp.max(v, axis=-1, keepdims=True)).astype(BF16) for v in scores]
        ones = jnp.ones((cap, LANES), BF16)
        outs = [nn(g, jnp.concatenate([p[2], ones], axis=1)) for g, p in zip(grown, pieces)]
        outs = [unstacked(o[:, :LANES] / o[:, LANES:]).astype(BF16) for o in outs]
        mixed = jnp.concatenate(
            [jnp.concatenate(outs[s * PAIRS : (s + 1) * PAIRS], axis=1) for s in range(seqs)], axis=0
        )
        mixed_o[...] = mixed
        copies[1].wait()
        attn_out = nn(mixed, b_out[...])
        rows = chosen + attn_out
        rows_o[...] = rows
        normed_mid = (rows * mean_square_scale(rows) * gain_mlp[...]).astype(BF16)
        member = info[1] & 3
        piece = b_in.shape[1] // PIECES
        mid_turned = jnp.transpose(normed_mid)
        count = mid_turned.shape[0] // PIECES
        sub = piece * QUAD
        slopes_at = sub + QUAD * count
        for dest in range(PIECES):
            at = sub + dest // QUAD * count
            shares[(dest % QUAD) ^ member, at : at + count, :] = mid_turned[dest * count : (dest + 1) * count, :]
        copies[2].wait()
        step = 768
        for first in range(0, b_in.shape[1], step):
            cols = slice(first, first + step)
            act, slope = gelu_parts(nn(normed_mid, b_in[:, cols]))
            act = act.astype(BF16)
            slope = slope.astype(BF16)
            act_b[:, cols] = act
            slope_o[:, cols] = slope
            chunk = first // step
            turned = jnp.transpose(slope)
            for relative in range(QUAD):
                shares[relative, slopes_at + first : slopes_at + first + step, :] = turned
            turned = jnp.transpose(act)
            for owner in range(QUAD):
                shares[owner ^ member, chunk * piece : (chunk + 1) * piece, :] = turned[
                    owner * piece : (owner + 1) * piece, :
                ]
        sends = [
            pltpu.make_async_copy(shares.at[n], out, out_sems.at[n])
            for n, out in enumerate((stay_o, over_x_o, over_y_o, over_xy_o))
        ]
        for send in sends:
            send.start()
        copies[3].wait()
        branch = attn_out + nn(act_b[...], b_back[...])
        branch_o[...] = branch
        opened = gates * slot_mask(valid)
        open_o[...] = jnp.broadcast_to(opened, open_o.shape)
        delta = (opened * branch).astype(BF16)
        near_o[...] = delta[:cap]
        away_o[:cap, :] = delta[cap:]
        for send in sends:
            send.wait()


def routed_backward_body(
    info, p_near, p_far, r_near, r_far, chosen_i, packed, rows_i, slope, branch, gate, valid, gain_attn, gain_mlp, router, swapped,
    w_next, w_qkv, w_out, w_in, w_back,
    ffn_o, attn_o, packed_o, chosen_o, small_o,
    b_qkv, b_out, b_in, b_back, hidden_b, sems,
):
    @pl.when(info[0] == 0)
    def _():
        copies = weight_copies((w_qkv, w_out, w_in, w_back), (b_qkv, b_out, b_in, b_back), sems)
        upper = pltpu.make_async_copy(w_next, b_qkv, sems.at[4])
        upper.start()
        for n in (3, 2, 1):
            copies[n].start()
        seqs, cap = valid.shape
        chosen = chosen_i[...].astype(F32)
        width = chosen.shape[1]
        upper.wait()
        upper_gain = dense_gain(info, gain_attn, swapped, 0)
        grad_sel = []
        for dense, carried in ((p_near, r_near), (p_far, r_far)):
            grad_normed = sum(nt(dense[n], b_qkv[:, n * width : (n + 1) * width]) for n in range(3))
            middle = carried[1]
            back, _ = norm_back(grad_normed, middle, mean_square_scale(middle), upper_gain)
            grad_sel.append((carried[0] + back).astype(BF16).astype(F32))
        grad_sel = jnp.concatenate(grad_sel, axis=0)
        copies[0].start()
        gates = gate[:, 0:1]
        mask = slot_mask(valid)
        logit = jnp.sum(grad_sel * branch[...], axis=-1, keepdims=True) * mask * gates * (1.0 - gates)
        grad = grad_sel * (gates * mask)
        grad_ffn = grad.astype(BF16)
        ffn_o[...] = grad_ffn
        copies[3].wait()
        copies[2].wait()
        step = 768
        for first in range(0, b_in.shape[1], step):
            cols = slice(first, first + step)
            hidden = (nt(grad_ffn, b_back[cols, :]) * slope[:, cols].astype(F32)).astype(BF16)
            hidden_b[:, cols] = hidden
        grad_mid = nt(hidden_b[...], b_in[...])
        rows = rows_i[...]
        grad_rows, gain_mlp_sum = norm_back(grad_mid, rows, mean_square_scale(rows), gain_mlp[...])
        grad_attn = (grad + grad_rows).astype(BF16)
        attn_o[...] = grad_attn
        copies[1].wait()
        grad_mixed = nt(grad_attn, b_out[...]).astype(BF16)
        work = [(seq, pair) for seq in range(seqs) for pair in range(PAIRS)]
        allowed = [slot_rule(valid[seq : seq + 1, :], cap) for seq in range(seqs)]
        pieces = [slot_pieces(packed, seq, pair, cap) for seq, pair in work]
        grads = [
            stacked(grad_mixed[seq * cap : (seq + 1) * cap, pair * LANES : (pair + 1) * LANES])
            for seq, pair in work
        ]
        scores = [jnp.where(allowed[w[0]], nt(p[0], p[1]), -1e30) for w, p in zip(work, pieces)]
        grad_probs = [nt(g, p[2]) for g, p in zip(grads, pieces)]
        grown = [jnp.exp(v - jnp.max(v, axis=-1, keepdims=True)) for v in scores]
        probs = [v / jnp.sum(v, axis=-1, keepdims=True) for v in grown]
        lows = [
            (p * (g - jnp.sum(p * g, axis=-1, keepdims=True))).astype(BF16) for p, g in zip(probs, grad_probs)
        ]
        for (seq, pair), piece, grad_head, prob, low in zip(work, pieces, grads, probs, lows):
            at = slice(seq * cap, (seq + 1) * cap)
            cols = slice(pair * LANES, (pair + 1) * LANES)
            packed_o[0, at, cols] = (unstacked(nn(low, piece[1])) * FACTOR).astype(BF16)
            packed_o[1, at, cols] = tn(low, piece[0]).astype(BF16)
            packed_o[2, at, cols] = tn(prob.astype(BF16), grad_head).astype(BF16)
        copies[0].wait()
        grad_normed = sum(nt(packed_o[n], b_qkv[:, n * width : (n + 1) * width]) for n in range(3))
        back, gain_attn_sum = norm_back(grad_normed, chosen, mean_square_scale(chosen), gain_attn[...])
        chosen_o[...] = grad_rows + back + logit * router[...]
        small_o[...] = jnp.zeros(small_o.shape, F32)
        small_o[0:1, :] = jnp.sum(logit * chosen, axis=0, keepdims=True)
        small_o[1:2, :] = gain_mlp_sum
        small_o[2:3, :] = gain_attn_sum


def dense_gain(info, local, swapped, row):
    first = swapped.shape[0] - EXTRA + row
    far = sum(swapped[first + n : first + n + 1, :].astype(F32) for n in (0, 2, 4))
    return jnp.where(info[0] == 1, local[...], far)


def dense_in_body(
    info, x, near, away, picks, gain, w_local, w_far, middle_o, normed_o, packed_o, sel_o, b_qkv, sem
):
    step = pl.program_id(0)

    @pl.when(step == 0)
    def _():
        fetch(info, w_local, w_far, b_qkv, sem)

    rows, width = x.shape
    cap = near.shape[0]
    delta = jnp.where(info[0] == 0, near[...], away[:cap, :])
    place = step * rows + lax.broadcasted_iota(jnp.int32, (rows, cap), 0)
    hot = (picks[pl.ds(info[0], 1), :] == place).astype(BF16)
    middle = x[...].astype(F32) + nn(hot, delta)
    middle_o[...] = middle

    @pl.when(step == 0)
    def _():
        sel_o[...] = delta.astype(F32)

    sel_o[...] += tn(hot, x[...])
    normed = (middle * mean_square_scale(middle) * dense_gain(info, gain, away, 0)).astype(BF16)
    normed_o[...] = normed

    @pl.when(step == 0)
    def _():
        arrived(w_local, b_qkv, sem)

    for n in range(3):
        packed_o[n] = nn(normed, b_qkv[:, n * width : (n + 1) * width]).astype(BF16)


def attend_forward_body(info, packed, mixed_o, logsum_o):
    seq_len = packed.shape[1]
    tile = 2 * TILE
    queries = packed[0] * BF16(FACTOR)
    keys = packed[1]
    ones = jnp.ones((seq_len, LANES), BF16)
    values = [jnp.concatenate([head_only(packed[2], h), ones], axis=1) for h in range(2)]
    below = lax.broadcasted_iota(jnp.int32, (tile, tile), 1) <= lax.broadcasted_iota(jnp.int32, (tile, tile), 0)
    for first in range(0, seq_len, tile):
        upto = first + tile
        at = slice(first, upto)
        scores = []
        for head in range(2):
            score = nt(head_only(queries[at], head), keys[:upto])
            last = jnp.where(below, score[:, first:], -1e30)
            scores.append(jnp.concatenate([score[:, :first], last], axis=1) if first else last)
        tops = [jnp.max(score, axis=-1, keepdims=True) for score in scores]
        grown = [jnp.exp(score - top).astype(BF16) for score, top in zip(scores, tops)]
        outs = [nn(g, value[:upto]) for g, value in zip(grown, values)]
        mixed = sum(out[:, :LANES] * (1.0 / out[:, LANES:]) for out in outs)
        mixed_o[at, :] = mixed.astype(BF16)
        sums = [top + jnp.log(out[:, LANES:]) for top, out in zip(tops, outs)]
        turned = jnp.transpose(jnp.where(top_lanes(tile), sums[0], sums[1]))
        logsum_o[0, 0:1, at] = turned[0:1]
        logsum_o[0, 1:2, at] = turned[HEAD_DIM : HEAD_DIM + 1]


def attend_backward_body(info, packed, grad, mixed, logsum, picks, *refs):
    out, sel_o, grad_q = refs[-3:]
    seq_len = packed.shape[1]
    queries = packed[0] * BF16(FACTOR)
    queries = [head_only(queries, h) for h in range(2)]
    key_heads = [head_only(packed[1], h) for h in range(2)]
    grads = [head_only(grad[...], h) for h in range(2)]
    product = grad[...].astype(F32) * mixed[...].astype(F32)
    pick_row = lax.broadcasted_iota(jnp.int32, (8, LANES), 0)
    pick_lane = lax.broadcasted_iota(jnp.int32, (8, LANES), 1)
    pick = (pick_row == pick_lane // HEAD_DIM).astype(F32)
    inner = lax.dot_general(
        pick, product, (((1,), (1,)), ((), ())), precision=lax.Precision.HIGHEST, preferred_element_type=F32
    )
    above = lax.broadcasted_iota(jnp.int32, (TILE, TILE), 0) <= lax.broadcasted_iota(
        jnp.int32, (TILE, TILE), 1
    )
    for first in range(0, seq_len, TILE):
        kat = slice(first, first + TILE)
        keys = packed[1, kat, :]
        values = packed[2, kat, :]
        dks, dvs, dqs = [], [], []
        for head in range(2):
            query = queries[head][first:]
            grad_head = grads[head][first:]
            probs = jnp.exp(nt(keys, query) - logsum[0, head : head + 1, first:])
            edge = jnp.where(above, probs[:, :TILE], 0.0)
            probs = jnp.concatenate([edge, probs[:, TILE:]], axis=1) if first + TILE < seq_len else edge
            grad_probs = nt(values, grad_head)
            low = (probs * (grad_probs - inner[head : head + 1, first:])).astype(BF16)
            dvs.append(nn(probs.astype(BF16), grad_head))
            dks.append(nn(low, query))
            dqs.append(tn(low, key_heads[head][kat]))
        if first == 0:
            grad_q[...] = dqs[0] + dqs[1]
        else:
            grad_q[first:, :] += dqs[0] + dqs[1]
        out[1, kat, :] = (dks[0] + dks[1]).astype(BF16)
        out[2, kat, :] = (dvs[0] + dvs[1]).astype(BF16)
    out[0] = (grad_q[...] * FACTOR).astype(BF16)
    cap = picks.shape[1]
    place = lax.broadcasted_iota(jnp.int32, (seq_len, cap), 0)
    hot = (picks[pl.ds(info[0], 1), :] == place).astype(BF16)
    for n in range(3):
        sel_o[n] = tn(hot, out[n]).astype(BF16)


def feed_body(
    info, mixed, normed, middle, out_grad, gain_in, swapped, picks, middle_sel, wo_l, wo_f, wi_l, wi_f, wb_l, wb_f,
    pack_o, act_o, hidden_o, mid_o, carry_o, mixed_o, gain_o, sel_o,
    b_out, b_in, b_back, sems,
):
    step = pl.program_id(0)

    @pl.when(step == 0)
    def _():
        fetch(info, wo_l, wo_f, b_out, sems.at[0])
        fetch(info, wi_l, wi_f, b_in, sems.at[1])
        fetch(info, wb_l, wb_f, b_back, sems.at[2])
        gain_o[...] = jnp.zeros(gain_o.shape, F32)
        sel_o[0] = jnp.zeros(middle_sel.shape, F32)
        sel_o[1] = middle_sel[...]
        arrived(wo_l, b_out, sems.at[0])

    gain = dense_gain(info, gain_in, swapped, 1)
    pack_o[2] = mixed[...]
    pack_o[3] = normed[...]
    rows = middle[...] + nn(mixed[...], b_out[...])
    scale = mean_square_scale(rows)
    normed_mid = (rows * scale * gain).astype(BF16)
    mid_o[...] = normed_mid

    @pl.when(step == 0)
    def _():
        arrived(wi_l, b_in, sems.at[1])
        arrived(wb_l, b_back, sems.at[2])

    grad_ffn = out_grad[...]
    width = 768
    for first in range(0, b_in.shape[1], width):
        cols = slice(first, first + width)
        act, slope = gelu_parts(nn(normed_mid, b_in[:, cols]))
        act_o[:, cols] = act.astype(BF16)
        hidden_o[:, cols] = (nt(grad_ffn, b_back[cols, :]) * slope).astype(BF16)
    pack_o[0] = (rows + nn(act_o[...], b_back[...])).astype(BF16)
    grad_mid = nt(hidden_o[...], b_in[...])
    back, gain_sum = norm_back(grad_mid, rows, scale, gain)
    carry = grad_ffn.astype(F32) + back
    carry_o[...] = carry
    grad_attn = carry.astype(BF16)
    pack_o[1] = grad_attn
    mixed_o[...] = nt(grad_attn, b_out[...]).astype(BF16)
    gain_o[3:4, :] += gain_sum
    count, cap = carry.shape[0], middle_sel.shape[0]
    place = step * count + lax.broadcasted_iota(jnp.int32, (count, cap), 0)
    hot = (picks[pl.ds(info[0], 1), :] == place).astype(BF16)
    sel_o[0] += tn(hot, grad_attn) + tn(hot, (carry - grad_attn.astype(F32)).astype(BF16))


def dense_out_body(
    info, packed, carry, middle, gain_in, swapped, w_local, w_far, grad_o, gain_o, b_qkv, sem
):
    step = pl.program_id(0)

    @pl.when(step == 0)
    def _():
        fetch(info, w_local, w_far, b_qkv, sem)
        gain_o[...] = jnp.zeros(gain_o.shape, F32)
        arrived(w_local, b_qkv, sem)

    width = middle.shape[1]
    grad_normed = sum(nt(packed[n], b_qkv[:, n * width : (n + 1) * width]) for n in range(3))
    rows = middle[...]
    gain = dense_gain(info, gain_in, swapped, 0)
    back, gain_sum = norm_back(grad_normed, rows, mean_square_scale(rows), gain)
    gain_o[4:5, :] += gain_sum
    grad_o[...] = (carry[...] + back).astype(BF16)


def ends_body(info, result_block, grad, far_block, far_grad, grad_chosen, picks, out):
    seq = pl.program_id(0)
    step = pl.program_id(1)

    @pl.when(info[0] == 1)
    def _():
        out[...] = jnp.where(seq == 1, result_block[0], far_block[0])

    @pl.when(info[0] == 0)
    def _():
        base = jnp.where(seq == 0, grad[...], far_grad[...]).astype(F32)
        rows = out.shape[0]
        cap = grad_chosen.shape[0]
        place = step * rows + lax.broadcasted_iota(jnp.int32, (rows, cap), 0)
        hot = (picks[pl.ds(seq, 1), :] == place).astype(BF16)
        high = grad_chosen[...].astype(BF16)
        low = (grad_chosen[...] - high.astype(F32)).astype(BF16)
        out[...] = (base + (nn(hot, high) + nn(hot, low))).astype(BF16)


def picked(info, refs):
    if len(refs) == 1:
        return refs[0][...]
    return jnp.where(info[0] == 0, refs[0][...], refs[1][...])


def put_block(info, base, out, product, slot):
    piece = product.shape[0] // PIECES
    for dest in range(PIECES):
        out[position(info, base, dest), slot * piece : (slot + 1) * piece, :] = product[
            dest * piece : (dest + 1) * piece, :
        ]


def feed_grad_body(
    info, mid, hidden, act, out_grad, out, mid_b, grad_b, hidden_b, act_b, ring_in, ring_back, in_sems, out_sems
):
    steps, rows, width = hidden_b.shape
    piece = width // PIECES

    def load(source, target, n):
        return pltpu.make_async_copy(source, target, in_sems.at[n])

    mine = pl.ds(pl.multiple_of(info[0] * rows, rows), rows)
    loads = [load(mid, mid_b, 0)]
    loads += [load(hidden.at[:, pl.ds(t * width, width)], hidden_b.at[t], 1 + t) for t in range(steps)]
    loads += [load(out_grad.at[mine], grad_b, 1 + steps)]
    loads += [load(act.at[:, pl.ds(t * width, width)], act_b.at[t], 2 + steps + t) for t in range(steps)]
    for copy in loads:
        copy.start()
    sent = []
    for n in range(2 * steps):
        t = n % steps
        if t == 0:
            loads[0 if n == 0 else 1 + steps].wait()
        loads[1 + t if n < steps else 2 + steps + t].wait()
        product = tn(mid_b[...], hidden_b[t]) if n < steps else tn(act_b[t], grad_b[...])
        ring = ring_in if n < steps else ring_back
        if t >= 2:
            sent[n - 2].wait()
        ring[n % 2] = product.astype(BF16).reshape(ring.shape[1:])
        target = out.at[1, :, :, pl.ds(t * piece, piece)] if n < steps else out.at[0, t]
        sent.append(pltpu.make_async_copy(ring.at[n % 2], target, out_sems.at[n // steps, n % 2]))
        sent[-1].start()
    for n in (steps - 2, steps - 1, 2 * steps - 2, 2 * steps - 1):
        sent[n].wait()


def origin(info, base, place):
    relative = 0
    for stage in range(STAGES):
        if place >> (STAGES - 1 - stage) & 1:
            relative = relative | (1 << info[base + stage])
    return info[1] ^ relative


def put_block(info, base, outs, product, slot, buf):
    piece = product.shape[0] // PIECES
    buf[...] = product.astype(BF16)
    at = slice(slot * piece, (slot + 1) * piece)
    for place in range(PIECES):
        dest = origin(info, base, place)
        rows = pl.ds(pl.multiple_of(dest * piece, piece), piece)
        outs[0 if place < PIECES // 2 else 1][place % (PIECES // 2), at, :] = buf[rows, :]


def side_grad_body(
    info, normed0, packed0, mixed0, attn0,
    p_near, p_far, near, far,
    out_stay, out_go,
    n_buf, p_buf, m_buf, a_buf, buf, sems,
):
    outs = (out_stay, out_go)

    @pl.when(info[0] == 0)
    def _():
        for n in range(3):
            put_block(info, SIDE, outs, tn(normed0[...], packed0[n]), n, buf)
        put_block(info, SIDE, outs, tn(mixed0[...], attn0[...]), 3, buf)

    @pl.when(info[0] == 1)
    def _():
        sources = [
            (source.at[which], target, n)
            for which, target in ((2, m_buf), (1, a_buf), (3, n_buf))
            for n, source in enumerate((near, far))
        ]
        copies = [
            pltpu.make_async_copy(source, target.at[n], sems.at[k])
            for k, (source, target, n) in enumerate(sources)
        ]
        blocks = [
            pltpu.make_async_copy(source.at[which], p_buf.at[n, which], sems.at[6 + 2 * which + n])
            for which in range(3)
            for n, source in enumerate((p_near, p_far))
        ]
        for copy in copies + blocks:
            copy.start()
        for copy in copies[:4]:
            copy.wait()
        put_block(info, SIDE, outs, tn(m_buf[0], a_buf[0]) + tn(m_buf[1], a_buf[1]), 3, buf)
        for copy in copies[4:]:
            copy.wait()
        for which in range(3):
            blocks[2 * which].wait()
            blocks[2 * which + 1].wait()
            product = tn(n_buf[0], p_buf[0, which]) + tn(n_buf[1], p_buf[1, which])
            put_block(info, SIDE, outs, product, which, buf)


def quad_grad_body(
    info, stay, from_x, from_y, from_xy, g_own, g_x, g_y, g_xy, w_back, go_o, stay_o,
    b_back, acts, slopes, mids, grads, hidden, sems,
):
    @pl.when(info[0] == 0)
    def _():
        rows = g_own.shape[0]
        width = grads.shape[1]
        sub = acts.shape[0]
        steps = b_back.shape[0] // width
        piece = sub // QUAD
        count = mids.shape[0] // QUAD
        copies = []

        def load(source, target, n, k):
            copies.append(pltpu.make_async_copy(source, target, sems.at[n, k]))
            copies[-1].start()
            return copies[-1]

        first = [load(g, grads.at[pl.ds(n * rows, rows)], 0, n) for n, g in enumerate((g_own, g_x, g_y, g_xy))]
        parts = (stay, from_x, from_y, from_xy)
        blocks, lefts = [], []
        for t in range(steps):
            at = pl.ds(t * width, width)
            blocks.append([load(w_back.at[at], b_back.at[at], 1 + t, QUAD)])
            for n, source in enumerate(parts):
                here = pl.ds(sub + QUAD * count + t * width, width)
                blocks[t].append(load(source.at[here], slopes.at[at, pl.ds(n * rows, rows)], 1 + t, n))
        for n, source in enumerate(parts):
            to = pl.ds(n * rows, rows)
            lefts.append(load(source.at[pl.ds(0, sub)], acts.at[:, to], 1 + steps, n))
            lefts.append(load(source.at[pl.ds(sub, QUAD * count)], mids.at[:, to], 2 + steps, n))
        for copy in first:
            copy.wait()
        for t in range(steps):
            at = slice(t * width, (t + 1) * width)
            for copy in blocks[t]:
                copy.wait()
            hidden[at, :] = (nt(b_back[at, :], grads[...]) * slopes[at, :].astype(F32)).astype(BF16)
        for copy in lefts:
            copy.wait()
        layer = info[1] >> 2

        def put(z, rows_at, value):
            place = layer ^ z
            place = ((place & 1) << 1) | (place >> 1)

            @pl.when(place < 2)
            def _():
                stay_o[place, rows_at, :] = value

            @pl.when(place >= 2)
            def _():
                go_o[place - 2, rows_at, :] = value

        product = nn(acts[...], grads[...]).astype(BF16)
        for z in range(QUAD):
            put(z, slice(0, piece), product[z * piece : (z + 1) * piece, :])
        for t in range(steps):
            product = nt(mids[...], hidden[t * width : (t + 1) * width, :]).astype(BF16)
            for z in range(QUAD):
                put(z, slice(piece + t * count, piece + (t + 1) * count), product[z * count : (z + 1) * count, :])


def feed_grad(info, mid, hidden, act, out_grad):
    depth, width = mid.shape
    steps = hidden.shape[1] // width
    piece = width // PIECES
    return run(
        feed_grad_body,
        info,
        [(v, ANY) for v in (mid, hidden, act, out_grad)],
        [(shape((2, QUAD, QUAD, steps * piece, width), BF16), ANY)],
        (1,),
        [
            pltpu.VMEM((depth, width), BF16),
            pltpu.VMEM((depth, width), BF16),
            pltpu.VMEM((steps, depth, width), BF16),
            pltpu.VMEM((steps, depth, width), BF16),
            pltpu.VMEM((2, QUAD, QUAD, piece, width), BF16),
            pltpu.VMEM((2, QUAD, steps * piece, width), BF16),
            pltpu.SemaphoreType.DMA((2 + 2 * steps,)),
            pltpu.SemaphoreType.DMA((2, 2)),
        ],
        flops=4 * depth * steps * width * width,
        moved=4 * (depth + depth * steps + steps * width) * width,
    )[0]


def side_grad(info, routed, dense):
    _, depth, width = dense[0].shape
    half = PIECES // 2
    piece = width // PIECES

    dims = (half, 4 * piece, width)
    return run(
        side_grad_body,
        info,
        [(v, whole(v.shape)) for v in routed] + [(v, ANY) for v in dense],
        [(shape(dims, BF16), whole(dims))] * 2,
        (1,),
        [
            pltpu.VMEM((2, depth, width), BF16),
            pltpu.VMEM((2, 3, depth, width), BF16),
            pltpu.VMEM((2, depth, width), BF16),
            pltpu.VMEM((2, depth, width), BF16),
            pltpu.VMEM((width, width), BF16),
            pltpu.SemaphoreType.DMA((12,)),
        ],
        flops=16 * depth * width * width,
        moved=24 * depth * width,
    )


def quad_grad(info, parts, grads, w_back):
    hidden, width = w_back.shape
    rows = grads[0].shape[0]
    sub = hidden // QUAD
    made = (shape((2, 2 * sub // QUAD, width), BF16), whole((2, 2 * sub // QUAD, width)))
    total = QUAD * rows
    return run(
        quad_grad_body,
        info,
        [(v, ANY) for v in parts + grads + [w_back]],
        [made, made],
        (1,),
        [
            pltpu.VMEM((hidden, width), BF16),
            pltpu.VMEM((sub, total), BF16),
            pltpu.VMEM((hidden, total), BF16),
            pltpu.VMEM((parts[0].shape[0] - sub - hidden, total), BF16),
            pltpu.VMEM((total, width), BF16),
            pltpu.VMEM((hidden, total), BF16),
            pltpu.SemaphoreType.DMA((3 + hidden // width, 1 + QUAD)),
        ],
        flops=8 * sub * total * width,
        moved=10 * sub * total,
    )


def to_section(value, source):
    return lax.ppermute(value, "section", [(source, 1 - source)])


def swap_section(value):
    return lax.ppermute(value, "section", [(0, 1), (1, 0)])


def after(value, *earlier):
    return lax.optimization_barrier((value, *earlier))[0]


def added_up(parts):
    total = parts[0].astype(F32)
    for part in parts[1:]:
        total = total + part.astype(F32)
    return total


def cross(orders, value, stage):
    count = lax.axis_size("dp")
    low = count // PIECES
    pairs = []
    for section, order in enumerate(orders):
        base = section * count
        flip = low << order[stage]
        pairs += [(base + n, base + (n ^ flip)) for n in range(count)]
    return lax.ppermute(value, ("section", "dp"), pairs)


def cross_first(value, *axes):
    count = lax.axis_size("dp")
    flip = sum((count // PIECES) << axis for axis in axes)
    return lax.ppermute(value, ("section", "dp"), [(n, n ^ flip) for n in range(count)])


def scatter_layers(value):
    stride = QUAD * (lax.axis_size("dp") // PIECES)
    groups = [[base + n * stride for n in range(QUAD)] for base in range(stride)]
    return lax.psum_scatter(value, "dp", scatter_dimension=0, axis_index_groups=groups, tiled=True)


class Exchange:
    def __init__(self, stay, go, swap, stages):
        self.stay, self.go, self.swap = stay, go, swap
        self.stages, self.stage, self.flying = stages, 0, None

    def start(self, info):
        if self.stage:
            half = self.stay[0].shape[0] // 2
            self.go = [part[half:] for part in self.stay]
            self.stay = [part[:half] for part in self.stay]
        send = added_up(self.go).astype(BF16) if len(self.go) > 1 else self.go[0]
        info, send = lax.optimization_barrier((info, send))
        self.flying = self.swap(send, self.stage)
        self.stage += 1
        return info

    def total(self):
        assert self.stage == self.stages
        return added_up(self.stay)[0]


def settle(info, *values):
    arrays = [value.flying if isinstance(value, Exchange) else value for value in values]
    info, *arrays = lax.optimization_barrier((info, *arrays))
    plain = []
    for value, array in zip(values, arrays):
        if isinstance(value, Exchange):
            value.stay = value.stay + [array]
        else:
            plain.append(array)
    return (info, *plain)


def share_out(piece):
    count = lax.axis_size("dp")
    low = count // PIECES
    if low > 1:
        rows, cols = piece.shape
        place = lax.axis_index("dp") % low
        parts = jnp.take(piece.reshape(low, rows // low, cols), jnp.arange(low) ^ place, axis=0)
        while parts.shape[0] > 1:
            half = parts.shape[0] // 2
            far = lax.ppermute(parts[half:], "dp", [(n, n ^ half) for n in range(count)])
            parts = parts[:half] + far
        piece = parts[0]
    return piece[None]


def across(value, flip):
    return lax.ppermute(value, "dp", [(n, n ^ flip) for n in range(lax.axis_size("dp"))])


X, Y, Z, ZZ = 0, 1, 2, 3
ORDERS = ((X, Y, Z, ZZ), (Y, X, Z, ZZ))
SIDE = 2


def shards(inputs, out_grad, picks, valid, router, gain_attn, w_qkv, w_out, gain_mlp, w_in, w_back):
    w_qkv, w_out, w_in, w_back = w_qkv[0], w_out[0], w_in[0], w_back[0]
    seqs, cap = picks.shape
    seq_len = inputs.shape[0] // seqs
    width = inputs.shape[1]
    hidden = w_in.shape[1]
    rows = seqs * cap
    tiles = seq_len // TILE
    section = lax.axis_index("section")
    spot = lax.axis_index("dp") // (lax.axis_size("dp") // PIECES)
    first = section == 0

    table = [(mine, 0) + ORDERS[mine] for mine in (0, 1)]
    facts = jnp.where(first, jnp.array(table[0]), jnp.array(table[1]))
    info = jnp.where(jnp.arange(len(table[0])) == 1, spot, facts).astype(jnp.int32)
    router = router[None]

    far_qkv = to_section(w_qkv, 1)
    far_out = to_section(w_out, 1)
    far_in = to_section(w_in, 1)

    weight_bufs = [pltpu.VMEM(w.shape, BF16) for w in (w_qkv, w_out, w_in, w_back)]
    weight_bufs.append(pltpu.SemaphoreType.DMA((4,)))
    weight_ins = [(w_qkv, ANY), (w_out, ANY), (w_in, ANY), (w_back, ANY)]

    def full(array):
        return (array, whole(array.shape))

    def made(dims, dtype):
        return (shape(dims, dtype), whole(dims))

    routed_flops = 2 * rows * (4 * width * width + 2 * width * hidden)
    weight_bytes = 2 * (4 * width * width + 2 * width * hidden)
    sub = hidden // QUAD
    (
        chosen, normed0, packed0, mixed0, rows0, slope0, branch0, gate0, open0, near, away,
        stay0, over_x, over_y, over_xy,
    ) = run(
        routed_forward_body,
        info,
        [full(v) for v in (inputs, picks, valid, gain_attn, gain_mlp, router)] + weight_ins,
        [
            made((rows, width), BF16),
            made((rows, width), BF16),
            made((rows, 3 * width), BF16),
            made((rows, width), BF16),
            made((rows, width), F32),
            made((rows, hidden), BF16),
            made((rows, width), F32),
            made((rows, LANES), F32),
            made((rows, LANES), F32),
            made((cap, width), BF16),
            made((cap + EXTRA, width), BF16),
        ]
        + [(shape((sub + width // QUAD + hidden, rows), BF16), ANY)] * QUAD,
        (1,),
        weight_bufs[:4]
        + [pltpu.VMEM((rows, hidden), BF16), pltpu.VMEM((QUAD, sub + width // QUAD + hidden, rows), BF16)]
        + weight_bufs[4:]
        + [pltpu.SemaphoreType.DMA((QUAD,))],
        flops=routed_flops,
        moved=weight_bytes,
    )
    info, far_qkv, far_out, far_in, near, away, over_x, over_y, over_xy, w_back_now = settle(
        info, far_qkv, far_out, far_in, near, away, over_x, over_y, over_xy, w_back
    )
    away = swap_section(away)

    def row_tile(dims):
        return pl.BlockSpec(dims, lambda i, info_ref: (i, 0))

    def seq_tile():
        return pl.BlockSpec((TILE, width), lambda i, info_ref: (info_ref[0] * tiles + i, 0))

    def tiled(cols, dtype):
        return (shape((seq_len, cols), dtype), row_tile((TILE, cols)))

    three_tile = pl.BlockSpec((3, TILE, width), lambda i, info_ref: (0, i, 0))
    three = shape((3, seq_len, width), BF16)

    middle, normed1, packed1, middle_sel = run(
        dense_in_body,
        info,
        [
            (inputs, seq_tile()),
            full(near),
            full(away),
            full(picks),
            full(gain_attn),
            (w_qkv, ANY),
            (far_qkv, ANY),
        ],
        [tiled(width, F32), tiled(width, BF16), (three, three_tile), made((cap, width), F32)],
        (tiles,),
        [pltpu.VMEM(w_qkv.shape, BF16), pltpu.SemaphoreType.DMA],
        flops=6 * seq_len * width * width,
        moved=seq_len * width * 12 + 6 * width * width,
    )

    info, packed1, over_x, over_y, over_xy, w_back_now = settle(
        info, packed1, over_x, over_y, over_xy, w_back_now
    )
    far_back = to_section(w_back_now, 1)
    from_x = cross_first(over_x, X)
    from_y = cross_first(over_y, Y)
    from_xy = cross_first(over_xy, X, Y)

    pair_spec = pl.BlockSpec((3, seq_len, LANES), lambda h, info_ref: (0, 0, h))
    column_spec = pl.BlockSpec((seq_len, LANES), lambda h, info_ref: (0, h))
    logsum_spec = pl.BlockSpec((1, 8, seq_len), lambda h, info_ref: (h, 0, 0))
    attend_flops = 2 * HEADS * seq_len * seq_len * TILE
    mixed1, logsum1 = run(
        attend_forward_body,
        info,
        [(packed1, pair_spec)],
        [
            (shape((seq_len, width), BF16), column_spec),
            (shape((PAIRS, 8, seq_len), F32), logsum_spec),
        ],
        (PAIRS,),
        flops=attend_flops,
        moved=8 * seq_len * width,
    )

    info, mixed1, far_back = settle(info, mixed1, far_back)
    pack1, act1, hidden1, mid1, carry, grad_mixed1, gain_mlp_sum, carried = run(
        feed_body,
        info,
        [
            (mixed1, row_tile((TILE, width))),
            (normed1, row_tile((TILE, width))),
            (middle, row_tile((TILE, width))),
            (out_grad, seq_tile()),
            full(gain_mlp),
            full(away),
            full(picks),
            full(middle_sel),
            (w_out, ANY),
            (far_out, ANY),
            (w_in, ANY),
            (far_in, ANY),
            (w_back, ANY),
            (far_back, ANY),
        ],
        [
            (shape((4, seq_len, width), BF16), pl.BlockSpec((4, TILE, width), lambda i, info_ref: (0, i, 0))),
            tiled(hidden, BF16),
            tiled(hidden, BF16),
            tiled(width, BF16),
            tiled(width, F32),
            tiled(width, BF16),
            made((8, width), F32),
            made((2, cap, width), F32),
        ],
        (tiles,),
        [
            pltpu.VMEM(w_out.shape, BF16),
            pltpu.VMEM(w_in.shape, BF16),
            pltpu.VMEM(w_back.shape, BF16),
            pltpu.SemaphoreType.DMA((3,)),
        ],
        flops=2 * seq_len * width * (2 * width + 4 * hidden),
        moved=seq_len * (20 * width + 4 * hidden) + 2 * width * (width + 2 * hidden),
    )
    info, mid1, pack1, carried, from_x, from_y, from_xy = settle(info, mid1, pack1, carried, from_x, from_y, from_xy)
    far_pack = to_section(pack1, 0)
    far_carried = to_section(carried, 1)
    feed = feed_grad(info, mid1, hidden1, act1, out_grad)
    info, feed, far_pack, far_carried = settle(info, feed, far_pack, far_carried)
    feed = lax.psum_scatter(feed.reshape(-1, width), "section", scatter_dimension=0, tiled=True)

    def attend_backward(info, start, held):
        def third(rows):
            return pl.BlockSpec((3, rows, LANES), lambda h, info_ref: (0, 0, start + h))

        column = pl.BlockSpec((seq_len, LANES), lambda h, info_ref: (0, start + h))
        logsums = pl.BlockSpec((1, 8, seq_len), lambda h, info_ref: (start + h, 0, 0))
        return run(
            attend_backward_body,
            info,
            [(packed1, third(seq_len)), (grad_mixed1, column), (mixed1, column), (logsum1, logsums), full(picks)]
            + [(v, ANY) for v in held],
            [(three, third(seq_len)), (shape((3, cap, width), BF16), third(cap))],
            (PAIRS // 2,),
            [pltpu.VMEM((seq_len, LANES), F32)],
            flops=5 * attend_flops // 4,
            moved=8 * seq_len * width,
            aliases={6: 0, 7: 1} if held else {},
        )

    held = attend_backward(info, 0, [])
    info, feed, *held = settle(info, feed, *held)
    feed = scatter_layers(feed)
    packed_grad1, packed_sel = attend_backward(info, PAIRS // 2, held)
    info, packed_grad1, packed_sel = settle(info, packed_grad1, packed_sel)
    far_packed_sel = to_section(packed_sel, 1)
    info, far_packed_sel, packed_grad1 = settle(info, far_packed_sel, packed_grad1)
    far_packed = to_section(packed_grad1, 0)

    g_own, attn0, packed_grad0, grad_chosen, small0 = run(
        routed_backward_body,
        info,
        [
            full(v)
            for v in (
                packed_sel, far_packed_sel, carried, far_carried,
                chosen, packed0, rows0, slope0, branch0, gate0, valid, gain_attn, gain_mlp, router, away,
            )
        ]
        + [(far_qkv, ANY)]
        + weight_ins,
        [
            made((rows, width), BF16),
            made((rows, width), BF16),
            made((3, rows, width), BF16),
            made((rows, width), F32),
            made((8, width), F32),
        ],
        (1,),
        weight_bufs[:4] + [pltpu.VMEM((rows, hidden), BF16), pltpu.SemaphoreType.DMA((5,))],
        flops=routed_flops,
        moved=weight_bytes,
    )
    info, small0, packed_grad0, far_packed, g_own = settle(info, small0, packed_grad0, far_packed, g_own)
    g_x = cross_first(g_own, X)
    g_y = cross_first(g_own, Y)
    g_xy = cross_first(g_own, X, Y)

    side_stay, side_go = side_grad(
        info,
        [normed0, packed_grad0, mixed0, attn0],
        [packed_grad1, far_packed, pack1, far_pack],
    )
    info, side_go, g_x, g_y, g_xy = settle(info, side_go, g_x, g_y, g_xy)
    side = Exchange([side_stay], [side_go], functools.partial(cross, ORDERS), STAGES)
    info = side.start(info)

    grad_middle, gain_attn_sum = run(
        dense_out_body,
        info,
        [
            (packed_grad1, three_tile),
            (carry, row_tile((TILE, width))),
            (middle, row_tile((TILE, width))),
            full(gain_attn),
            full(away),
            (w_qkv, ANY),
            (far_qkv, ANY),
        ],
        [tiled(width, BF16), made((8, width), F32)],
        (tiles,),
        [pltpu.VMEM(w_qkv.shape, BF16), pltpu.SemaphoreType.DMA],
        flops=6 * seq_len * width * width,
        moved=seq_len * width * 16 + 6 * width * width,
    )
    info, grad_middle, gain_attn_sum = settle(info, grad_middle, gain_attn_sum)
    far_grad = to_section(grad_middle, 1)
    small = jnp.where(first, small0, 0.0) + gain_mlp_sum + gain_attn_sum
    small_far = swap_section(small)
    quad_go, quad_stay = quad_grad(
        info, [stay0, from_x, from_y, from_xy],
        [g_own, g_x, g_y, g_xy], w_back,
    )
    info, quad_go, far_grad, small_far, feed = settle(info, quad_go, far_grad, small_far, feed, side)
    info = side.start(info)
    small = small + small_far
    small_far = across(small, 1)
    quad = Exchange([quad_stay], [quad_go], lambda value, stage: cross_first(value, (Z, ZZ)[stage]), 2)
    info = quad.start(info)
    far_places = jnp.where(first, jnp.array([0, 2, 1, 3]), jnp.array([0, 1, 2, 3])) ^ (spot & 3)
    feed = jnp.take(feed.reshape(QUAD, -1, width), far_places, axis=0)
    feed = Exchange([feed[:2]], [feed[2:]], functools.partial(cross, ORDERS), 2)
    info = feed.start(info)

    def end_spec(core, seq, paired):
        def at(s, i, info_ref):
            step = jnp.where((info_ref[0] == core) & (s == seq), i, 0)
            return (0, step, 0) if paired else (step, 0)

        return pl.BlockSpec((1, TILE, width) if paired else (TILE, width), at)

    ends = run(
        ends_body,
        info,
        [
            (pack1, end_spec(1, 1, True)),
            (grad_middle, end_spec(0, 0, False)),
            (far_pack, end_spec(1, 0, True)),
            (far_grad, end_spec(0, 1, False)),
            (grad_chosen, pl.BlockSpec((cap, width), lambda s, i, info_ref: (s, 0))),
            (picks, pl.BlockSpec((seqs, cap), lambda s, i, info_ref: (0, 0))),
        ],
        [
            (
                shape((seqs * seq_len, width), BF16),
                pl.BlockSpec((TILE, width), lambda s, i, info_ref: (s * tiles + i, 0)),
            )
        ],
        (seqs, tiles),
        flops=4 * seqs * seq_len * cap * width,
        moved=8 * seqs * seq_len * width,
    )[0]

    info, ends, small_far = settle(info, ends, small_far, side, quad, feed)
    info = side.start(info)
    info = feed.start(info)
    small = small + small_far
    small_far = across(small, 2)
    info = quad.start(info)
    info, small_far = settle(info, small_far, feed)
    small = small + small_far
    small_far = across(small, 4)
    feed1 = feed.total()
    back1 = to_section(feed1.astype(BF16), 0).astype(F32)
    info, = settle(info, side)
    info = side.start(info)
    info, small_far, back1 = settle(info, small_far, back1)
    small = small + small_far
    small_far = across(small, 8)
    info, small_far = settle(info, small_far, quad)

    def gain_share(routed_row, dense_row):
        row = jnp.where(first, small[routed_row], small[dense_row])
        return lax.dynamic_slice_in_dim(row, lax.axis_index("dp") * share, share)[None]

    piece = width // PIECES
    small = small + small_far
    for step in range(PIECES, lax.axis_size("dp"), PIECES):
        small = small + across(small, step)
    share = width // lax.axis_size("dp")
    quad_sum = quad.total()
    back0, in0 = quad_sum[: hidden // PIECES], quad_sum[hidden // PIECES :]
    in0 = in0.reshape(QUAD, piece, width).transpose(1, 0, 2).reshape(piece, hidden)

    in1 = feed1.reshape(QUAD, piece, width).transpose(1, 0, 2).reshape(piece, hidden)
    settle(info, side)
    attend_sum = side.total()
    return (
        ends[None],
        small[0],
        gain_share(2, 4),
        share_out(jnp.concatenate([attend_sum[n : n + piece] for n in range(0, 3 * piece, piece)], axis=1)),
        share_out(attend_sum[3 * piece :]),
        gain_share(1, 3),
        share_out(jnp.where(first, in0, in1)),
        share_out(jnp.where(first, back0, back1)),
    )


def solution(mesh):
    placed = (
        P("dp", None),
        P("dp", None),
        P("dp", None),
        P("dp", None),
        P(),
        P("section", None),
        P("section", None, None),
        P("section", None, None),
        P("section", None),
        P("section", None, None),
        P("section", None, None),
    )
    return jax.shard_map(
        shards,
        mesh=mesh,
        in_specs=placed,
        out_specs=(
            P("section", "dp", None),
            P(),
            P("section", "dp"),
            P("section", "dp", None),
            P("section", "dp", None),
            P("section", "dp"),
            P("section", "dp", None),
            P("section", "dp", None),
        ),
        check_vma=False,
    )
```

```python
import functools

import jax
import jax.numpy as jnp
from jax import lax
from jax.experimental import pallas as pl
from jax.experimental.pallas import tpu as pltpu
from jax.sharding import PartitionSpec as P

HEADS = 12
HEAD_DIM = 64
LANES = 128
PAIRS = HEADS * HEAD_DIM // LANES
EPS = 1e-06
FACTOR = HEAD_DIM ** (-0.5)
PIECES = 16
STAGES = 4
QUAD = 4
EXTRA = 16
TILE = 256
WIDE = 512
VMEM_BYTES = 56 * 1024 * 1024
BF16 = jnp.bfloat16
F32 = jnp.float32


def nn(a, b):
    return lax.dot_general(a, b, (((1,), (0,)), ((), ())), preferred_element_type=F32)


def nt(a, b):
    return lax.dot_general(a, b, (((1,), (1,)), ((), ())), preferred_element_type=F32)


def tn(a, b):
    return lax.dot_general(a, b, (((0,), (0,)), ((), ())), preferred_element_type=F32)


def shape(dims, dtype):
    return jax.ShapeDtypeStruct(dims, dtype)


def whole(dims):
    zeros = (0,) * len(dims)
    return pl.BlockSpec(dims, lambda *_: zeros)


ANY = pl.BlockSpec(memory_space=pl.ANY)


def run(body, info, ins, outs, grid, scratch=(), flops=0, moved=0, aliases=()):
    arrays, in_specs = zip(*ins)
    shapes, out_specs = zip(*outs)
    return pl.pallas_call(
        body,
        out_shape=shapes,
        input_output_aliases=dict(aliases),
        grid_spec=pltpu.PrefetchScalarGridSpec(
            num_scalar_prefetch=1,
            grid=grid,
            in_specs=in_specs,
            out_specs=out_specs,
            scratch_shapes=scratch,
        ),
        compiler_params=pltpu.CompilerParams(
            vmem_limit_bytes=VMEM_BYTES, dimension_semantics=("arbitrary",) * len(grid)
        ),
        cost_estimate=pl.CostEstimate(flops=flops // 4, bytes_accessed=moved // 4, transcendentals=0),
    )(info, *arrays)


def top_lanes(rows):
    return lax.broadcasted_iota(jnp.int32, (rows, LANES), 1) < HEAD_DIM


def lane_head(rows, which):
    lane = lax.broadcasted_iota(jnp.int32, (rows, LANES), 1)
    return (lane < HEAD_DIM) if which == 0 else (lane >= HEAD_DIM)


def head_only(value, which):
    return jnp.where(lane_head(value.shape[0], which), value, jnp.zeros_like(value))


def mean_square_scale(rows):
    return lax.rsqrt(jnp.mean(rows * rows, axis=-1, keepdims=True) + EPS)


def norm_back(grad, rows, scale, gain):
    hat = rows * scale
    scaled = grad * gain
    back = scale * (scaled - hat * jnp.mean(scaled * hat, axis=-1, keepdims=True))
    return back, jnp.sum(grad * hat, axis=0, keepdims=True)


def gelu_parts(pre):
    root = 0.7978845608028654
    square = pre * pre
    bent = jnp.tanh(root * pre * (1.0 + 0.044715 * square))
    half = 0.5 * (1.0 + bent)
    slope = half + 0.5 * pre * (1.0 - bent * bent) * (root * (1.0 + 0.134145 * square))
    return pre * half, slope


def fetch(info, local, remote, buf, sem):
    @pl.when(info[0] == 1)
    def _():
        pltpu.make_async_copy(local, buf, sem).start()

    @pl.when(info[0] == 0)
    def _():
        pltpu.make_async_copy(remote, buf, sem).start()


def arrived(source, buf, sem):
    pltpu.make_async_copy(source, buf, sem).wait()


def stacked(value):
    return jnp.concatenate([head_only(value, h) for h in range(2)], axis=0)


def unstacked(value):
    half = value.shape[0] // 2
    return jnp.where(top_lanes(half), value[:half], value[half:])


def slot_pieces(packed, seq, pair, cap):
    rows = slice(seq * cap, (seq + 1) * cap)
    width = HEADS * HEAD_DIM
    first = pair * LANES
    queries = stacked(packed[rows, first : first + LANES] * BF16(FACTOR))
    keys = packed[rows, width + first : width + first + LANES]
    values = packed[rows, 2 * width + first : 2 * width + first + LANES]
    return queries, keys, values


def slot_rule(valid_row, cap):
    query = lax.broadcasted_iota(jnp.int32, (cap, cap), 0)
    key = lax.broadcasted_iota(jnp.int32, (cap, cap), 1)
    rule = (key <= query) & ((valid_row > 0) | (key == query))
    return jnp.concatenate([rule, rule], axis=0)


def column_of(row):
    return jnp.transpose(jnp.broadcast_to(row, (row.shape[1], row.shape[1])))


def slot_mask(valid):
    seqs = valid.shape[0]
    return jnp.concatenate([column_of(valid[s : s + 1, :].astype(F32)) for s in range(seqs)], axis=0)[:, 0:1]


def weight_copies(sources, bufs, sems):
    return [pltpu.make_async_copy(a, b, sems.at[n]) for n, (a, b) in enumerate(zip(sources, bufs))]


def routed_forward_body(
    info, x, picks, valid, gain_attn, gain_mlp, router, w_qkv, w_out, w_in, w_back,
    gate_o, open_o, near_o, away_o, chosen_h, normed_h, packed_h, mixed_h, rows_h, slope_h, branch_h,
    stay_o, over_x_o, over_y_o, over_xy_o,
    chosen_o, normed_o, packed_o, mixed_o, rows_o, slope_o, branch_o,
    b_x, b_qkv, b_out, b_in, b_back, act_b, shares, slope_t, sems, x_sems, out_sems,
):
    @pl.when(info[0] == 1)
    def _():
        rest = jnp.concatenate([gain_attn[...], gain_mlp[...]], axis=0)
        count = away_o.shape[0] - EXTRA
        for part in range(3):
            rounded = rest.astype(BF16)
            away_o[count + 2 * part : count + 2 * part + 2, :] = rounded
            rest = rest - rounded.astype(F32)

    @pl.when(info[0] == 0)
    def _():
        copies = weight_copies((w_qkv, w_out, w_in, w_back), (b_qkv, b_out, b_in, b_back), sems)
        seqs, cap = valid.shape
        seq_len = x.shape[0] // seqs
        loads = []
        for seq in range(seqs):
            at = pl.ds(seq * seq_len, seq_len)
            loads.append(pltpu.make_async_copy(x.at[at], b_x.at[at], x_sems.at[seq]))
        for copy in loads + copies:
            copy.start()
        sends = []

        def send(source, target):
            sends.append(pltpu.make_async_copy(source, target, out_sems.at[len(sends)]))
            sends[-1].start()

        parts = []
        for seq in range(seqs):
            place = lax.broadcasted_iota(jnp.int32, (seq_len, cap), 0)
            hot = (picks[seq : seq + 1, :] == place).astype(BF16)
            loads[seq].wait()
            parts.append(tn(hot, b_x[seq * seq_len : (seq + 1) * seq_len, :]))
        chosen = jnp.concatenate(parts, axis=0)
        chosen_o[...] = chosen.astype(BF16)
        send(chosen_o, chosen_h)
        gates = jax.nn.sigmoid(jnp.sum(chosen * router[...].reshape(1, -1), axis=-1, keepdims=True))
        gate_o[...] = jnp.broadcast_to(gates, gate_o.shape)
        normed = (chosen * mean_square_scale(chosen) * gain_attn[...]).astype(BF16)
        normed_o[...] = normed
        send(normed_o, normed_h)
        copies[0].wait()
        packed_o[...] = nn(normed, b_qkv[...]).astype(BF16)
        send(packed_o, packed_h)
        work = [(seq, pair) for seq in range(seqs) for pair in range(PAIRS)]
        allowed = [slot_rule(valid[seq : seq + 1, :], cap) for seq in range(seqs)]
        pieces = [slot_pieces(packed_o, seq, pair, cap) for seq, pair in work]
        scores = [jnp.where(allowed[w[0]], nt(p[0], p[1]), -1e30) for w, p in zip(work, pieces)]
        grown = [jnp.exp(v - jnp.max(v, axis=-1, keepdims=True)).astype(BF16) for v in scores]
        ones = jnp.ones((cap, LANES), BF16)
        outs = [nn(g, jnp.concatenate([p[2], ones], axis=1)) for g, p in zip(grown, pieces)]
        outs = [unstacked(o[:, :LANES] / o[:, LANES:]).astype(BF16) for o in outs]
        mixed = jnp.concatenate(
            [jnp.concatenate(outs[s * PAIRS : (s + 1) * PAIRS], axis=1) for s in range(seqs)], axis=0
        )
        mixed_o[...] = mixed
        send(mixed_o, mixed_h)
        copies[1].wait()
        attn_out = nn(mixed, b_out[...])
        rows = chosen + attn_out
        rows_o[...] = rows
        send(rows_o, rows_h)
        normed_mid = (rows * mean_square_scale(rows) * gain_mlp[...]).astype(BF16)
        member = info[1] & 3
        piece = b_in.shape[1] // PIECES
        mid_turned = jnp.transpose(normed_mid)
        count = mid_turned.shape[0] // PIECES
        sub = piece * QUAD
        for dest in range(PIECES):
            at = sub + dest // QUAD * count
            shares[(dest % QUAD) ^ member, at : at + count, :] = mid_turned[dest * count : (dest + 1) * count, :]
        copies[2].wait()
        step = 768
        for first in range(0, b_in.shape[1], step):
            cols = slice(first, first + step)
            act, slope = gelu_parts(nn(normed_mid, b_in[:, cols]))
            act = act.astype(BF16)
            slope = slope.astype(BF16)
            act_b[:, cols] = act
            slope_o[:, cols] = slope
            chunk = first // step
            slope_t[first : first + step, :] = jnp.transpose(slope)
            turned = jnp.transpose(act)
            for owner in range(QUAD):
                shares[owner ^ member, chunk * piece : (chunk + 1) * piece, :] = turned[
                    owner * piece : (owner + 1) * piece, :
                ]
        send(slope_o, slope_h)
        for n, out in enumerate((stay_o, over_x_o, over_y_o, over_xy_o)):
            send(shares.at[n], out.at[pl.ds(0, shares.shape[1])])
            send(slope_t, out.at[pl.ds(shares.shape[1], slope_t.shape[0])])
        copies[3].wait()
        branch = attn_out + nn(act_b[...], b_back[...])
        branch_o[...] = branch
        send(branch_o, branch_h)
        opened = gates * slot_mask(valid)
        open_o[...] = jnp.broadcast_to(opened, open_o.shape)
        delta = (opened * branch).astype(BF16)
        near_o[...] = delta[:cap]
        away_o[:cap, :] = delta[cap:]
        for copy in sends:
            copy.wait()


def routed_backward_body(
    info, p_near, p_far, r_near, r_far, chosen_i, branch, gate, valid, gain_attn, gain_mlp, router, swapped,
    packed_h, rows_h, slope_h, w_next, w_qkv, w_out, w_in, w_back,
    chosen_o, small_o, ffn_h, attn_h, packed_out,
    b_qkv, b_out, b_in, b_back, hidden_b, packed, rows_i, slope, ffn_o, attn_o, packed_o, sems, in_sems, out_sems,
):
    @pl.when(info[0] == 0)
    def _():
        copies = weight_copies((w_qkv, w_out, w_in, w_back), (b_qkv, b_out, b_in, b_back), sems)
        upper = pltpu.make_async_copy(w_next, b_qkv, sems.at[4])
        upper.start()
        loads = [
            pltpu.make_async_copy(source, target, in_sems.at[n])
            for n, (source, target) in enumerate(((slope_h, slope), (rows_h, rows_i), (packed_h, packed)))
        ]
        for copy in (copies[3], loads[0], copies[2], loads[1], copies[1], loads[2]):
            copy.start()
        sends = []

        def send(source, target):
            sends.append(pltpu.make_async_copy(source, target, out_sems.at[len(sends)]))
            sends[-1].start()

        seqs, cap = valid.shape
        chosen = chosen_i[...].astype(F32)
        width = chosen.shape[1]
        upper.wait()
        upper_gain = dense_gain(info, gain_attn, swapped, 0)
        grad_sel = []
        for dense, carried in ((p_near, r_near), (p_far, r_far)):
            grad_normed = sum(nt(dense[n], b_qkv[:, n * width : (n + 1) * width]) for n in range(3))
            middle = carried[1]
            back, _ = norm_back(grad_normed, middle, mean_square_scale(middle), upper_gain)
            grad_sel.append((carried[0] + back).astype(BF16).astype(F32))
        grad_sel = jnp.concatenate(grad_sel, axis=0)
        copies[0].start()
        gates = gate[:, 0:1]
        mask = slot_mask(valid)
        logit = jnp.sum(grad_sel * branch[...], axis=-1, keepdims=True) * mask * gates * (1.0 - gates)
        grad = grad_sel * (gates * mask)
        grad_ffn = grad.astype(BF16)
        ffn_o[...] = grad_ffn
        send(ffn_o, ffn_h)
        copies[3].wait()
        loads[0].wait()
        step = 768
        for first in range(0, b_in.shape[1], step):
            cols = slice(first, first + step)
            hidden = (nt(grad_ffn, b_back[cols, :]) * slope[:, cols].astype(F32)).astype(BF16)
            hidden_b[:, cols] = hidden
        copies[2].wait()
        grad_mid = nt(hidden_b[...], b_in[...])
        loads[1].wait()
        rows = rows_i[...]
        grad_rows, gain_mlp_sum = norm_back(grad_mid, rows, mean_square_scale(rows), gain_mlp[...])
        grad_attn = (grad + grad_rows).astype(BF16)
        attn_o[...] = grad_attn
        send(attn_o, attn_h)
        copies[1].wait()
        grad_mixed = nt(grad_attn, b_out[...]).astype(BF16)
        loads[2].wait()
        work = [(seq, pair) for seq in range(seqs) for pair in range(PAIRS)]
        allowed = [slot_rule(valid[seq : seq + 1, :], cap) for seq in range(seqs)]
        pieces = [slot_pieces(packed, seq, pair, cap) for seq, pair in work]
        grads = [
            stacked(grad_mixed[seq * cap : (seq + 1) * cap, pair * LANES : (pair + 1) * LANES])
            for seq, pair in work
        ]
        scores = [jnp.where(allowed[w[0]], nt(p[0], p[1]), -1e30) for w, p in zip(work, pieces)]
        grad_probs = [nt(g, p[2]) for g, p in zip(grads, pieces)]
        grown = [jnp.exp(v - jnp.max(v, axis=-1, keepdims=True)) for v in scores]
        probs = [v / jnp.sum(v, axis=-1, keepdims=True) for v in grown]
        lows = [
            (p * (g - jnp.sum(p * g, axis=-1, keepdims=True))).astype(BF16) for p, g in zip(probs, grad_probs)
        ]
        for (seq, pair), piece, grad_head, prob, low in zip(work, pieces, grads, probs, lows):
            at = slice(seq * cap, (seq + 1) * cap)
            cols = slice(pair * LANES, (pair + 1) * LANES)
            packed_o[0, at, cols] = (unstacked(nn(low, piece[1])) * FACTOR).astype(BF16)
            packed_o[1, at, cols] = tn(low, piece[0]).astype(BF16)
            packed_o[2, at, cols] = tn(prob.astype(BF16), grad_head).astype(BF16)
        send(packed_o, packed_out)
        copies[0].wait()
        grad_normed = sum(nt(packed_o[n], b_qkv[:, n * width : (n + 1) * width]) for n in range(3))
        back, gain_attn_sum = norm_back(grad_normed, chosen, mean_square_scale(chosen), gain_attn[...])
        chosen_o[...] = grad_rows + back + logit * router[...].reshape(1, -1)
        small_o[...] = jnp.zeros(small_o.shape, F32)
        small_o[0:1, :] = jnp.sum(logit * chosen, axis=0, keepdims=True)
        small_o[1:2, :] = gain_mlp_sum
        small_o[2:3, :] = gain_attn_sum
        for copy in sends:
            copy.wait()


def dense_gain(info, local, swapped, row):
    first = swapped.shape[0] - EXTRA + row
    far = sum(swapped[first + n : first + n + 1, :].astype(F32) for n in (0, 2, 4))
    return jnp.where(info[0] == 1, local[...], far)


def dense_in_body(
    info, x, near, away, picks, gain, w_local, w_far, middle_o, normed_o, packed_o, sel_o, b_qkv, sem
):
    step = pl.program_id(0)

    @pl.when(step == 0)
    def _():
        fetch(info, w_local, w_far, b_qkv, sem)

    rows, width = x.shape
    cap = near.shape[0]
    delta = jnp.where(info[0] == 0, near[...], away[:cap, :])
    place = step * rows + lax.broadcasted_iota(jnp.int32, (rows, cap), 0)
    hot = (picks[pl.ds(info[0], 1), :] == place).astype(BF16)
    middle = x[...].astype(F32) + nn(hot, delta)
    middle_o[...] = middle

    @pl.when(step == 0)
    def _():
        sel_o[...] = delta.astype(F32)

    sel_o[...] += tn(hot, x[...])
    normed = (middle * mean_square_scale(middle) * dense_gain(info, gain, away, 0)).astype(BF16)
    normed_o[...] = normed

    @pl.when(step == 0)
    def _():
        arrived(w_local, b_qkv, sem)

    for n in range(3):
        packed_o[n] = nn(normed, b_qkv[:, n * width : (n + 1) * width]).astype(BF16)


def attend_forward_body(info, packed, mixed_o, logsum_o):
    seq_len = packed.shape[1]
    tile = 2 * TILE
    queries = packed[0] * BF16(FACTOR)
    keys = packed[1]
    ones = jnp.ones((seq_len, LANES), BF16)
    values = [jnp.concatenate([head_only(packed[2], h), ones], axis=1) for h in range(2)]
    below = lax.broadcasted_iota(jnp.int32, (tile, tile), 1) <= lax.broadcasted_iota(jnp.int32, (tile, tile), 0)
    for first in range(0, seq_len, tile):
        upto = first + tile
        at = slice(first, upto)
        scores = []
        for head in range(2):
            score = nt(head_only(queries[at], head), keys[:upto])
            last = jnp.where(below, score[:, first:], -1e30)
            scores.append(jnp.concatenate([score[:, :first], last], axis=1) if first else last)
        tops = [jnp.max(score, axis=-1, keepdims=True) for score in scores]
        grown = [jnp.exp(score - top).astype(BF16) for score, top in zip(scores, tops)]
        outs = [nn(g, value[:upto]) for g, value in zip(grown, values)]
        mixed = sum(out[:, :LANES] * (1.0 / out[:, LANES:]) for out in outs)
        mixed_o[at, :] = mixed.astype(BF16)
        sums = [top + jnp.log(out[:, LANES:]) for top, out in zip(tops, outs)]
        turned = jnp.transpose(jnp.where(top_lanes(tile), sums[0], sums[1]))
        logsum_o[0, 0:1, at] = turned[0:1]
        logsum_o[0, 1:2, at] = turned[HEAD_DIM : HEAD_DIM + 1]


def attend_backward_body(info, packed, grad, mixed, logsum, picks, *refs):
    out, sel_o, grad_q = refs[-3:]
    seq_len = packed.shape[1]
    queries = packed[0] * BF16(FACTOR)
    queries = [head_only(queries, h) for h in range(2)]
    key_heads = [head_only(packed[1], h) for h in range(2)]
    grads = [head_only(grad[...], h) for h in range(2)]
    product = grad[...].astype(F32) * mixed[...].astype(F32)
    pick_row = lax.broadcasted_iota(jnp.int32, (8, LANES), 0)
    pick_lane = lax.broadcasted_iota(jnp.int32, (8, LANES), 1)
    pick = (pick_row == pick_lane // HEAD_DIM).astype(F32)
    inner = lax.dot_general(
        pick, product, (((1,), (1,)), ((), ())), precision=lax.Precision.HIGHEST, preferred_element_type=F32
    )
    above = lax.broadcasted_iota(jnp.int32, (TILE, TILE), 0) <= lax.broadcasted_iota(
        jnp.int32, (TILE, TILE), 1
    )
    for first in range(0, seq_len, TILE):
        kat = slice(first, first + TILE)
        keys = packed[1, kat, :]
        values = packed[2, kat, :]
        dks, dvs, dqs = [], [], []
        for head in range(2):
            query = queries[head][first:]
            grad_head = grads[head][first:]
            probs = jnp.exp(nt(keys, query) - logsum[0, head : head + 1, first:])
            edge = jnp.where(above, probs[:, :TILE], 0.0)
            probs = jnp.concatenate([edge, probs[:, TILE:]], axis=1) if first + TILE < seq_len else edge
            grad_probs = nt(values, grad_head)
            low = (probs * (grad_probs - inner[head : head + 1, first:])).astype(BF16)
            dvs.append(nn(probs.astype(BF16), grad_head))
            dks.append(nn(low, query))
            dqs.append(tn(low, key_heads[head][kat]))
        if first == 0:
            grad_q[...] = dqs[0] + dqs[1]
        else:
            grad_q[first:, :] += dqs[0] + dqs[1]
        out[1, kat, :] = (dks[0] + dks[1]).astype(BF16)
        out[2, kat, :] = (dvs[0] + dvs[1]).astype(BF16)
    out[0] = (grad_q[...] * FACTOR).astype(BF16)
    cap = picks.shape[1]
    place = lax.broadcasted_iota(jnp.int32, (seq_len, cap), 0)
    hot = (picks[pl.ds(info[0], 1), :] == place).astype(BF16)
    for n in range(3):
        sel_o[n] = tn(hot, out[n]).astype(BF16)


def feed_body(
    info, mixed, normed, middle, out_grad, gain_in, swapped, picks, middle_sel, wo_l, wo_f, wi_l, wi_f, wb_l, wb_f,
    pack_o, act_o, hidden_o, mid_o, carry_o, mixed_o, gain_o, sel_o,
    b_out, b_in, b_back, sems,
):
    step = pl.program_id(0)
    width = middle.shape[1]
    starts = range(0, b_in.shape[1], width)

    @pl.when(step == 0)
    def _():
        fetch(info, wo_l, wo_f, b_out, sems.at[0])
        for n, first in enumerate(starts):
            cols = pl.ds(first, width)
            fetch(info, wi_l.at[:, cols], wi_f.at[:, cols], b_in.at[:, cols], sems.at[1 + 2 * n])
            fetch(info, wb_l.at[cols], wb_f.at[cols], b_back.at[cols], sems.at[2 + 2 * n])
        gain_o[...] = jnp.zeros(gain_o.shape, F32)
        sel_o[0] = jnp.zeros(middle_sel.shape, F32)
        sel_o[1] = middle_sel[...]
        arrived(wo_l, b_out, sems.at[0])

    gain = dense_gain(info, gain_in, swapped, 1)
    pack_o[2] = mixed[...]
    pack_o[3] = normed[...]
    rows = middle[...] + nn(mixed[...], b_out[...])
    scale = mean_square_scale(rows)
    normed_mid = (rows * scale * gain).astype(BF16)
    mid_o[...] = normed_mid
    grad_ffn = out_grad[...]

    def hidden_block(first):
        cols = slice(first, first + width)
        act, slope = gelu_parts(nn(mid_o[...], b_in[:, cols]))
        act_o[:, cols] = act.astype(BF16)
        hidden_o[:, cols] = (nt(out_grad[...], b_back[cols, :]) * slope).astype(BF16)

    @pl.when(step == 0)
    def _():
        for n, first in enumerate(starts):
            cols = pl.ds(first, width)
            arrived(wi_l.at[:, cols], b_in.at[:, cols], sems.at[1 + 2 * n])
            arrived(wb_l.at[cols], b_back.at[cols], sems.at[2 + 2 * n])
            hidden_block(first)

    @pl.when(step > 0)
    def _():
        for first in starts:
            hidden_block(first)

    pack_o[0] = (rows + nn(act_o[...], b_back[...])).astype(BF16)
    grad_mid = nt(hidden_o[...], b_in[...])
    back, gain_sum = norm_back(grad_mid, rows, scale, gain)
    carry = grad_ffn.astype(F32) + back
    carry_o[...] = carry
    grad_attn = carry.astype(BF16)
    pack_o[1] = grad_attn
    mixed_o[...] = nt(grad_attn, b_out[...]).astype(BF16)
    gain_o[3:4, :] += gain_sum
    count, cap = carry.shape[0], middle_sel.shape[0]
    place = step * count + lax.broadcasted_iota(jnp.int32, (count, cap), 0)
    hot = (picks[pl.ds(info[0], 1), :] == place).astype(BF16)
    sel_o[0] += tn(hot, grad_attn) + tn(hot, (carry - grad_attn.astype(F32)).astype(BF16))


def dense_out_body(
    info, packed, carry, middle, gain_in, swapped, w_local, w_far, grad_o, gain_o, b_qkv, sem
):
    step = pl.program_id(0)

    @pl.when(step == 0)
    def _():
        fetch(info, w_local, w_far, b_qkv, sem)
        gain_o[...] = jnp.zeros(gain_o.shape, F32)
        arrived(w_local, b_qkv, sem)

    width = middle.shape[1]
    grad_normed = sum(nt(packed[n], b_qkv[:, n * width : (n + 1) * width]) for n in range(3))
    rows = middle[...]
    gain = dense_gain(info, gain_in, swapped, 0)
    back, gain_sum = norm_back(grad_normed, rows, mean_square_scale(rows), gain)
    gain_o[4:5, :] += gain_sum
    grad_o[...] = (carry[...] + back).astype(BF16)


def ends_body(info, result_block, grad, far_block, far_grad, grad_chosen, picks, out):
    seq = pl.program_id(0)
    step = pl.program_id(1)

    @pl.when(info[0] == 1)
    def _():
        out[...] = jnp.where(seq == 1, result_block[0], far_block[0])

    @pl.when(info[0] == 0)
    def _():
        base = jnp.where(seq == 0, grad[...], far_grad[...]).astype(F32)
        rows = out.shape[0]
        cap = grad_chosen.shape[0]
        place = step * rows + lax.broadcasted_iota(jnp.int32, (rows, cap), 0)
        hot = (picks[pl.ds(seq, 1), :] == place).astype(BF16)
        high = grad_chosen[...].astype(BF16)
        low = (grad_chosen[...] - high.astype(F32)).astype(BF16)
        out[...] = (base + (nn(hot, high) + nn(hot, low))).astype(BF16)


def feed_grad_body(
    info, mid, hidden, act, out_grad, out, mid_b, grad_b, hidden_b, act_b, ring_in, ring_back, in_sems, out_sems
):
    steps, rows, width = hidden_b.shape
    piece = width // PIECES

    def load(source, target, n):
        return pltpu.make_async_copy(source, target, in_sems.at[n])

    mine = pl.ds(pl.multiple_of(info[0] * rows, rows), rows)
    loads = [load(mid, mid_b, 0)]
    loads += [load(hidden.at[:, pl.ds(t * width, width)], hidden_b.at[t], 1 + t) for t in range(steps)]
    loads += [load(out_grad.at[mine], grad_b, 1 + steps)]
    loads += [load(act.at[:, pl.ds(t * width, width)], act_b.at[t], 2 + steps + t) for t in range(steps)]
    for copy in loads:
        copy.start()
    sent = []
    for n in range(2 * steps):
        t = n % steps
        if t == 0:
            loads[0 if n == 0 else 1 + steps].wait()
        loads[1 + t if n < steps else 2 + steps + t].wait()
        product = tn(mid_b[...], hidden_b[t]) if n < steps else tn(act_b[t], grad_b[...])
        ring = ring_in if n < steps else ring_back
        if t >= 2:
            sent[n - 2].wait()
        ring[n % 2] = product.astype(BF16).reshape(ring.shape[1:])
        target = out.at[1, :, :, pl.ds(t * piece, piece)] if n < steps else out.at[0, t]
        sent.append(pltpu.make_async_copy(ring.at[n % 2], target, out_sems.at[n // steps, n % 2]))
        sent[-1].start()
    for n in (steps - 2, steps - 1, 2 * steps - 2, 2 * steps - 1):
        sent[n].wait()


def origin(info, base, place):
    relative = 0
    for stage in range(STAGES):
        if place >> (STAGES - 1 - stage) & 1:
            relative = relative | (1 << info[base + stage])
    return info[1] ^ relative


def put_block(info, outs, product, slot, spot, ring, sems):
    piece = product.shape[0] // PIECES
    ring[spot] = product.astype(BF16)
    half = PIECES // 2
    sent = []
    for place in range(PIECES):
        rows = pl.ds(pl.multiple_of(origin(info, SIDE, place) * piece, piece), piece)
        target = outs[place // half].at[place % half, pl.ds(slot * piece, piece)]
        sent.append(pltpu.make_async_copy(ring.at[spot, rows], target, sems.at[slot, place]))
        sent[-1].start()
    return sent


def side_grad_body(
    info, normed0, packed0, mixed0, attn0,
    p_near, p_far, near, far,
    out_stay, out_go,
    n_buf, p_buf, m_buf, a_buf, ring, sems, out_sems,
):
    outs = (out_stay, out_go)

    def put_all(order, product):
        sent = []
        for n, slot in enumerate(order):
            value = product(slot)
            if n >= 2:
                for copy in sent[n - 2]:
                    copy.wait()
            sent.append(put_block(info, outs, value, slot, n % 2, ring, out_sems))
        for copies in sent[-2:]:
            for copy in copies:
                copy.wait()

    @pl.when(info[0] == 0)
    def _():
        put_all((3, 0, 1, 2), lambda n: tn(normed0[...], packed0[n]) if n < 3 else tn(mixed0[...], attn0[...]))

    @pl.when(info[0] == 1)
    def _():
        sources = [
            (source.at[which], target, n)
            for which, target in ((2, m_buf), (1, a_buf), (3, n_buf))
            for n, source in enumerate((near, far))
        ]
        copies = [
            pltpu.make_async_copy(source, target.at[n], sems.at[k])
            for k, (source, target, n) in enumerate(sources)
        ]
        blocks = [
            pltpu.make_async_copy(source.at[which], p_buf.at[n, which], sems.at[6 + 2 * which + n])
            for which in range(3)
            for n, source in enumerate((p_near, p_far))
        ]
        for copy in copies + blocks:
            copy.start()

        def product(n):
            if n == 3:
                for copy in copies[:4]:
                    copy.wait()
                return tn(m_buf[0], a_buf[0]) + tn(m_buf[1], a_buf[1])
            for copy in (copies[4:] if n == 0 else []) + blocks[2 * n : 2 * n + 2]:
                copy.wait()
            return tn(n_buf[0], p_buf[0, n]) + tn(n_buf[1], p_buf[1, n])

        put_all((3, 0, 1, 2), product)


def quad_grad_body(
    info, stay, from_x, from_y, from_xy, g_own, g_x, g_y, g_xy, w_back, go_o, stay_o,
    b_back, acts, slopes, mids, grads, hidden, held, sems, out_sems,
):
    @pl.when(info[0] == 0)
    def _():
        rows = g_own.shape[0]
        width = grads.shape[1]
        sub = acts.shape[0]
        steps = b_back.shape[0] // width
        piece = sub // QUAD
        count = mids.shape[0] // QUAD
        copies = []

        def load(source, target, n, k):
            copies.append(pltpu.make_async_copy(source, target, sems.at[n, k]))
            copies[-1].start()
            return copies[-1]

        first = [load(g, grads.at[pl.ds(n * rows, rows)], 0, n) for n, g in enumerate((g_own, g_x, g_y, g_xy))]
        parts = (stay, from_x, from_y, from_xy)
        blocks, lefts = [], []
        for t in range(steps):
            at = pl.ds(t * width, width)
            blocks.append([load(w_back.at[at], b_back.at[at], 1 + t, QUAD)])
            for n, source in enumerate(parts):
                here = pl.ds(sub + QUAD * count + t * width, width)
                blocks[t].append(load(source.at[here], slopes.at[at, pl.ds(n * rows, rows)], 1 + t, n))
        for n, source in enumerate(parts):
            to = pl.ds(n * rows, rows)
            lefts.append(load(source.at[pl.ds(0, sub)], acts.at[:, to], 1 + steps, n))
            lefts.append(load(source.at[pl.ds(sub, QUAD * count)], mids.at[:, to], 2 + steps, n))
        for copy in first:
            copy.wait()
        for t in range(steps):
            at = slice(t * width, (t + 1) * width)
            for copy in blocks[t]:
                copy.wait()
            hidden[at, :] = (nt(b_back[at, :], grads[...]) * slopes[at, :].astype(F32)).astype(BF16)
        for copy in lefts:
            copy.wait()
        layer = info[1] >> 2

        def put(z, rows_at, value):
            place = layer ^ z
            place = ((place & 1) << 1) | (place >> 1)

            held[place, rows_at, :] = value

        product = nn(acts[...], grads[...]).astype(BF16)
        for z in range(QUAD):
            put(z, slice(0, piece), product[z * piece : (z + 1) * piece, :])
        for t in range(steps):
            product = nt(mids[...], hidden[t * width : (t + 1) * width, :]).astype(BF16)
            for z in range(QUAD):
                put(z, slice(piece + t * count, piece + (t + 1) * count), product[z * count : (z + 1) * count, :])
        outs = [
            pltpu.make_async_copy(held.at[pl.ds(first, 2)], out, out_sems.at[n])
            for n, (first, out) in enumerate(((2, go_o), (0, stay_o)))
        ]
        for copy in outs:
            copy.start()
        for copy in outs:
            copy.wait()


def feed_grad(info, mid, hidden, act, out_grad):
    depth, width = mid.shape
    steps = hidden.shape[1] // width
    piece = width // PIECES
    return run(
        feed_grad_body,
        info,
        [(v, ANY) for v in (mid, hidden, act, out_grad)],
        [(shape((2, QUAD, QUAD, steps * piece, width), BF16), ANY)],
        (1,),
        [
            pltpu.VMEM((depth, width), BF16),
            pltpu.VMEM((depth, width), BF16),
            pltpu.VMEM((steps, depth, width), BF16),
            pltpu.VMEM((steps, depth, width), BF16),
            pltpu.VMEM((2, QUAD, QUAD, piece, width), BF16),
            pltpu.VMEM((2, QUAD, steps * piece, width), BF16),
            pltpu.SemaphoreType.DMA((2 + 2 * steps,)),
            pltpu.SemaphoreType.DMA((2, 2)),
        ],
        flops=4 * depth * steps * width * width,
        moved=4 * (depth + depth * steps + steps * width) * width,
    )[0]


def side_grad(info, routed, dense):
    _, depth, width = dense[0].shape
    half = PIECES // 2
    piece = width // PIECES

    dims = (half, 4 * piece, width)
    return run(
        side_grad_body,
        info,
        [(v, whole(v.shape)) for v in routed] + [(v, ANY) for v in dense],
        [(shape(dims, BF16), ANY)] * 2,
        (1,),
        [
            pltpu.VMEM((2, depth, width), BF16),
            pltpu.VMEM((2, 3, depth, width), BF16),
            pltpu.VMEM((2, depth, width), BF16),
            pltpu.VMEM((2, depth, width), BF16),
            pltpu.VMEM((2, width, width), BF16),
            pltpu.SemaphoreType.DMA((12,)),
            pltpu.SemaphoreType.DMA((4, PIECES)),
        ],
        flops=16 * depth * width * width,
        moved=24 * depth * width,
    )


def quad_grad(info, parts, grads, w_back):
    hidden, width = w_back.shape
    rows = grads[0].shape[0]
    sub = hidden // QUAD
    dims = (2, 2 * sub // QUAD, width)
    total = QUAD * rows
    return run(
        quad_grad_body,
        info,
        [(v, ANY) for v in parts + grads + [w_back]],
        [(shape(dims, BF16), ANY)] * 2,
        (1,),
        [
            pltpu.VMEM((hidden, width), BF16),
            pltpu.VMEM((sub, total), BF16),
            pltpu.VMEM((hidden, total), BF16),
            pltpu.VMEM((parts[0].shape[0] - sub - hidden, total), BF16),
            pltpu.VMEM((total, width), BF16),
            pltpu.VMEM((hidden, total), BF16),
            pltpu.VMEM((QUAD, *dims[1:]), BF16),
            pltpu.SemaphoreType.DMA((3 + hidden // width, 1 + QUAD)),
            pltpu.SemaphoreType.DMA((2,)),
        ],
        flops=8 * sub * total * width,
        moved=10 * sub * total,
    )


def to_section(value, source):
    return lax.ppermute(value, "section", [(source, 1 - source)])


def swap_section(value):
    return lax.ppermute(value, "section", [(0, 1), (1, 0)])


def after(value, *earlier):
    return lax.optimization_barrier((value, *earlier))[0]


def added_up(parts):
    total = parts[0].astype(F32)
    for part in parts[1:]:
        total = total + part.astype(F32)
    return total


def cross(orders, value, stage):
    count = lax.axis_size("dp")
    low = count // PIECES
    pairs = []
    for section, order in enumerate(orders):
        base = section * count
        flip = low << order[stage]
        pairs += [(base + n, base + (n ^ flip)) for n in range(count)]
    return lax.ppermute(value, ("section", "dp"), pairs)


def cross_first(value, *axes):
    count = lax.axis_size("dp")
    flip = sum((count // PIECES) << axis for axis in axes)
    return lax.ppermute(value, ("section", "dp"), [(n, n ^ flip) for n in range(count)])


def scatter_layers(value):
    stride = QUAD * (lax.axis_size("dp") // PIECES)
    groups = [[base + n * stride for n in range(QUAD)] for base in range(stride)]
    return lax.psum_scatter(value, "dp", scatter_dimension=0, axis_index_groups=groups, tiled=True)


class Exchange:
    def __init__(self, stay, go, swap, stages):
        self.stay, self.go, self.swap = stay, go, swap
        self.stages, self.stage, self.flying = stages, 0, None

    def start(self, info):
        if self.stage:
            half = self.stay[0].shape[0] // 2
            self.go = [part[half:] for part in self.stay]
            self.stay = [part[:half] for part in self.stay]
        send = added_up(self.go).astype(BF16) if len(self.go) > 1 else self.go[0]
        info, send = lax.optimization_barrier((info, send))
        self.flying = self.swap(send, self.stage)
        self.stage += 1
        return info

    def total(self):
        assert self.stage == self.stages
        return added_up(self.stay)[0]


def settle(info, *values):
    arrays = [value.flying if isinstance(value, Exchange) else value for value in values]
    info, *arrays = lax.optimization_barrier((info, *arrays))
    plain = []
    for value, array in zip(values, arrays):
        if isinstance(value, Exchange):
            value.stay = value.stay + [array]
        else:
            plain.append(array)
    return (info, *plain)


def share_out(piece):
    count = lax.axis_size("dp")
    low = count // PIECES
    if low > 1:
        rows, cols = piece.shape
        place = lax.axis_index("dp") % low
        parts = jnp.take(piece.reshape(low, rows // low, cols), jnp.arange(low) ^ place, axis=0)
        while parts.shape[0] > 1:
            half = parts.shape[0] // 2
            far = lax.ppermute(parts[half:], "dp", [(n, n ^ half) for n in range(count)])
            parts = parts[:half] + far
        piece = parts[0]
    return piece[None]


def across(value, flip):
    return lax.ppermute(value, "dp", [(n, n ^ flip) for n in range(lax.axis_size("dp"))])


X, Y, Z, ZZ = 0, 1, 2, 3
ORDERS = ((X, Y, Z, ZZ), (Y, X, Z, ZZ))
SIDE = 2


def shards(inputs, out_grad, picks, valid, router, gain_attn, w_qkv, w_out, gain_mlp, w_in, w_back):
    w_qkv, w_out, w_in, w_back = w_qkv[0], w_out[0], w_in[0], w_back[0]
    seqs, cap = picks.shape
    seq_len = inputs.shape[0] // seqs
    width = inputs.shape[1]
    hidden = w_in.shape[1]
    rows = seqs * cap
    tiles = seq_len // TILE
    section = lax.axis_index("section")
    spot = lax.axis_index("dp") // (lax.axis_size("dp") // PIECES)
    first = section == 0

    table = [(mine, 0) + ORDERS[mine] for mine in (0, 1)]
    facts = jnp.where(first, jnp.array(table[0]), jnp.array(table[1]))
    info = jnp.where(jnp.arange(len(table[0])) == 1, spot, facts).astype(jnp.int32)

    far_qkv = to_section(w_qkv, 1)
    far_out = to_section(w_out, 1)
    far_in = to_section(w_in, 1)

    weight_bufs = [pltpu.VMEM(w.shape, BF16) for w in (w_qkv, w_out, w_in, w_back)]
    weight_bufs.append(pltpu.SemaphoreType.DMA((4,)))
    weight_ins = [(w_qkv, ANY), (w_out, ANY), (w_in, ANY), (w_back, ANY)]

    def full(array):
        return (array, whole(array.shape))

    def made(dims, dtype):
        return (shape(dims, dtype), whole(dims))

    routed_flops = 2 * rows * (4 * width * width + 2 * width * hidden)
    weight_bytes = 2 * (4 * width * width + 2 * width * hidden)
    sub = hidden // QUAD
    kept = [
        shape((rows, width), BF16),
        shape((rows, width), BF16),
        shape((rows, 3 * width), BF16),
        shape((rows, width), BF16),
        shape((rows, width), F32),
        shape((rows, hidden), BF16),
        shape((rows, width), F32),
    ]
    (
        gate0, open0, near, away, chosen, normed0, packed0, mixed0, rows0, slope0, branch0,
        stay0, over_x, over_y, over_xy,
    ) = run(
        routed_forward_body,
        info,
        [(inputs, ANY)] + [full(v) for v in (picks, valid, gain_attn, gain_mlp, router)] + weight_ins,
        [
            made((rows, LANES), F32),
            made((rows, LANES), F32),
            made((cap, width), BF16),
            made((cap + EXTRA, width), BF16),
        ]
        + [(v, ANY) for v in kept]
        + [(shape((sub + width // QUAD + hidden, rows), BF16), ANY)] * QUAD,
        (1,),
        [pltpu.VMEM(v.shape, v.dtype) for v in kept]
        + [pltpu.VMEM(inputs.shape, BF16)]
        + weight_bufs[:4]
        + [pltpu.VMEM((rows, hidden), BF16), pltpu.VMEM((QUAD, sub + width // QUAD, rows), BF16), pltpu.VMEM((hidden, rows), BF16)]
        + weight_bufs[4:]
        + [pltpu.SemaphoreType.DMA((seqs,)), pltpu.SemaphoreType.DMA((len(kept) + 2 * QUAD,))],
        flops=routed_flops,
        moved=weight_bytes,
    )
    info, far_qkv, far_out, far_in, near, away, over_x, over_y, over_xy, w_back_now = settle(
        info, far_qkv, far_out, far_in, near, away, over_x, over_y, over_xy, w_back
    )
    away = swap_section(away)

    def row_tile(dims):
        return pl.BlockSpec(dims, lambda i, info_ref: (i, 0))

    def seq_tile(tile=TILE):
        return pl.BlockSpec((tile, width), lambda i, info_ref: (info_ref[0] * (seq_len // tile) + i, 0))

    def tiled(cols, dtype, tile=TILE):
        return (shape((seq_len, cols), dtype), row_tile((tile, cols)))

    three_tile = pl.BlockSpec((3, WIDE, width), lambda i, info_ref: (0, i, 0))
    three_low = pl.BlockSpec((3, TILE, width), lambda i, info_ref: (0, i, 0))
    three = shape((3, seq_len, width), BF16)

    middle, normed1, packed1, middle_sel = run(
        dense_in_body,
        info,
        [
            (inputs, seq_tile(WIDE)),
            full(near),
            full(away),
            full(picks),
            full(gain_attn),
            (w_qkv, ANY),
            (far_qkv, ANY),
        ],
        [tiled(width, F32, WIDE), tiled(width, BF16, WIDE), (three, three_tile), made((cap, width), F32)],
        (seq_len // WIDE,),
        [pltpu.VMEM(w_qkv.shape, BF16), pltpu.SemaphoreType.DMA],
        flops=6 * seq_len * width * width,
        moved=seq_len * width * 12 + 6 * width * width,
    )

    info, packed1, over_x, over_y, over_xy, w_back_now = settle(
        info, packed1, over_x, over_y, over_xy, w_back_now
    )
    far_back = to_section(w_back_now, 1)
    from_x = cross_first(over_x, X)
    from_y = cross_first(over_y, Y)
    from_xy = cross_first(over_xy, X, Y)

    pair_spec = pl.BlockSpec((3, seq_len, LANES), lambda h, info_ref: (0, 0, h))
    column_spec = pl.BlockSpec((seq_len, LANES), lambda h, info_ref: (0, h))
    logsum_spec = pl.BlockSpec((1, 8, seq_len), lambda h, info_ref: (h, 0, 0))
    attend_flops = 2 * HEADS * seq_len * seq_len * TILE
    mixed1, logsum1 = run(
        attend_forward_body,
        info,
        [(packed1, pair_spec)],
        [
            (shape((seq_len, width), BF16), column_spec),
            (shape((PAIRS, 8, seq_len), F32), logsum_spec),
        ],
        (PAIRS,),
        flops=attend_flops,
        moved=8 * seq_len * width,
    )

    info, mixed1, far_back = settle(info, mixed1, far_back)
    pack1, act1, hidden1, mid1, carry, grad_mixed1, gain_mlp_sum, carried = run(
        feed_body,
        info,
        [
            (mixed1, row_tile((TILE, width))),
            (normed1, row_tile((TILE, width))),
            (middle, row_tile((TILE, width))),
            (out_grad, seq_tile()),
            full(gain_mlp),
            full(away),
            full(picks),
            full(middle_sel),
            (w_out, ANY),
            (far_out, ANY),
            (w_in, ANY),
            (far_in, ANY),
            (w_back, ANY),
            (far_back, ANY),
        ],
        [
            (shape((4, seq_len, width), BF16), pl.BlockSpec((4, TILE, width), lambda i, info_ref: (0, i, 0))),
            tiled(hidden, BF16),
            tiled(hidden, BF16),
            tiled(width, BF16),
            tiled(width, F32),
            tiled(width, BF16),
            made((8, width), F32),
            made((2, cap, width), F32),
        ],
        (tiles,),
        [
            pltpu.VMEM(w_out.shape, BF16),
            pltpu.VMEM(w_in.shape, BF16),
            pltpu.VMEM(w_back.shape, BF16),
            pltpu.SemaphoreType.DMA((1 + 2 * hidden // width,)),
        ],
        flops=2 * seq_len * width * (2 * width + 4 * hidden),
        moved=seq_len * (20 * width + 4 * hidden) + 2 * width * (width + 2 * hidden),
    )
    info, mid1, pack1, carried, from_x, from_y, from_xy = settle(info, mid1, pack1, carried, from_x, from_y, from_xy)
    far_pack = to_section(pack1, 0)
    far_carried = to_section(carried, 1)
    feed = feed_grad(info, mid1, hidden1, act1, out_grad)
    info, feed, far_pack, far_carried = settle(info, feed, far_pack, far_carried)
    feed = lax.psum_scatter(feed.reshape(-1, width), "section", scatter_dimension=0, tiled=True)

    def attend_backward(info, start, held):
        def third(rows):
            return pl.BlockSpec((3, rows, LANES), lambda h, info_ref: (0, 0, start + h))

        column = pl.BlockSpec((seq_len, LANES), lambda h, info_ref: (0, start + h))
        logsums = pl.BlockSpec((1, 8, seq_len), lambda h, info_ref: (start + h, 0, 0))
        return run(
            attend_backward_body,
            info,
            [(packed1, third(seq_len)), (grad_mixed1, column), (mixed1, column), (logsum1, logsums), full(picks)]
            + [(v, ANY) for v in held],
            [(three, third(seq_len)), (shape((3, cap, width), BF16), third(cap))],
            (PAIRS // 2,),
            [pltpu.VMEM((seq_len, LANES), F32)],
            flops=5 * attend_flops // 4,
            moved=8 * seq_len * width,
            aliases={6: 0, 7: 1} if held else {},
        )

    held = attend_backward(info, 0, [])
    info, feed, *held = settle(info, feed, *held)
    feed = scatter_layers(feed)
    packed_grad1, packed_sel = attend_backward(info, PAIRS // 2, held)
    info, packed_grad1, packed_sel = settle(info, packed_grad1, packed_sel)
    far_packed_sel = to_section(packed_sel, 1)
    info, far_packed_sel, packed_grad1 = settle(info, far_packed_sel, packed_grad1)
    far_packed = to_section(packed_grad1, 0)

    made_back = [shape((rows, width), BF16), shape((rows, width), BF16), shape((3, rows, width), BF16)]
    grad_chosen, small0, g_own, attn0, packed_grad0 = run(
        routed_backward_body,
        info,
        [
            full(v)
            for v in (
                packed_sel, far_packed_sel, carried, far_carried,
                chosen, branch0, gate0, valid, gain_attn, gain_mlp, router, away,
            )
        ]
        + [(v, ANY) for v in (packed0, rows0, slope0, far_qkv)]
        + weight_ins,
        [made((rows, width), F32), made((8, width), F32)] + [(v, ANY) for v in made_back],
        (1,),
        weight_bufs[:4]
        + [pltpu.VMEM((rows, hidden), BF16)]
        + [pltpu.VMEM(v.shape, v.dtype) for v in (packed0, rows0, slope0, *made_back)]
        + [pltpu.SemaphoreType.DMA((5,)), pltpu.SemaphoreType.DMA((3,)), pltpu.SemaphoreType.DMA((3,))],
        flops=routed_flops,
        moved=weight_bytes,
    )
    info, small0, packed_grad0, far_packed, g_own = settle(info, small0, packed_grad0, far_packed, g_own)
    g_x = cross_first(g_own, X)
    g_y = cross_first(g_own, Y)
    g_xy = cross_first(g_own, X, Y)

    side_stay, side_go = side_grad(
        info,
        [normed0, packed_grad0, mixed0, attn0],
        [packed_grad1, far_packed, pack1, far_pack],
    )
    info, side_go, g_x, g_y, g_xy = settle(info, side_go, g_x, g_y, g_xy)
    side = Exchange([side_stay], [side_go], functools.partial(cross, ORDERS), STAGES)
    info = side.start(info)

    grad_middle, gain_attn_sum = run(
        dense_out_body,
        info,
        [
            (packed_grad1, three_low),
            (carry, row_tile((TILE, width))),
            (middle, row_tile((TILE, width))),
            full(gain_attn),
            full(away),
            (w_qkv, ANY),
            (far_qkv, ANY),
        ],
        [tiled(width, BF16), made((8, width), F32)],
        (tiles,),
        [pltpu.VMEM(w_qkv.shape, BF16), pltpu.SemaphoreType.DMA],
        flops=6 * seq_len * width * width,
        moved=seq_len * width * 16 + 6 * width * width,
    )
    info, grad_middle, gain_attn_sum = settle(info, grad_middle, gain_attn_sum)
    far_grad = to_section(grad_middle, 1)
    small = jnp.where(first, small0, 0.0) + gain_mlp_sum + gain_attn_sum
    small_far = swap_section(small)
    info, small_far = settle(info, small_far)
    small = small + small_far
    small_far = across(small, 8)
    quad_go, quad_stay = quad_grad(
        info, [stay0, from_x, from_y, from_xy],
        [g_own, g_x, g_y, g_xy], w_back,
    )
    info, quad_go, far_grad, small_far, feed = settle(info, quad_go, far_grad, small_far, feed, side)
    info = side.start(info)
    small = after(small + small_far, info)
    small_far = across(small, 2)
    quad = Exchange([quad_stay], [quad_go], lambda value, stage: cross_first(value, (Z, ZZ)[stage]), 2)
    info = quad.start(info)
    far_places = jnp.where(first, jnp.array([0, 2, 1, 3]), jnp.array([0, 1, 2, 3])) ^ (spot & 3)
    feed = jnp.take(feed.reshape(QUAD, -1, width), far_places, axis=0)
    feed = Exchange([feed[:2]], [feed[2:]], functools.partial(cross, ORDERS), 2)
    info = feed.start(info)

    def end_spec(core, seq, paired):
        def at(s, i, info_ref):
            step = jnp.where((info_ref[0] == core) & (s == seq), i, 0)
            return (0, step, 0) if paired else (step, 0)

        return pl.BlockSpec((1, WIDE, width) if paired else (WIDE, width), at)

    ends = run(
        ends_body,
        info,
        [
            (pack1, end_spec(1, 1, True)),
            (grad_middle, end_spec(0, 0, False)),
            (far_pack, end_spec(1, 0, True)),
            (far_grad, end_spec(0, 1, False)),
            (grad_chosen, pl.BlockSpec((cap, width), lambda s, i, info_ref: (s, 0))),
            (picks, pl.BlockSpec((seqs, cap), lambda s, i, info_ref: (0, 0))),
        ],
        [
            (
                shape((seqs * seq_len, width), BF16),
                pl.BlockSpec((WIDE, width), lambda s, i, info_ref: (s * (seq_len // WIDE) + i, 0)),
            )
        ],
        (seqs, seq_len // WIDE),
        flops=4 * seqs * seq_len * cap * width,
        moved=8 * seqs * seq_len * width,
    )[0]

    info, ends = settle(info, ends, side)
    info = side.start(info)
    info, small_far = settle(info, small_far, quad, feed)
    small = small + small_far
    small_far = across(small, 4)
    info = quad.start(info)
    info = feed.start(info)
    info, small_far = settle(info, small_far, side)
    info = side.start(info)
    small = after(small + small_far, info)
    small_far = across(small, 1)
    info, = settle(info, feed)
    feed1 = feed.total()
    back1 = to_section(feed1.astype(BF16), 0).astype(F32)
    info, small_far, back1 = settle(info, small_far, back1)
    info, small_far = settle(info, small_far, quad)

    def gain_share(routed_row, dense_row):
        row = jnp.where(first, small[routed_row], small[dense_row])
        return lax.dynamic_slice_in_dim(row, lax.axis_index("dp") * share, share)[None]

    piece = width // PIECES
    small = small + small_far
    flip = PIECES
    while flip < lax.axis_size("dp"):
        small = small + across(small, flip)
        flip *= 2
    share = width // lax.axis_size("dp")
    quad_sum = quad.total()
    back0, in0 = quad_sum[: hidden // PIECES], quad_sum[hidden // PIECES :]
    in0 = in0.reshape(QUAD, piece, width).transpose(1, 0, 2).reshape(piece, hidden)

    in1 = feed1.reshape(QUAD, piece, width).transpose(1, 0, 2).reshape(piece, hidden)
    settle(info, side)
    attend_sum = side.total()
    return (
        ends[None],
        small[0],
        gain_share(2, 4),
        share_out(jnp.concatenate([attend_sum[n : n + piece] for n in range(0, 3 * piece, piece)], axis=1)),
        share_out(attend_sum[3 * piece :]),
        gain_share(1, 3),
        share_out(jnp.where(first, in0, in1)),
        share_out(jnp.where(first, back0, back1)),
    )


def solution(mesh):
    placed = (
        P("dp", None),
        P("dp", None),
        P("dp", None),
        P("dp", None),
        P(),
        P("section", None),
        P("section", None, None),
        P("section", None, None),
        P("section", None),
        P("section", None, None),
        P("section", None, None),
    )
    return jax.shard_map(
        shards,
        mesh=mesh,
        in_specs=placed,
        out_specs=(
            P("section", "dp", None),
            P(),
            P("section", "dp"),
            P("section", "dp", None),
            P("section", "dp", None),
            P("section", "dp"),
            P("section", "dp", None),
            P("section", "dp", None),
        ),
        check_vma=False,
    )
```

```python
import functools

import jax
import jax.numpy as jnp
from jax import lax
from jax.experimental import pallas as pl
from jax.experimental.pallas import tpu as pltpu
from jax.sharding import PartitionSpec as P

HEADS = 12
HEAD_DIM = 64
LANES = 128
PAIRS = HEADS * HEAD_DIM // LANES
EPS = 1e-06
FACTOR = HEAD_DIM ** (-0.5)
PIECES = 16
STAGES = 4
QUAD = 4
EXTRA = 16
TILE = 256
WIDE = 512
VMEM_BYTES = 56 * 1024 * 1024
BF16 = jnp.bfloat16
F32 = jnp.float32


def nn(a, b):
    return lax.dot_general(a, b, (((1,), (0,)), ((), ())), preferred_element_type=F32)


def nt(a, b):
    return lax.dot_general(a, b, (((1,), (1,)), ((), ())), preferred_element_type=F32)


def tn(a, b):
    return lax.dot_general(a, b, (((0,), (0,)), ((), ())), preferred_element_type=F32)


def shape(dims, dtype):
    return jax.ShapeDtypeStruct(dims, dtype)


def whole(dims):
    zeros = (0,) * len(dims)
    return pl.BlockSpec(dims, lambda *_: zeros)


ANY = pl.BlockSpec(memory_space=pl.ANY)


def run(body, info, ins, outs, grid, scratch=(), flops=0, moved=0, aliases=()):
    arrays, in_specs = zip(*ins)
    shapes, out_specs = zip(*outs)
    return pl.pallas_call(
        body,
        out_shape=shapes,
        input_output_aliases=dict(aliases),
        grid_spec=pltpu.PrefetchScalarGridSpec(
            num_scalar_prefetch=1,
            grid=grid,
            in_specs=in_specs,
            out_specs=out_specs,
            scratch_shapes=scratch,
        ),
        compiler_params=pltpu.CompilerParams(
            vmem_limit_bytes=VMEM_BYTES, dimension_semantics=("arbitrary",) * len(grid)
        ),
        cost_estimate=pl.CostEstimate(flops=flops // 4, bytes_accessed=moved // 4, transcendentals=0),
    )(info, *arrays)


def top_lanes(rows):
    return lax.broadcasted_iota(jnp.int32, (rows, LANES), 1) < HEAD_DIM


def lane_head(rows, which):
    lane = lax.broadcasted_iota(jnp.int32, (rows, LANES), 1)
    return (lane < HEAD_DIM) if which == 0 else (lane >= HEAD_DIM)


def head_only(value, which):
    return jnp.where(lane_head(value.shape[0], which), value, jnp.zeros_like(value))


def mean_square_scale(rows):
    return lax.rsqrt(jnp.mean(rows * rows, axis=-1, keepdims=True) + EPS)


def norm_back(grad, rows, scale, gain):
    hat = rows * scale
    scaled = grad * gain
    back = scale * (scaled - hat * jnp.mean(scaled * hat, axis=-1, keepdims=True))
    return back, jnp.sum(grad * hat, axis=0, keepdims=True)


def gelu_parts(pre):
    root = 0.7978845608028654
    square = pre * pre
    bent = jnp.tanh(root * pre * (1.0 + 0.044715 * square))
    half = 0.5 * (1.0 + bent)
    slope = half + 0.5 * pre * (1.0 - bent * bent) * (root * (1.0 + 0.134145 * square))
    return pre * half, slope


def fetch(info, local, remote, buf, sem):
    @pl.when(info[0] == 1)
    def _():
        pltpu.make_async_copy(local, buf, sem).start()

    @pl.when(info[0] == 0)
    def _():
        pltpu.make_async_copy(remote, buf, sem).start()


def arrived(source, buf, sem):
    pltpu.make_async_copy(source, buf, sem).wait()


def stacked(value):
    return jnp.concatenate([head_only(value, h) for h in range(2)], axis=0)


def unstacked(value):
    half = value.shape[0] // 2
    return jnp.where(top_lanes(half), value[:half], value[half:])


def slot_pieces(packed, seq, pair, cap):
    rows = slice(seq * cap, (seq + 1) * cap)
    width = HEADS * HEAD_DIM
    first = pair * LANES
    queries = stacked(packed[rows, first : first + LANES] * BF16(FACTOR))
    keys = packed[rows, width + first : width + first + LANES]
    values = packed[rows, 2 * width + first : 2 * width + first + LANES]
    return queries, keys, values


def slot_rule(valid_row, cap):
    query = lax.broadcasted_iota(jnp.int32, (cap, cap), 0)
    key = lax.broadcasted_iota(jnp.int32, (cap, cap), 1)
    rule = (key <= query) & ((valid_row > 0) | (key == query))
    return jnp.concatenate([rule, rule], axis=0)


def column_of(row):
    return jnp.transpose(jnp.broadcast_to(row, (row.shape[1], row.shape[1])))


def slot_mask(valid):
    seqs = valid.shape[0]
    return jnp.concatenate([column_of(valid[s : s + 1, :].astype(F32)) for s in range(seqs)], axis=0)[:, 0:1]


def weight_copies(sources, bufs, sems):
    return [pltpu.make_async_copy(a, b, sems.at[n]) for n, (a, b) in enumerate(zip(sources, bufs))]


def routed_forward_body(
    info, x, picks, valid, gain_attn, gain_mlp, router, w_qkv, w_out, w_in, w_back,
    gate_o, open_o, near_o, away_o, chosen_h, normed_h, packed_h, mixed_h, rows_h, slope_h, branch_h,
    stay_o, over_x_o, over_y_o, over_xy_o,
    chosen_o, normed_o, packed_o, mixed_o, rows_o, slope_o, branch_o,
    b_x, b_qkv, b_out, b_in, b_back, act_b, shares, slope_t, sems, x_sems, out_sems,
):
    @pl.when(info[0] == 1)
    def _():
        rest = jnp.concatenate([gain_attn[...], gain_mlp[...]], axis=0)
        count = away_o.shape[0] - EXTRA
        for part in range(3):
            rounded = rest.astype(BF16)
            away_o[count + 2 * part : count + 2 * part + 2, :] = rounded
            rest = rest - rounded.astype(F32)

    @pl.when(info[0] == 0)
    def _():
        copies = weight_copies((w_qkv, w_out, w_in, w_back), (b_qkv, b_out, b_in, b_back), sems)
        seqs, cap = valid.shape
        seq_len = x.shape[0] // seqs
        loads = []
        for seq in range(seqs):
            at = pl.ds(seq * seq_len, seq_len)
            loads.append(pltpu.make_async_copy(x.at[at], b_x.at[at], x_sems.at[seq]))
        for copy in loads + copies:
            copy.start()
        sends = []

        def send(source, target):
            sends.append(pltpu.make_async_copy(source, target, out_sems.at[len(sends)]))
            sends[-1].start()

        parts = []
        for seq in range(seqs):
            place = lax.broadcasted_iota(jnp.int32, (seq_len, cap), 0)
            hot = (picks[seq : seq + 1, :] == place).astype(BF16)
            loads[seq].wait()
            parts.append(tn(hot, b_x[seq * seq_len : (seq + 1) * seq_len, :]))
        chosen = jnp.concatenate(parts, axis=0)
        chosen_o[...] = chosen.astype(BF16)
        send(chosen_o, chosen_h)
        gates = jax.nn.sigmoid(jnp.sum(chosen * router[...].reshape(1, -1), axis=-1, keepdims=True))
        gate_o[...] = jnp.broadcast_to(gates, gate_o.shape)
        normed = (chosen * mean_square_scale(chosen) * gain_attn[...]).astype(BF16)
        normed_o[...] = normed
        send(normed_o, normed_h)
        copies[0].wait()
        packed_o[...] = nn(normed, b_qkv[...]).astype(BF16)
        send(packed_o, packed_h)
        work = [(seq, pair) for seq in range(seqs) for pair in range(PAIRS)]
        allowed = [slot_rule(valid[seq : seq + 1, :], cap) for seq in range(seqs)]
        pieces = [slot_pieces(packed_o, seq, pair, cap) for seq, pair in work]
        scores = [jnp.where(allowed[w[0]], nt(p[0], p[1]), -1e30) for w, p in zip(work, pieces)]
        grown = [jnp.exp(v - jnp.max(v, axis=-1, keepdims=True)).astype(BF16) for v in scores]
        ones = jnp.ones((cap, LANES), BF16)
        outs = [nn(g, jnp.concatenate([p[2], ones], axis=1)) for g, p in zip(grown, pieces)]
        outs = [unstacked(o[:, :LANES] / o[:, LANES:]).astype(BF16) for o in outs]
        mixed = jnp.concatenate(
            [jnp.concatenate(outs[s * PAIRS : (s + 1) * PAIRS], axis=1) for s in range(seqs)], axis=0
        )
        mixed_o[...] = mixed
        send(mixed_o, mixed_h)
        copies[1].wait()
        attn_out = nn(mixed, b_out[...])
        rows = chosen + attn_out
        rows_o[...] = rows
        send(rows_o, rows_h)
        normed_mid = (rows * mean_square_scale(rows) * gain_mlp[...]).astype(BF16)
        member = info[1] & 3
        piece = b_in.shape[1] // PIECES
        mid_turned = jnp.transpose(normed_mid)
        count = mid_turned.shape[0] // PIECES
        sub = piece * QUAD
        for dest in range(PIECES):
            at = sub + dest // QUAD * count
            shares[(dest % QUAD) ^ member, at : at + count, :] = mid_turned[dest * count : (dest + 1) * count, :]
        copies[2].wait()
        step = 768
        for first in range(0, b_in.shape[1], step):
            cols = slice(first, first + step)
            act, slope = gelu_parts(nn(normed_mid, b_in[:, cols]))
            act = act.astype(BF16)
            slope = slope.astype(BF16)
            act_b[:, cols] = act
            slope_o[:, cols] = slope
            chunk = first // step
            slope_t[first : first + step, :] = jnp.transpose(slope)
            turned = jnp.transpose(act)
            for owner in range(QUAD):
                shares[owner ^ member, chunk * piece : (chunk + 1) * piece, :] = turned[
                    owner * piece : (owner + 1) * piece, :
                ]
        send(slope_o, slope_h)
        for n, out in enumerate((stay_o, over_x_o, over_y_o, over_xy_o)):
            send(shares.at[n], out.at[pl.ds(0, shares.shape[1])])
            send(slope_t, out.at[pl.ds(shares.shape[1], slope_t.shape[0])])
        copies[3].wait()
        branch = attn_out + nn(act_b[...], b_back[...])
        branch_o[...] = branch
        send(branch_o, branch_h)
        opened = gates * slot_mask(valid)
        open_o[...] = jnp.broadcast_to(opened, open_o.shape)
        delta = (opened * branch).astype(BF16)
        near_o[...] = delta[:cap]
        away_o[:cap, :] = delta[cap:]
        for copy in sends:
            copy.wait()


def routed_backward_body(
    info, p_near, p_far, r_near, r_far, chosen_i, branch, gate, valid, gain_attn, gain_mlp, router, swapped,
    packed_h, rows_h, slope_h, w_next, w_qkv, w_out, w_in, w_back,
    chosen_o, small_o, ffn_h, attn_h, packed_out,
    b_qkv, b_out, b_in, b_back, hidden_b, packed, rows_i, slope, ffn_o, attn_o, packed_o, sems, in_sems, out_sems,
):
    @pl.when(info[0] == 0)
    def _():
        copies = weight_copies((w_qkv, w_out, w_in, w_back), (b_qkv, b_out, b_in, b_back), sems)
        upper = pltpu.make_async_copy(w_next, b_qkv, sems.at[4])
        upper.start()
        loads = [
            pltpu.make_async_copy(source, target, in_sems.at[n])
            for n, (source, target) in enumerate(((slope_h, slope), (rows_h, rows_i), (packed_h, packed)))
        ]
        for copy in (copies[3], loads[0], copies[2], loads[1], copies[1], loads[2]):
            copy.start()
        sends = []

        def send(source, target):
            sends.append(pltpu.make_async_copy(source, target, out_sems.at[len(sends)]))
            sends[-1].start()

        seqs, cap = valid.shape
        chosen = chosen_i[...].astype(F32)
        width = chosen.shape[1]
        upper.wait()
        upper_gain = dense_gain(info, gain_attn, swapped, 0)
        grad_sel = []
        for dense, carried in ((p_near, r_near), (p_far, r_far)):
            grad_normed = sum(nt(dense[n], b_qkv[:, n * width : (n + 1) * width]) for n in range(3))
            middle = carried[1]
            back, _ = norm_back(grad_normed, middle, mean_square_scale(middle), upper_gain)
            grad_sel.append((carried[0] + back).astype(BF16).astype(F32))
        grad_sel = jnp.concatenate(grad_sel, axis=0)
        copies[0].start()
        gates = gate[:, 0:1]
        mask = slot_mask(valid)
        logit = jnp.sum(grad_sel * branch[...], axis=-1, keepdims=True) * mask * gates * (1.0 - gates)
        grad = grad_sel * (gates * mask)
        grad_ffn = grad.astype(BF16)
        ffn_o[...] = grad_ffn
        send(ffn_o, ffn_h)
        copies[3].wait()
        loads[0].wait()
        step = 768
        for first in range(0, b_in.shape[1], step):
            cols = slice(first, first + step)
            hidden = (nt(grad_ffn, b_back[cols, :]) * slope[:, cols].astype(F32)).astype(BF16)
            hidden_b[:, cols] = hidden
        copies[2].wait()
        grad_mid = nt(hidden_b[...], b_in[...])
        loads[1].wait()
        rows = rows_i[...]
        grad_rows, gain_mlp_sum = norm_back(grad_mid, rows, mean_square_scale(rows), gain_mlp[...])
        grad_attn = (grad + grad_rows).astype(BF16)
        attn_o[...] = grad_attn
        send(attn_o, attn_h)
        copies[1].wait()
        grad_mixed = nt(grad_attn, b_out[...]).astype(BF16)
        loads[2].wait()
        work = [(seq, pair) for seq in range(seqs) for pair in range(PAIRS)]
        allowed = [slot_rule(valid[seq : seq + 1, :], cap) for seq in range(seqs)]
        pieces = [slot_pieces(packed, seq, pair, cap) for seq, pair in work]
        grads = [
            stacked(grad_mixed[seq * cap : (seq + 1) * cap, pair * LANES : (pair + 1) * LANES])
            for seq, pair in work
        ]
        scores = [jnp.where(allowed[w[0]], nt(p[0], p[1]), -1e30) for w, p in zip(work, pieces)]
        grad_probs = [nt(g, p[2]) for g, p in zip(grads, pieces)]
        grown = [jnp.exp(v - jnp.max(v, axis=-1, keepdims=True)) for v in scores]
        probs = [v / jnp.sum(v, axis=-1, keepdims=True) for v in grown]
        lows = [
            (p * (g - jnp.sum(p * g, axis=-1, keepdims=True))).astype(BF16) for p, g in zip(probs, grad_probs)
        ]
        for (seq, pair), piece, grad_head, prob, low in zip(work, pieces, grads, probs, lows):
            at = slice(seq * cap, (seq + 1) * cap)
            cols = slice(pair * LANES, (pair + 1) * LANES)
            packed_o[0, at, cols] = (unstacked(nn(low, piece[1])) * FACTOR).astype(BF16)
            packed_o[1, at, cols] = tn(low, piece[0]).astype(BF16)
            packed_o[2, at, cols] = tn(prob.astype(BF16), grad_head).astype(BF16)
        send(packed_o, packed_out)
        copies[0].wait()
        grad_normed = sum(nt(packed_o[n], b_qkv[:, n * width : (n + 1) * width]) for n in range(3))
        back, gain_attn_sum = norm_back(grad_normed, chosen, mean_square_scale(chosen), gain_attn[...])
        chosen_o[...] = grad_rows + back + logit * router[...].reshape(1, -1)
        small_o[...] = jnp.zeros(small_o.shape, F32)
        small_o[0:1, :] = jnp.sum(logit * chosen, axis=0, keepdims=True)
        small_o[1:2, :] = gain_mlp_sum
        small_o[2:3, :] = gain_attn_sum
        for copy in sends:
            copy.wait()


def dense_gain(info, local, swapped, row):
    first = swapped.shape[0] - EXTRA + row
    far = sum(swapped[first + n : first + n + 1, :].astype(F32) for n in (0, 2, 4))
    return jnp.where(info[0] == 1, local[...], far)


def dense_in_body(
    info, x, near, away, picks, gain, w_local, w_far, middle_o, normed_o, packed_o, sel_o, b_qkv, sem
):
    step = pl.program_id(0)

    @pl.when(step == 0)
    def _():
        fetch(info, w_local, w_far, b_qkv, sem)

    rows, width = x.shape
    cap = near.shape[0]
    delta = jnp.where(info[0] == 0, near[...], away[:cap, :])
    place = step * rows + lax.broadcasted_iota(jnp.int32, (rows, cap), 0)
    hot = (picks[pl.ds(info[0], 1), :] == place).astype(BF16)
    middle = x[...].astype(F32) + nn(hot, delta)
    middle_o[...] = middle

    @pl.when(step == 0)
    def _():
        sel_o[...] = delta.astype(F32)

    sel_o[...] += tn(hot, x[...])
    normed = (middle * mean_square_scale(middle) * dense_gain(info, gain, away, 0)).astype(BF16)
    normed_o[...] = normed

    @pl.when(step == 0)
    def _():
        arrived(w_local, b_qkv, sem)

    for n in range(3):
        packed_o[n] = nn(normed, b_qkv[:, n * width : (n + 1) * width]).astype(BF16)


def attend_forward_body(info, packed, mixed_o, logsum_o):
    seq_len = packed.shape[1]
    tile = 2 * TILE
    queries = packed[0] * BF16(FACTOR)
    keys = packed[1]
    ones = jnp.ones((seq_len, LANES), BF16)
    values = [jnp.concatenate([head_only(packed[2], h), ones], axis=1) for h in range(2)]
    below = lax.broadcasted_iota(jnp.int32, (tile, tile), 1) <= lax.broadcasted_iota(jnp.int32, (tile, tile), 0)
    for first in range(0, seq_len, tile):
        upto = first + tile
        at = slice(first, upto)
        scores = []
        for head in range(2):
            score = nt(head_only(queries[at], head), keys[:upto])
            last = jnp.where(below, score[:, first:], -1e30)
            scores.append(jnp.concatenate([score[:, :first], last], axis=1) if first else last)
        tops = [jnp.max(score, axis=-1, keepdims=True) for score in scores]
        grown = [jnp.exp(score - top).astype(BF16) for score, top in zip(scores, tops)]
        outs = [nn(g, value[:upto]) for g, value in zip(grown, values)]
        mixed = sum(out[:, :LANES] * (1.0 / out[:, LANES:]) for out in outs)
        mixed_o[at, :] = mixed.astype(BF16)
        sums = [top + jnp.log(out[:, LANES:]) for top, out in zip(tops, outs)]
        turned = jnp.transpose(jnp.where(top_lanes(tile), sums[0], sums[1]))
        logsum_o[0, 0:1, at] = turned[0:1]
        logsum_o[0, 1:2, at] = turned[HEAD_DIM : HEAD_DIM + 1]


def attend_backward_body(info, packed, grad, mixed, logsum, picks, *refs):
    out, sel_o, grad_q = refs[-3:]
    seq_len = packed.shape[1]
    queries = packed[0] * BF16(FACTOR)
    queries = [head_only(queries, h) for h in range(2)]
    key_heads = [head_only(packed[1], h) for h in range(2)]
    grads = [head_only(grad[...], h) for h in range(2)]
    product = grad[...].astype(F32) * mixed[...].astype(F32)
    pick_row = lax.broadcasted_iota(jnp.int32, (8, LANES), 0)
    pick_lane = lax.broadcasted_iota(jnp.int32, (8, LANES), 1)
    pick = (pick_row == pick_lane // HEAD_DIM).astype(F32)
    inner = lax.dot_general(
        pick, product, (((1,), (1,)), ((), ())), precision=lax.Precision.HIGHEST, preferred_element_type=F32
    )
    above = lax.broadcasted_iota(jnp.int32, (TILE, TILE), 0) <= lax.broadcasted_iota(
        jnp.int32, (TILE, TILE), 1
    )
    for first in range(0, seq_len, TILE):
        kat = slice(first, first + TILE)
        keys = packed[1, kat, :]
        values = packed[2, kat, :]
        dks, dvs, dqs = [], [], []
        for head in range(2):
            query = queries[head][first:]
            grad_head = grads[head][first:]
            probs = jnp.exp(nt(keys, query) - logsum[0, head : head + 1, first:])
            edge = jnp.where(above, probs[:, :TILE], 0.0)
            probs = jnp.concatenate([edge, probs[:, TILE:]], axis=1) if first + TILE < seq_len else edge
            grad_probs = nt(values, grad_head)
            low = (probs * (grad_probs - inner[head : head + 1, first:])).astype(BF16)
            dvs.append(nn(probs.astype(BF16), grad_head))
            dks.append(nn(low, query))
            dqs.append(tn(low, key_heads[head][kat]))
        if first == 0:
            grad_q[...] = dqs[0] + dqs[1]
        else:
            grad_q[first:, :] += dqs[0] + dqs[1]
        out[1, kat, :] = (dks[0] + dks[1]).astype(BF16)
        out[2, kat, :] = (dvs[0] + dvs[1]).astype(BF16)
    out[0] = (grad_q[...] * FACTOR).astype(BF16)
    cap = picks.shape[1]
    place = lax.broadcasted_iota(jnp.int32, (seq_len, cap), 0)
    hot = (picks[pl.ds(info[0], 1), :] == place).astype(BF16)
    for n in range(3):
        sel_o[n] = tn(hot, out[n]).astype(BF16)


def feed_body(
    info, mixed, normed, middle, out_grad, gain_in, swapped, picks, middle_sel, wo_l, wo_f, wi_l, wi_f, wb_l, wb_f,
    pack_o, act_o, hidden_o, mid_o, carry_o, mixed_o, gain_o, sel_o,
    b_out, b_in, b_back, sems,
):
    step = pl.program_id(0)
    width = middle.shape[1]
    starts = range(0, b_in.shape[1], width)

    @pl.when(step == 0)
    def _():
        fetch(info, wo_l, wo_f, b_out, sems.at[0])
        for n, first in enumerate(starts):
            cols = pl.ds(first, width)
            fetch(info, wi_l.at[:, cols], wi_f.at[:, cols], b_in.at[:, cols], sems.at[1 + 2 * n])
            fetch(info, wb_l.at[cols], wb_f.at[cols], b_back.at[cols], sems.at[2 + 2 * n])
        gain_o[...] = jnp.zeros(gain_o.shape, F32)
        sel_o[0] = jnp.zeros(middle_sel.shape, F32)
        sel_o[1] = middle_sel[...]
        arrived(wo_l, b_out, sems.at[0])

    gain = dense_gain(info, gain_in, swapped, 1)
    pack_o[2] = mixed[...]
    pack_o[3] = normed[...]
    rows = middle[...] + nn(mixed[...], b_out[...])
    scale = mean_square_scale(rows)
    normed_mid = (rows * scale * gain).astype(BF16)
    mid_o[...] = normed_mid
    grad_ffn = out_grad[...]

    def hidden_block(first):
        cols = slice(first, first + width)
        act, slope = gelu_parts(nn(mid_o[...], b_in[:, cols]))
        act_o[:, cols] = act.astype(BF16)
        hidden_o[:, cols] = (nt(out_grad[...], b_back[cols, :]) * slope).astype(BF16)

    @pl.when(step == 0)
    def _():
        for n, first in enumerate(starts):
            cols = pl.ds(first, width)
            arrived(wi_l.at[:, cols], b_in.at[:, cols], sems.at[1 + 2 * n])
            arrived(wb_l.at[cols], b_back.at[cols], sems.at[2 + 2 * n])
            hidden_block(first)

    @pl.when(step > 0)
    def _():
        for first in starts:
            hidden_block(first)

    pack_o[0] = (rows + nn(act_o[...], b_back[...])).astype(BF16)
    grad_mid = nt(hidden_o[...], b_in[...])
    back, gain_sum = norm_back(grad_mid, rows, scale, gain)
    carry = grad_ffn.astype(F32) + back
    carry_o[...] = carry
    grad_attn = carry.astype(BF16)
    pack_o[1] = grad_attn
    mixed_o[...] = nt(grad_attn, b_out[...]).astype(BF16)
    gain_o[3:4, :] += gain_sum
    count, cap = carry.shape[0], middle_sel.shape[0]
    place = step * count + lax.broadcasted_iota(jnp.int32, (count, cap), 0)
    hot = (picks[pl.ds(info[0], 1), :] == place).astype(BF16)
    sel_o[0] += tn(hot, grad_attn) + tn(hot, (carry - grad_attn.astype(F32)).astype(BF16))


def dense_out_body(
    info, packed, carry, middle, gain_in, swapped, w_local, w_far, grad_o, gain_o, b_qkv, sem
):
    step = pl.program_id(0)

    @pl.when(step == 0)
    def _():
        fetch(info, w_local, w_far, b_qkv, sem)
        gain_o[...] = jnp.zeros(gain_o.shape, F32)
        arrived(w_local, b_qkv, sem)

    width = middle.shape[1]
    grad_normed = sum(nt(packed[n], b_qkv[:, n * width : (n + 1) * width]) for n in range(3))
    rows = middle[...]
    gain = dense_gain(info, gain_in, swapped, 0)
    back, gain_sum = norm_back(grad_normed, rows, mean_square_scale(rows), gain)
    gain_o[4:5, :] += gain_sum
    grad_o[...] = (carry[...] + back).astype(BF16)


def ends_body(info, result_block, grad, far_block, far_grad, grad_chosen, picks, out):
    seq = pl.program_id(0)
    step = pl.program_id(1)

    @pl.when(info[0] == 1)
    def _():
        out[...] = jnp.where(seq == 1, result_block[0], far_block[0])

    @pl.when(info[0] == 0)
    def _():
        base = jnp.where(seq == 0, grad[...], far_grad[...]).astype(F32)
        rows = out.shape[0]
        cap = grad_chosen.shape[0]
        place = step * rows + lax.broadcasted_iota(jnp.int32, (rows, cap), 0)
        hot = (picks[pl.ds(seq, 1), :] == place).astype(BF16)
        high = grad_chosen[...].astype(BF16)
        low = (grad_chosen[...] - high.astype(F32)).astype(BF16)
        out[...] = (base + (nn(hot, high) + nn(hot, low))).astype(BF16)


def feed_grad_body(
    info, mid, hidden, act, out_grad, out, mid_b, grad_b, hidden_b, act_b, ring_in, ring_back, in_sems, out_sems
):
    steps, rows, width = hidden_b.shape
    piece = width // PIECES

    def load(source, target, n):
        return pltpu.make_async_copy(source, target, in_sems.at[n])

    mine = pl.ds(pl.multiple_of(info[0] * rows, rows), rows)
    loads = [load(mid, mid_b, 0)]
    loads += [load(hidden.at[:, pl.ds(t * width, width)], hidden_b.at[t], 1 + t) for t in range(steps)]
    loads += [load(out_grad.at[mine], grad_b, 1 + steps)]
    loads += [load(act.at[:, pl.ds(t * width, width)], act_b.at[t], 2 + steps + t) for t in range(steps)]
    for copy in loads:
        copy.start()
    sent = []
    for n in range(2 * steps):
        t = n % steps
        if t == 0:
            loads[0 if n == 0 else 1 + steps].wait()
        loads[1 + t if n < steps else 2 + steps + t].wait()
        product = tn(mid_b[...], hidden_b[t]) if n < steps else tn(act_b[t], grad_b[...])
        ring = ring_in if n < steps else ring_back
        if t >= 2:
            sent[n - 2].wait()
        ring[n % 2] = product.astype(BF16).reshape(ring.shape[1:])
        target = out.at[1, :, :, pl.ds(t * piece, piece)] if n < steps else out.at[0, t]
        sent.append(pltpu.make_async_copy(ring.at[n % 2], target, out_sems.at[n // steps, n % 2]))
        sent[-1].start()
    for n in (steps - 2, steps - 1, 2 * steps - 2, 2 * steps - 1):
        sent[n].wait()


def origin(info, base, place):
    relative = 0
    for stage in range(STAGES):
        if place >> (STAGES - 1 - stage) & 1:
            relative = relative | (1 << info[base + stage])
    return info[1] ^ relative


def put_block(info, outs, product, slot, spot, ring, sems):
    piece = product.shape[0] // PIECES
    ring[spot] = product.astype(BF16)
    half = PIECES // 2
    sent = []
    for place in range(PIECES):
        rows = pl.ds(pl.multiple_of(origin(info, SIDE, place) * piece, piece), piece)
        target = outs[place // half].at[place % half, pl.ds(slot * piece, piece)]
        sent.append(pltpu.make_async_copy(ring.at[spot, rows], target, sems.at[slot, place]))
        sent[-1].start()
    return sent


def side_grad_body(
    info, normed0, packed0, mixed0, attn0,
    p_near, p_far, near, far,
    out_stay, out_go,
    n_buf, p_buf, m_buf, a_buf, ring, sems, out_sems,
):
    outs = (out_stay, out_go)

    def put_all(order, product):
        sent = []
        for n, slot in enumerate(order):
            value = product(slot)
            if n >= 2:
                for copy in sent[n - 2]:
                    copy.wait()
            sent.append(put_block(info, outs, value, slot, n % 2, ring, out_sems))
        for copies in sent[-2:]:
            for copy in copies:
                copy.wait()

    @pl.when(info[0] == 0)
    def _():
        put_all((3, 0, 1, 2), lambda n: tn(normed0[...], packed0[n]) if n < 3 else tn(mixed0[...], attn0[...]))

    @pl.when(info[0] == 1)
    def _():
        sources = [
            (source.at[which], target, n)
            for which, target in ((2, m_buf), (1, a_buf), (3, n_buf))
            for n, source in enumerate((near, far))
        ]
        copies = [
            pltpu.make_async_copy(source, target.at[n], sems.at[k])
            for k, (source, target, n) in enumerate(sources)
        ]
        blocks = [
            pltpu.make_async_copy(source.at[which], p_buf.at[n, which], sems.at[6 + 2 * which + n])
            for which in range(3)
            for n, source in enumerate((p_near, p_far))
        ]
        for copy in copies + blocks:
            copy.start()

        def product(n):
            if n == 3:
                for copy in copies[:4]:
                    copy.wait()
                return tn(m_buf[0], a_buf[0]) + tn(m_buf[1], a_buf[1])
            for copy in (copies[4:] if n == 0 else []) + blocks[2 * n : 2 * n + 2]:
                copy.wait()
            return tn(n_buf[0], p_buf[0, n]) + tn(n_buf[1], p_buf[1, n])

        put_all((3, 0, 1, 2), product)


def quad_grad_body(
    info, stay, from_x, from_y, from_xy, g_own, g_x, g_y, g_xy, w_back, go_o, stay_o,
    b_back, acts, slopes, mids, grads, hidden, held, sems, out_sems,
):
    @pl.when(info[0] == 0)
    def _():
        rows = g_own.shape[0]
        width = grads.shape[1]
        sub = acts.shape[0]
        steps = b_back.shape[0] // width
        piece = sub // QUAD
        count = mids.shape[0] // QUAD
        copies = []

        def load(source, target, n, k):
            copies.append(pltpu.make_async_copy(source, target, sems.at[n, k]))
            copies[-1].start()
            return copies[-1]

        first = [load(g, grads.at[pl.ds(n * rows, rows)], 0, n) for n, g in enumerate((g_own, g_x, g_y, g_xy))]
        parts = (stay, from_x, from_y, from_xy)
        blocks, lefts = [], []
        for t in range(steps):
            at = pl.ds(t * width, width)
            blocks.append([load(w_back.at[at], b_back.at[at], 1 + t, QUAD)])
            for n, source in enumerate(parts):
                here = pl.ds(sub + QUAD * count + t * width, width)
                blocks[t].append(load(source.at[here], slopes.at[at, pl.ds(n * rows, rows)], 1 + t, n))
        for n, source in enumerate(parts):
            to = pl.ds(n * rows, rows)
            lefts.append(load(source.at[pl.ds(0, sub)], acts.at[:, to], 1 + steps, n))
            lefts.append(load(source.at[pl.ds(sub, QUAD * count)], mids.at[:, to], 2 + steps, n))
        for copy in first:
            copy.wait()
        for t in range(steps):
            at = slice(t * width, (t + 1) * width)
            for copy in blocks[t]:
                copy.wait()
            hidden[at, :] = (nt(b_back[at, :], grads[...]) * slopes[at, :].astype(F32)).astype(BF16)
        for copy in lefts:
            copy.wait()
        layer = info[1] >> 2

        def put(z, rows_at, value):
            place = layer ^ z
            place = ((place & 1) << 1) | (place >> 1)

            held[place, rows_at, :] = value

        product = nn(acts[...], grads[...]).astype(BF16)
        for z in range(QUAD):
            put(z, slice(0, piece), product[z * piece : (z + 1) * piece, :])
        for t in range(steps):
            product = nt(mids[...], hidden[t * width : (t + 1) * width, :]).astype(BF16)
            for z in range(QUAD):
                put(z, slice(piece + t * count, piece + (t + 1) * count), product[z * count : (z + 1) * count, :])
        outs = [
            pltpu.make_async_copy(held.at[pl.ds(first, 2)], out, out_sems.at[n])
            for n, (first, out) in enumerate(((2, go_o), (0, stay_o)))
        ]
        for copy in outs:
            copy.start()
        for copy in outs:
            copy.wait()


def feed_grad(info, mid, hidden, act, out_grad):
    depth, width = mid.shape
    steps = hidden.shape[1] // width
    piece = width // PIECES
    return run(
        feed_grad_body,
        info,
        [(v, ANY) for v in (mid, hidden, act, out_grad)],
        [(shape((2, QUAD, QUAD, steps * piece, width), BF16), ANY)],
        (1,),
        [
            pltpu.VMEM((depth, width), BF16),
            pltpu.VMEM((depth, width), BF16),
            pltpu.VMEM((steps, depth, width), BF16),
            pltpu.VMEM((steps, depth, width), BF16),
            pltpu.VMEM((2, QUAD, QUAD, piece, width), BF16),
            pltpu.VMEM((2, QUAD, steps * piece, width), BF16),
            pltpu.SemaphoreType.DMA((2 + 2 * steps,)),
            pltpu.SemaphoreType.DMA((2, 2)),
        ],
        flops=4 * depth * steps * width * width,
        moved=4 * (depth + depth * steps + steps * width) * width,
    )[0]


def side_grad(info, routed, dense):
    _, depth, width = dense[0].shape
    half = PIECES // 2
    piece = width // PIECES

    dims = (half, 4 * piece, width)
    return run(
        side_grad_body,
        info,
        [(v, whole(v.shape)) for v in routed] + [(v, ANY) for v in dense],
        [(shape(dims, BF16), ANY)] * 2,
        (1,),
        [
            pltpu.VMEM((2, depth, width), BF16),
            pltpu.VMEM((2, 3, depth, width), BF16),
            pltpu.VMEM((2, depth, width), BF16),
            pltpu.VMEM((2, depth, width), BF16),
            pltpu.VMEM((2, width, width), BF16),
            pltpu.SemaphoreType.DMA((12,)),
            pltpu.SemaphoreType.DMA((4, PIECES)),
        ],
        flops=16 * depth * width * width,
        moved=24 * depth * width,
    )


def quad_grad(info, parts, grads, w_back):
    hidden, width = w_back.shape
    rows = grads[0].shape[0]
    sub = hidden // QUAD
    dims = (2, 2 * sub // QUAD, width)
    total = QUAD * rows
    return run(
        quad_grad_body,
        info,
        [(v, ANY) for v in parts + grads + [w_back]],
        [(shape(dims, BF16), ANY)] * 2,
        (1,),
        [
            pltpu.VMEM((hidden, width), BF16),
            pltpu.VMEM((sub, total), BF16),
            pltpu.VMEM((hidden, total), BF16),
            pltpu.VMEM((parts[0].shape[0] - sub - hidden, total), BF16),
            pltpu.VMEM((total, width), BF16),
            pltpu.VMEM((hidden, total), BF16),
            pltpu.VMEM((QUAD, *dims[1:]), BF16),
            pltpu.SemaphoreType.DMA((3 + hidden // width, 1 + QUAD)),
            pltpu.SemaphoreType.DMA((2,)),
        ],
        flops=8 * sub * total * width,
        moved=10 * sub * total,
    )


def to_section(value, source):
    return lax.ppermute(value, "section", [(source, 1 - source)])


def swap_section(value):
    return lax.ppermute(value, "section", [(0, 1), (1, 0)])


def after(value, *earlier):
    return lax.optimization_barrier((value, *earlier))[0]


def added_up(parts):
    total = parts[0].astype(F32)
    for part in parts[1:]:
        total = total + part.astype(F32)
    return total


def cross(orders, value, stage):
    count = lax.axis_size("dp")
    low = count // PIECES
    pairs = []
    for section, order in enumerate(orders):
        base = section * count
        flip = low << order[stage]
        pairs += [(base + n, base + (n ^ flip)) for n in range(count)]
    return lax.ppermute(value, ("section", "dp"), pairs)


def cross_first(value, *axes):
    count = lax.axis_size("dp")
    flip = sum((count // PIECES) << axis for axis in axes)
    return lax.ppermute(value, ("section", "dp"), [(n, n ^ flip) for n in range(count)])


def scatter_layers(value):
    stride = QUAD * (lax.axis_size("dp") // PIECES)
    groups = [[base + n * stride for n in range(QUAD)] for base in range(stride)]
    return lax.psum_scatter(value, "dp", scatter_dimension=0, axis_index_groups=groups, tiled=True)


class Exchange:
    def __init__(self, stay, go, swap, stages):
        self.stay, self.go, self.swap = stay, go, swap
        self.stages, self.stage, self.flying = stages, 0, None

    def start(self, info):
        if self.stage:
            half = self.stay[0].shape[0] // 2
            self.go = [part[half:] for part in self.stay]
            self.stay = [part[:half] for part in self.stay]
        send = added_up(self.go).astype(BF16) if len(self.go) > 1 else self.go[0]
        info, send = lax.optimization_barrier((info, send))
        self.flying = self.swap(send, self.stage)
        self.stage += 1
        return info

    def total(self):
        assert self.stage == self.stages
        return added_up(self.stay)[0]


def settle(info, *values):
    arrays = [value.flying if isinstance(value, Exchange) else value for value in values]
    info, *arrays = lax.optimization_barrier((info, *arrays))
    plain = []
    for value, array in zip(values, arrays):
        if isinstance(value, Exchange):
            value.stay = value.stay + [array]
        else:
            plain.append(array)
    return (info, *plain)


def share_out(piece):
    count = lax.axis_size("dp")
    low = count // PIECES
    if low > 1:
        rows, cols = piece.shape
        place = lax.axis_index("dp") % low
        parts = jnp.take(piece.reshape(low, rows // low, cols), jnp.arange(low) ^ place, axis=0)
        while parts.shape[0] > 1:
            half = parts.shape[0] // 2
            far = lax.ppermute(parts[half:], "dp", [(n, n ^ half) for n in range(count)])
            parts = parts[:half] + far
        piece = parts[0]
    return piece[None]


def across(value, flip):
    return lax.ppermute(value, "dp", [(n, n ^ flip) for n in range(lax.axis_size("dp"))])


X, Y, Z, ZZ = 0, 1, 2, 3
ORDERS = ((X, Y, Z, ZZ), (Y, X, Z, ZZ))
SIDE = 2


def shards(inputs, out_grad, picks, valid, router, gain_attn, w_qkv, w_out, gain_mlp, w_in, w_back):
    w_qkv, w_out, w_in, w_back = w_qkv[0], w_out[0], w_in[0], w_back[0]
    seqs, cap = picks.shape
    seq_len = inputs.shape[0] // seqs
    width = inputs.shape[1]
    hidden = w_in.shape[1]
    rows = seqs * cap
    tiles = seq_len // TILE
    section = lax.axis_index("section")
    spot = lax.axis_index("dp") // (lax.axis_size("dp") // PIECES)
    first = section == 0

    table = [(mine, 0) + ORDERS[mine] for mine in (0, 1)]
    facts = jnp.where(first, jnp.array(table[0]), jnp.array(table[1]))
    info = jnp.where(jnp.arange(len(table[0])) == 1, spot, facts).astype(jnp.int32)

    far_qkv = to_section(w_qkv, 1)
    far_out = to_section(w_out, 1)
    far_in = to_section(w_in, 1)

    weight_bufs = [pltpu.VMEM(w.shape, BF16) for w in (w_qkv, w_out, w_in, w_back)]
    weight_bufs.append(pltpu.SemaphoreType.DMA((4,)))
    weight_ins = [(w_qkv, ANY), (w_out, ANY), (w_in, ANY), (w_back, ANY)]

    def full(array):
        return (array, whole(array.shape))

    def made(dims, dtype):
        return (shape(dims, dtype), whole(dims))

    routed_flops = 2 * rows * (4 * width * width + 2 * width * hidden)
    weight_bytes = 2 * (4 * width * width + 2 * width * hidden)
    sub = hidden // QUAD
    kept = [
        shape((rows, width), BF16),
        shape((rows, width), BF16),
        shape((rows, 3 * width), BF16),
        shape((rows, width), BF16),
        shape((rows, width), F32),
        shape((rows, hidden), BF16),
        shape((rows, width), F32),
    ]
    (
        gate0, open0, near, away, chosen, normed0, packed0, mixed0, rows0, slope0, branch0,
        stay0, over_x, over_y, over_xy,
    ) = run(
        routed_forward_body,
        info,
        [(inputs, ANY)] + [full(v) for v in (picks, valid, gain_attn, gain_mlp, router)] + weight_ins,
        [
            made((rows, LANES), F32),
            made((rows, LANES), F32),
            made((cap, width), BF16),
            made((cap + EXTRA, width), BF16),
        ]
        + [(v, ANY) for v in kept]
        + [(shape((sub + width // QUAD + hidden, rows), BF16), ANY)] * QUAD,
        (1,),
        [pltpu.VMEM(v.shape, v.dtype) for v in kept]
        + [pltpu.VMEM(inputs.shape, BF16)]
        + weight_bufs[:4]
        + [pltpu.VMEM((rows, hidden), BF16), pltpu.VMEM((QUAD, sub + width // QUAD, rows), BF16), pltpu.VMEM((hidden, rows), BF16)]
        + weight_bufs[4:]
        + [pltpu.SemaphoreType.DMA((seqs,)), pltpu.SemaphoreType.DMA((len(kept) + 2 * QUAD,))],
        flops=routed_flops,
        moved=weight_bytes,
    )
    info, far_qkv, far_out, far_in, near, away, over_x, over_y, over_xy, w_back_now = settle(
        info, far_qkv, far_out, far_in, near, away, over_x, over_y, over_xy, w_back
    )
    away = swap_section(away)

    def row_tile(dims):
        return pl.BlockSpec(dims, lambda i, info_ref: (i, 0))

    def seq_tile(tile=TILE):
        return pl.BlockSpec((tile, width), lambda i, info_ref: (info_ref[0] * (seq_len // tile) + i, 0))

    def tiled(cols, dtype, tile=TILE):
        return (shape((seq_len, cols), dtype), row_tile((tile, cols)))

    three_tile = pl.BlockSpec((3, WIDE, width), lambda i, info_ref: (0, i, 0))
    three_low = pl.BlockSpec((3, TILE, width), lambda i, info_ref: (0, i, 0))
    three = shape((3, seq_len, width), BF16)

    middle, normed1, packed1, middle_sel = run(
        dense_in_body,
        info,
        [
            (inputs, seq_tile(WIDE)),
            full(near),
            full(away),
            full(picks),
            full(gain_attn),
            (w_qkv, ANY),
            (far_qkv, ANY),
        ],
        [tiled(width, F32, WIDE), tiled(width, BF16, WIDE), (three, three_tile), made((cap, width), F32)],
        (seq_len // WIDE,),
        [pltpu.VMEM(w_qkv.shape, BF16), pltpu.SemaphoreType.DMA],
        flops=6 * seq_len * width * width,
        moved=seq_len * width * 12 + 6 * width * width,
    )

    info, packed1, over_x, over_y, over_xy, w_back_now = settle(
        info, packed1, over_x, over_y, over_xy, w_back_now
    )
    far_back = to_section(w_back_now, 1)
    from_x = cross_first(over_x, X)
    from_y = cross_first(over_y, Y)
    from_xy = cross_first(over_xy, X, Y)

    pair_spec = pl.BlockSpec((3, seq_len, LANES), lambda h, info_ref: (0, 0, h))
    column_spec = pl.BlockSpec((seq_len, LANES), lambda h, info_ref: (0, h))
    logsum_spec = pl.BlockSpec((1, 8, seq_len), lambda h, info_ref: (h, 0, 0))
    attend_flops = 2 * HEADS * seq_len * seq_len * TILE
    mixed1, logsum1 = run(
        attend_forward_body,
        info,
        [(packed1, pair_spec)],
        [
            (shape((seq_len, width), BF16), column_spec),
            (shape((PAIRS, 8, seq_len), F32), logsum_spec),
        ],
        (PAIRS,),
        flops=attend_flops,
        moved=8 * seq_len * width,
    )

    info, mixed1, far_back = settle(info, mixed1, far_back)
    pack1, act1, hidden1, mid1, carry, grad_mixed1, gain_mlp_sum, carried = run(
        feed_body,
        info,
        [
            (mixed1, row_tile((TILE, width))),
            (normed1, row_tile((TILE, width))),
            (middle, row_tile((TILE, width))),
            (out_grad, seq_tile()),
            full(gain_mlp),
            full(away),
            full(picks),
            full(middle_sel),
            (w_out, ANY),
            (far_out, ANY),
            (w_in, ANY),
            (far_in, ANY),
            (w_back, ANY),
            (far_back, ANY),
        ],
        [
            (shape((4, seq_len, width), BF16), pl.BlockSpec((4, TILE, width), lambda i, info_ref: (0, i, 0))),
            tiled(hidden, BF16),
            tiled(hidden, BF16),
            tiled(width, BF16),
            tiled(width, F32),
            tiled(width, BF16),
            made((8, width), F32),
            made((2, cap, width), F32),
        ],
        (tiles,),
        [
            pltpu.VMEM(w_out.shape, BF16),
            pltpu.VMEM(w_in.shape, BF16),
            pltpu.VMEM(w_back.shape, BF16),
            pltpu.SemaphoreType.DMA((1 + 2 * hidden // width,)),
        ],
        flops=2 * seq_len * width * (2 * width + 4 * hidden),
        moved=seq_len * (20 * width + 4 * hidden) + 2 * width * (width + 2 * hidden),
    )
    info, mid1, pack1, carried, from_x, from_y, from_xy = settle(info, mid1, pack1, carried, from_x, from_y, from_xy)
    feed = feed_grad(info, mid1, hidden1, act1, out_grad)
    info, feed = settle(info, feed)
    feed = lax.psum_scatter(feed.reshape(-1, width), "section", scatter_dimension=0, tiled=True)

    def attend_backward(info, start, held):
        def third(rows):
            return pl.BlockSpec((3, rows, LANES), lambda h, info_ref: (0, 0, start + h))

        column = pl.BlockSpec((seq_len, LANES), lambda h, info_ref: (0, start + h))
        logsums = pl.BlockSpec((1, 8, seq_len), lambda h, info_ref: (start + h, 0, 0))
        return run(
            attend_backward_body,
            info,
            [(packed1, third(seq_len)), (grad_mixed1, column), (mixed1, column), (logsum1, logsums), full(picks)]
            + [(v, ANY) for v in held],
            [(three, third(seq_len)), (shape((3, cap, width), BF16), third(cap))],
            (PAIRS // 2,),
            [pltpu.VMEM((seq_len, LANES), F32)],
            flops=5 * attend_flops // 4,
            moved=8 * seq_len * width,
            aliases={6: 0, 7: 1} if held else {},
        )

    held = attend_backward(info, 0, [])
    info, pack1, carried, *held = settle(info, pack1, carried, *held)
    far_pack = to_section(pack1, 0)
    far_carried = to_section(carried, 1)
    info, feed = settle(info, feed)
    feed = scatter_layers(feed)
    packed_grad1, packed_sel = attend_backward(info, PAIRS // 2, held)
    info, packed_grad1, packed_sel, far_pack, far_carried = settle(
        info, packed_grad1, packed_sel, far_pack, far_carried
    )
    far_packed_sel = to_section(packed_sel, 1)
    info, far_packed_sel, packed_grad1 = settle(info, far_packed_sel, packed_grad1)
    far_packed = to_section(packed_grad1, 0)

    made_back = [shape((rows, width), BF16), shape((rows, width), BF16), shape((3, rows, width), BF16)]
    grad_chosen, small0, g_own, attn0, packed_grad0 = run(
        routed_backward_body,
        info,
        [
            full(v)
            for v in (
                packed_sel, far_packed_sel, carried, far_carried,
                chosen, branch0, gate0, valid, gain_attn, gain_mlp, router, away,
            )
        ]
        + [(v, ANY) for v in (packed0, rows0, slope0, far_qkv)]
        + weight_ins,
        [made((rows, width), F32), made((8, width), F32)] + [(v, ANY) for v in made_back],
        (1,),
        weight_bufs[:4]
        + [pltpu.VMEM((rows, hidden), BF16)]
        + [pltpu.VMEM(v.shape, v.dtype) for v in (packed0, rows0, slope0, *made_back)]
        + [pltpu.SemaphoreType.DMA((5,)), pltpu.SemaphoreType.DMA((3,)), pltpu.SemaphoreType.DMA((3,))],
        flops=routed_flops,
        moved=weight_bytes,
    )
    info, small0, packed_grad0, far_packed, g_own = settle(info, small0, packed_grad0, far_packed, g_own)
    g_x = cross_first(g_own, X)
    g_y = cross_first(g_own, Y)
    g_xy = cross_first(g_own, X, Y)

    side_stay, side_go = side_grad(
        info,
        [normed0, packed_grad0, mixed0, attn0],
        [packed_grad1, far_packed, pack1, far_pack],
    )
    info, side_go, g_x, g_y, g_xy = settle(info, side_go, g_x, g_y, g_xy)
    side = Exchange([side_stay], [side_go], functools.partial(cross, ORDERS), STAGES)
    info = side.start(info)

    grad_middle, gain_attn_sum = run(
        dense_out_body,
        info,
        [
            (packed_grad1, three_low),
            (carry, row_tile((TILE, width))),
            (middle, row_tile((TILE, width))),
            full(gain_attn),
            full(away),
            (w_qkv, ANY),
            (far_qkv, ANY),
        ],
        [tiled(width, BF16), made((8, width), F32)],
        (tiles,),
        [pltpu.VMEM(w_qkv.shape, BF16), pltpu.SemaphoreType.DMA],
        flops=6 * seq_len * width * width,
        moved=seq_len * width * 16 + 6 * width * width,
    )
    info, grad_middle, gain_attn_sum = settle(info, grad_middle, gain_attn_sum)
    far_grad = to_section(grad_middle, 1)
    small = jnp.where(first, small0, 0.0) + gain_mlp_sum + gain_attn_sum
    small_far = swap_section(small)
    info, small_far = settle(info, small_far)
    small = small + small_far
    small_far = across(small, 8)
    quad_go, quad_stay = quad_grad(
        info, [stay0, from_x, from_y, from_xy],
        [g_own, g_x, g_y, g_xy], w_back,
    )
    info, quad_go, far_grad, small_far, feed = settle(info, quad_go, far_grad, small_far, feed, side)
    info = side.start(info)
    small = after(small + small_far, info)
    small_far = across(small, 2)
    quad = Exchange([quad_stay], [quad_go], lambda value, stage: cross_first(value, (Z, ZZ)[stage]), 2)
    info = quad.start(info)
    far_places = jnp.where(first, jnp.array([0, 2, 1, 3]), jnp.array([0, 1, 2, 3])) ^ (spot & 3)
    feed = jnp.take(feed.reshape(QUAD, -1, width), far_places, axis=0)
    feed = Exchange([feed[:2]], [feed[2:]], functools.partial(cross, ORDERS), 2)
    info = feed.start(info)

    def end_spec(core, seq, paired):
        def at(s, i, info_ref):
            step = jnp.where((info_ref[0] == core) & (s == seq), i, 0)
            return (0, step, 0) if paired else (step, 0)

        return pl.BlockSpec((1, WIDE, width) if paired else (WIDE, width), at)

    ends = run(
        ends_body,
        info,
        [
            (pack1, end_spec(1, 1, True)),
            (grad_middle, end_spec(0, 0, False)),
            (far_pack, end_spec(1, 0, True)),
            (far_grad, end_spec(0, 1, False)),
            (grad_chosen, pl.BlockSpec((cap, width), lambda s, i, info_ref: (s, 0))),
            (picks, pl.BlockSpec((seqs, cap), lambda s, i, info_ref: (0, 0))),
        ],
        [
            (
                shape((seqs * seq_len, width), BF16),
                pl.BlockSpec((WIDE, width), lambda s, i, info_ref: (s * (seq_len // WIDE) + i, 0)),
            )
        ],
        (seqs, seq_len // WIDE),
        flops=4 * seqs * seq_len * cap * width,
        moved=8 * seqs * seq_len * width,
    )[0]

    info, ends = settle(info, ends, side)
    info = side.start(info)
    info, = settle(info, quad)
    info = quad.start(info)
    info, small_far = settle(info, small_far, feed)
    small = after(small + small_far, info)
    small_far = across(small, 4)
    info = feed.start(info)
    info, small_far = settle(info, small_far, side)
    info = side.start(info)
    small = after(small + small_far, info)
    small_far = across(small, 1)
    info, = settle(info, feed)
    feed1 = feed.total()
    back1 = to_section(feed1.astype(BF16), 0).astype(F32)
    info, small_far, back1 = settle(info, small_far, back1)
    info, small_far = settle(info, small_far, quad)

    def gain_share(routed_row, dense_row):
        row = jnp.where(first, small[routed_row], small[dense_row])
        return lax.dynamic_slice_in_dim(row, lax.axis_index("dp") * share, share)[None]

    piece = width // PIECES
    small = small + small_far
    flip = PIECES
    while flip < lax.axis_size("dp"):
        small = small + across(small, flip)
        flip *= 2
    share = width // lax.axis_size("dp")
    quad_sum = quad.total()
    back0, in0 = quad_sum[: hidden // PIECES], quad_sum[hidden // PIECES :]
    in0 = in0.reshape(QUAD, piece, width).transpose(1, 0, 2).reshape(piece, hidden)

    in1 = feed1.reshape(QUAD, piece, width).transpose(1, 0, 2).reshape(piece, hidden)
    w_in_out = share_out(jnp.where(first, in0, in1))
    w_back_out = share_out(jnp.where(first, back0, back1))
    gain_attn_out, gain_mlp_out = gain_share(2, 4), gain_share(1, 3)
    info, w_in_out, w_back_out, gain_attn_out, gain_mlp_out, small = settle(
        info, w_in_out, w_back_out, gain_attn_out, gain_mlp_out, small, side
    )
    attend_sum = side.total()
    return (
        ends[None],
        small[0],
        gain_attn_out,
        share_out(jnp.concatenate([attend_sum[n : n + piece] for n in range(0, 3 * piece, piece)], axis=1)),
        share_out(attend_sum[3 * piece :]),
        gain_mlp_out,
        w_in_out,
        w_back_out,
    )


def solution(mesh):
    placed = (
        P("dp", None),
        P("dp", None),
        P("dp", None),
        P("dp", None),
        P(),
        P("section", None),
        P("section", None, None),
        P("section", None, None),
        P("section", None),
        P("section", None, None),
        P("section", None, None),
    )
    return jax.shard_map(
        shards,
        mesh=mesh,
        in_specs=placed,
        out_specs=(
            P("section", "dp", None),
            P(),
            P("section", "dp"),
            P("section", "dp", None),
            P("section", "dp", None),
            P("section", "dp"),
            P("section", "dp", None),
            P("section", "dp", None),
        ),
        check_vma=False,
    )
```

```python
import functools

import jax
import jax.numpy as jnp
from jax import lax
from jax.experimental import pallas as pl
from jax.experimental.pallas import tpu as pltpu
from jax.sharding import PartitionSpec as P

HEADS = 12
HEAD_DIM = 64
LANES = 128
PAIRS = HEADS * HEAD_DIM // LANES
EPS = 1e-06
FACTOR = HEAD_DIM ** (-0.5)
PIECES = 16
STAGES = 4
QUAD = 4
EXTRA = 16
TILE = 256
WIDE = 512
VMEM_BYTES = 56 * 1024 * 1024
BF16 = jnp.bfloat16
F32 = jnp.float32


def nn(a, b):
    return lax.dot_general(a, b, (((1,), (0,)), ((), ())), preferred_element_type=F32)


def nt(a, b):
    return lax.dot_general(a, b, (((1,), (1,)), ((), ())), preferred_element_type=F32)


def tn(a, b):
    return lax.dot_general(a, b, (((0,), (0,)), ((), ())), preferred_element_type=F32)


def shape(dims, dtype):
    return jax.ShapeDtypeStruct(dims, dtype)


def whole(dims):
    zeros = (0,) * len(dims)
    return pl.BlockSpec(dims, lambda *_: zeros)


ANY = pl.BlockSpec(memory_space=pl.ANY)


def run(body, info, ins, outs, grid, scratch=(), flops=0, moved=0, aliases=()):
    arrays, in_specs = zip(*ins)
    shapes, out_specs = zip(*outs)
    return pl.pallas_call(
        body,
        out_shape=shapes,
        input_output_aliases=dict(aliases),
        grid_spec=pltpu.PrefetchScalarGridSpec(
            num_scalar_prefetch=1,
            grid=grid,
            in_specs=in_specs,
            out_specs=out_specs,
            scratch_shapes=scratch,
        ),
        compiler_params=pltpu.CompilerParams(
            vmem_limit_bytes=VMEM_BYTES, dimension_semantics=("arbitrary",) * len(grid)
        ),
        cost_estimate=pl.CostEstimate(flops=flops // 4, bytes_accessed=moved // 4, transcendentals=0),
    )(info, *arrays)


def top_lanes(rows):
    return lax.broadcasted_iota(jnp.int32, (rows, LANES), 1) < HEAD_DIM


def lane_head(rows, which):
    lane = lax.broadcasted_iota(jnp.int32, (rows, LANES), 1)
    return (lane < HEAD_DIM) if which == 0 else (lane >= HEAD_DIM)


def head_only(value, which):
    return jnp.where(lane_head(value.shape[0], which), value, jnp.zeros_like(value))


def mean_square_scale(rows):
    return lax.rsqrt(jnp.mean(rows * rows, axis=-1, keepdims=True) + EPS)


def norm_back(grad, rows, scale, gain):
    hat = rows * scale
    scaled = grad * gain
    back = scale * (scaled - hat * jnp.mean(scaled * hat, axis=-1, keepdims=True))
    return back, jnp.sum(grad * hat, axis=0, keepdims=True)


def gelu_parts(pre):
    root = 0.7978845608028654
    square = pre * pre
    bent = jnp.tanh(root * pre * (1.0 + 0.044715 * square))
    half = 0.5 * (1.0 + bent)
    slope = half + 0.5 * pre * (1.0 - bent * bent) * (root * (1.0 + 0.134145 * square))
    return pre * half, slope


def fetch(info, local, remote, buf, sem):
    @pl.when(info[0] == 1)
    def _():
        pltpu.make_async_copy(local, buf, sem).start()

    @pl.when(info[0] == 0)
    def _():
        pltpu.make_async_copy(remote, buf, sem).start()


def arrived(source, buf, sem):
    pltpu.make_async_copy(source, buf, sem).wait()


def stacked(value):
    return jnp.concatenate([head_only(value, h) for h in range(2)], axis=0)


def unstacked(value):
    half = value.shape[0] // 2
    return jnp.where(top_lanes(half), value[:half], value[half:])


def slot_pieces(packed, seq, pair, cap):
    rows = slice(seq * cap, (seq + 1) * cap)
    width = HEADS * HEAD_DIM
    first = pair * LANES
    queries = stacked(packed[rows, first : first + LANES] * BF16(FACTOR))
    keys = packed[rows, width + first : width + first + LANES]
    values = packed[rows, 2 * width + first : 2 * width + first + LANES]
    return queries, keys, values


def slot_rule(valid_row, cap):
    query = lax.broadcasted_iota(jnp.int32, (cap, cap), 0)
    key = lax.broadcasted_iota(jnp.int32, (cap, cap), 1)
    rule = (key <= query) & ((valid_row > 0) | (key == query))
    return jnp.concatenate([rule, rule], axis=0)


def column_of(row):
    return jnp.transpose(jnp.broadcast_to(row, (row.shape[1], row.shape[1])))


def slot_mask(valid):
    seqs = valid.shape[0]
    return jnp.concatenate([column_of(valid[s : s + 1, :].astype(F32)) for s in range(seqs)], axis=0)[:, 0:1]


def weight_copies(sources, bufs, sems):
    return [pltpu.make_async_copy(a, b, sems.at[n]) for n, (a, b) in enumerate(zip(sources, bufs))]


def routed_forward_body(
    info, x, picks, valid, gain_attn, gain_mlp, router, w_qkv, w_out, w_in, w_back,
    gate_o, open_o, near_o, away_o, chosen_h, normed_h, packed_h, mixed_h, rows_h, slope_h, branch_h,
    stay_o, over_x_o, over_y_o, over_xy_o,
    chosen_o, normed_o, packed_o, mixed_o, rows_o, slope_o, branch_o,
    b_x, b_qkv, b_out, b_in, b_back, act_b, shares, slope_t, sems, x_sems, out_sems,
):
    @pl.when(info[0] == 1)
    def _():
        rest = jnp.concatenate([gain_attn[...], gain_mlp[...]], axis=0)
        count = away_o.shape[0] - EXTRA
        for part in range(3):
            rounded = rest.astype(BF16)
            away_o[count + 2 * part : count + 2 * part + 2, :] = rounded
            rest = rest - rounded.astype(F32)

    @pl.when(info[0] == 0)
    def _():
        copies = weight_copies((w_qkv, w_out, w_in, w_back), (b_qkv, b_out, b_in, b_back), sems)
        seqs, cap = valid.shape
        seq_len = x.shape[0] // seqs
        loads = []
        for seq in range(seqs):
            at = pl.ds(seq * seq_len, seq_len)
            loads.append(pltpu.make_async_copy(x.at[at], b_x.at[at], x_sems.at[seq]))
        for copy in loads + copies:
            copy.start()
        sends = []

        def send(source, target):
            sends.append(pltpu.make_async_copy(source, target, out_sems.at[len(sends)]))
            sends[-1].start()

        parts = []
        for seq in range(seqs):
            place = lax.broadcasted_iota(jnp.int32, (seq_len, cap), 0)
            hot = (picks[seq : seq + 1, :] == place).astype(BF16)
            loads[seq].wait()
            parts.append(tn(hot, b_x[seq * seq_len : (seq + 1) * seq_len, :]))
        chosen = jnp.concatenate(parts, axis=0)
        chosen_o[...] = chosen.astype(BF16)
        send(chosen_o, chosen_h)
        gates = jax.nn.sigmoid(jnp.sum(chosen * router[...].reshape(1, -1), axis=-1, keepdims=True))
        gate_o[...] = jnp.broadcast_to(gates, gate_o.shape)
        normed = (chosen * mean_square_scale(chosen) * gain_attn[...]).astype(BF16)
        normed_o[...] = normed
        send(normed_o, normed_h)
        copies[0].wait()
        packed_o[...] = nn(normed, b_qkv[...]).astype(BF16)
        send(packed_o, packed_h)
        work = [(seq, pair) for seq in range(seqs) for pair in range(PAIRS)]
        allowed = [slot_rule(valid[seq : seq + 1, :], cap) for seq in range(seqs)]
        pieces = [slot_pieces(packed_o, seq, pair, cap) for seq, pair in work]
        scores = [jnp.where(allowed[w[0]], nt(p[0], p[1]), -1e30) for w, p in zip(work, pieces)]
        grown = [jnp.exp(v - jnp.max(v, axis=-1, keepdims=True)).astype(BF16) for v in scores]
        ones = jnp.ones((cap, LANES), BF16)
        outs = [nn(g, jnp.concatenate([p[2], ones], axis=1)) for g, p in zip(grown, pieces)]
        outs = [unstacked(o[:, :LANES] / o[:, LANES:]).astype(BF16) for o in outs]
        mixed = jnp.concatenate(
            [jnp.concatenate(outs[s * PAIRS : (s + 1) * PAIRS], axis=1) for s in range(seqs)], axis=0
        )
        mixed_o[...] = mixed
        send(mixed_o, mixed_h)
        copies[1].wait()
        attn_out = nn(mixed, b_out[...])
        rows = chosen + attn_out
        rows_o[...] = rows
        send(rows_o, rows_h)
        normed_mid = (rows * mean_square_scale(rows) * gain_mlp[...]).astype(BF16)
        member = info[1] & 3
        piece = b_in.shape[1] // PIECES
        mid_turned = jnp.transpose(normed_mid)
        count = mid_turned.shape[0] // PIECES
        sub = piece * QUAD
        for dest in range(PIECES):
            at = sub + dest // QUAD * count
            shares[(dest % QUAD) ^ member, at : at + count, :] = mid_turned[dest * count : (dest + 1) * count, :]
        copies[2].wait()
        step = 768
        for first in range(0, b_in.shape[1], step):
            cols = slice(first, first + step)
            act, slope = gelu_parts(nn(normed_mid, b_in[:, cols]))
            act = act.astype(BF16)
            slope = slope.astype(BF16)
            act_b[:, cols] = act
            slope_o[:, cols] = slope
            chunk = first // step
            slope_t[first : first + step, :] = jnp.transpose(slope)
            turned = jnp.transpose(act)
            for owner in range(QUAD):
                shares[owner ^ member, chunk * piece : (chunk + 1) * piece, :] = turned[
                    owner * piece : (owner + 1) * piece, :
                ]
        send(slope_o, slope_h)
        for n, out in enumerate((stay_o, over_x_o, over_y_o, over_xy_o)):
            send(shares.at[n], out.at[pl.ds(0, shares.shape[1])])
            send(slope_t, out.at[pl.ds(shares.shape[1], slope_t.shape[0])])
        copies[3].wait()
        branch = attn_out + nn(act_b[...], b_back[...])
        branch_o[...] = branch
        send(branch_o, branch_h)
        opened = gates * slot_mask(valid)
        open_o[...] = jnp.broadcast_to(opened, open_o.shape)
        delta = (opened * branch).astype(BF16)
        near_o[...] = delta[:cap]
        away_o[:cap, :] = delta[cap:]
        for copy in sends:
            copy.wait()


def routed_backward_body(
    info, p_near, p_far, r_near, r_far, chosen_i, branch, gate, valid, gain_attn, gain_mlp, router, swapped,
    packed_h, rows_h, slope_h, w_next, w_qkv, w_out, w_in, w_back,
    chosen_o, small_o, ffn_h, attn_h, packed_out,
    b_qkv, b_out, b_in, b_back, hidden_b, packed, rows_i, slope, ffn_o, attn_o, packed_o, sems, in_sems, out_sems,
):
    @pl.when(info[0] == 0)
    def _():
        copies = weight_copies((w_qkv, w_out, w_in, w_back), (b_qkv, b_out, b_in, b_back), sems)
        upper = pltpu.make_async_copy(w_next, b_qkv, sems.at[4])
        upper.start()
        loads = [
            pltpu.make_async_copy(source, target, in_sems.at[n])
            for n, (source, target) in enumerate(((slope_h, slope), (rows_h, rows_i), (packed_h, packed)))
        ]
        for copy in (copies[3], loads[0], copies[2], loads[1], copies[1], loads[2]):
            copy.start()
        sends = []

        def send(source, target):
            sends.append(pltpu.make_async_copy(source, target, out_sems.at[len(sends)]))
            sends[-1].start()

        seqs, cap = valid.shape
        chosen = chosen_i[...].astype(F32)
        width = chosen.shape[1]
        upper.wait()
        upper_gain = dense_gain(info, gain_attn, swapped, 0)
        grad_sel = []
        for dense, carried in ((p_near, r_near), (p_far, r_far)):
            grad_normed = sum(nt(dense[n], b_qkv[:, n * width : (n + 1) * width]) for n in range(3))
            middle = carried[1]
            back, _ = norm_back(grad_normed, middle, mean_square_scale(middle), upper_gain)
            grad_sel.append((carried[0] + back).astype(BF16).astype(F32))
        grad_sel = jnp.concatenate(grad_sel, axis=0)
        copies[0].start()
        gates = gate[:, 0:1]
        mask = slot_mask(valid)
        logit = jnp.sum(grad_sel * branch[...], axis=-1, keepdims=True) * mask * gates * (1.0 - gates)
        grad = grad_sel * (gates * mask)
        grad_ffn = grad.astype(BF16)
        ffn_o[...] = grad_ffn
        send(ffn_o, ffn_h)
        copies[3].wait()
        loads[0].wait()
        step = 768
        for first in range(0, b_in.shape[1], step):
            cols = slice(first, first + step)
            hidden = (nt(grad_ffn, b_back[cols, :]) * slope[:, cols].astype(F32)).astype(BF16)
            hidden_b[:, cols] = hidden
        copies[2].wait()
        grad_mid = nt(hidden_b[...], b_in[...])
        loads[1].wait()
        rows = rows_i[...]
        grad_rows, gain_mlp_sum = norm_back(grad_mid, rows, mean_square_scale(rows), gain_mlp[...])
        grad_attn = (grad + grad_rows).astype(BF16)
        attn_o[...] = grad_attn
        send(attn_o, attn_h)
        copies[1].wait()
        grad_mixed = nt(grad_attn, b_out[...]).astype(BF16)
        loads[2].wait()
        work = [(seq, pair) for seq in range(seqs) for pair in range(PAIRS)]
        allowed = [slot_rule(valid[seq : seq + 1, :], cap) for seq in range(seqs)]
        pieces = [slot_pieces(packed, seq, pair, cap) for seq, pair in work]
        grads = [
            stacked(grad_mixed[seq * cap : (seq + 1) * cap, pair * LANES : (pair + 1) * LANES])
            for seq, pair in work
        ]
        scores = [jnp.where(allowed[w[0]], nt(p[0], p[1]), -1e30) for w, p in zip(work, pieces)]
        grad_probs = [nt(g, p[2]) for g, p in zip(grads, pieces)]
        grown = [jnp.exp(v - jnp.max(v, axis=-1, keepdims=True)) for v in scores]
        probs = [v / jnp.sum(v, axis=-1, keepdims=True) for v in grown]
        lows = [
            (p * (g - jnp.sum(p * g, axis=-1, keepdims=True))).astype(BF16) for p, g in zip(probs, grad_probs)
        ]
        for (seq, pair), piece, grad_head, prob, low in zip(work, pieces, grads, probs, lows):
            at = slice(seq * cap, (seq + 1) * cap)
            cols = slice(pair * LANES, (pair + 1) * LANES)
            packed_o[0, at, cols] = (unstacked(nn(low, piece[1])) * FACTOR).astype(BF16)
            packed_o[1, at, cols] = tn(low, piece[0]).astype(BF16)
            packed_o[2, at, cols] = tn(prob.astype(BF16), grad_head).astype(BF16)
        send(packed_o, packed_out)
        copies[0].wait()
        grad_normed = sum(nt(packed_o[n], b_qkv[:, n * width : (n + 1) * width]) for n in range(3))
        back, gain_attn_sum = norm_back(grad_normed, chosen, mean_square_scale(chosen), gain_attn[...])
        chosen_o[...] = grad_rows + back + logit * router[...].reshape(1, -1)
        small_o[...] = jnp.zeros(small_o.shape, F32)
        small_o[0:1, :] = jnp.sum(logit * chosen, axis=0, keepdims=True)
        small_o[1:2, :] = gain_mlp_sum
        small_o[2:3, :] = gain_attn_sum
        for copy in sends:
            copy.wait()


def dense_gain(info, local, swapped, row):
    first = swapped.shape[0] - EXTRA + row
    far = sum(swapped[first + n : first + n + 1, :].astype(F32) for n in (0, 2, 4))
    return jnp.where(info[0] == 1, local[...], far)


def dense_in_body(
    info, x, near, away, picks, gain, w_local, w_far, middle_o, normed_o, packed_o, sel_o, b_qkv, sem
):
    step = pl.program_id(0)

    @pl.when(step == 0)
    def _():
        fetch(info, w_local, w_far, b_qkv, sem)

    rows, width = x.shape
    cap = near.shape[0]
    delta = jnp.where(info[0] == 0, near[...], away[:cap, :])
    place = step * rows + lax.broadcasted_iota(jnp.int32, (rows, cap), 0)
    hot = (picks[pl.ds(info[0], 1), :] == place).astype(BF16)
    middle = x[...].astype(F32) + nn(hot, delta)
    middle_o[...] = middle

    @pl.when(step == 0)
    def _():
        sel_o[...] = delta.astype(F32)

    sel_o[...] += tn(hot, x[...])
    normed = (middle * mean_square_scale(middle) * dense_gain(info, gain, away, 0)).astype(BF16)
    normed_o[...] = normed

    @pl.when(step == 0)
    def _():
        arrived(w_local, b_qkv, sem)

    for n in range(3):
        packed_o[n] = nn(normed, b_qkv[:, n * width : (n + 1) * width]).astype(BF16)


def attend_forward_body(info, packed, mixed_o, logsum_o):
    seq_len = packed.shape[1]
    tile = 2 * TILE
    queries = packed[0] * BF16(FACTOR)
    keys = packed[1]
    ones = jnp.ones((seq_len, LANES), BF16)
    values = [jnp.concatenate([head_only(packed[2], h), ones], axis=1) for h in range(2)]
    below = lax.broadcasted_iota(jnp.int32, (tile, tile), 1) <= lax.broadcasted_iota(jnp.int32, (tile, tile), 0)
    for first in range(0, seq_len, tile):
        upto = first + tile
        at = slice(first, upto)
        scores = []
        for head in range(2):
            score = nt(head_only(queries[at], head), keys[:upto])
            last = jnp.where(below, score[:, first:], -1e30)
            scores.append(jnp.concatenate([score[:, :first], last], axis=1) if first else last)
        tops = [jnp.max(score, axis=-1, keepdims=True) for score in scores]
        grown = [jnp.exp(score - top).astype(BF16) for score, top in zip(scores, tops)]
        outs = [nn(g, value[:upto]) for g, value in zip(grown, values)]
        mixed = sum(out[:, :LANES] * (1.0 / out[:, LANES:]) for out in outs)
        mixed_o[at, :] = mixed.astype(BF16)
        sums = [top + jnp.log(out[:, LANES:]) for top, out in zip(tops, outs)]
        turned = jnp.transpose(jnp.where(top_lanes(tile), sums[0], sums[1]))
        logsum_o[0, 0:1, at] = turned[0:1]
        logsum_o[0, 1:2, at] = turned[HEAD_DIM : HEAD_DIM + 1]


def attend_backward_body(info, packed, grad, mixed, logsum, picks, *refs):
    out, sel_o, grad_q = refs[-3:]
    seq_len = packed.shape[1]
    queries = packed[0] * BF16(FACTOR)
    queries = [head_only(queries, h) for h in range(2)]
    key_heads = [head_only(packed[1], h) for h in range(2)]
    grads = [head_only(grad[...], h) for h in range(2)]
    product = grad[...].astype(F32) * mixed[...].astype(F32)
    pick_row = lax.broadcasted_iota(jnp.int32, (8, LANES), 0)
    pick_lane = lax.broadcasted_iota(jnp.int32, (8, LANES), 1)
    pick = (pick_row == pick_lane // HEAD_DIM).astype(F32)
    inner = lax.dot_general(
        pick, product, (((1,), (1,)), ((), ())), precision=lax.Precision.HIGHEST, preferred_element_type=F32
    )
    above = lax.broadcasted_iota(jnp.int32, (TILE, TILE), 0) <= lax.broadcasted_iota(
        jnp.int32, (TILE, TILE), 1
    )
    for first in range(0, seq_len, TILE):
        kat = slice(first, first + TILE)
        keys = packed[1, kat, :]
        values = packed[2, kat, :]
        dks, dvs, dqs = [], [], []
        for head in range(2):
            query = queries[head][first:]
            grad_head = grads[head][first:]
            probs = jnp.exp(nt(keys, query) - logsum[0, head : head + 1, first:])
            edge = jnp.where(above, probs[:, :TILE], 0.0)
            probs = jnp.concatenate([edge, probs[:, TILE:]], axis=1) if first + TILE < seq_len else edge
            grad_probs = nt(values, grad_head)
            low = (probs * (grad_probs - inner[head : head + 1, first:])).astype(BF16)
            dvs.append(nn(probs.astype(BF16), grad_head))
            dks.append(nn(low, query))
            dqs.append(tn(low, key_heads[head][kat]))
        if first == 0:
            grad_q[...] = dqs[0] + dqs[1]
        else:
            grad_q[first:, :] += dqs[0] + dqs[1]
        out[1, kat, :] = (dks[0] + dks[1]).astype(BF16)
        out[2, kat, :] = (dvs[0] + dvs[1]).astype(BF16)
    out[0] = (grad_q[...] * FACTOR).astype(BF16)
    cap = picks.shape[1]
    place = lax.broadcasted_iota(jnp.int32, (seq_len, cap), 0)
    hot = (picks[pl.ds(info[0], 1), :] == place).astype(BF16)
    for n in range(3):
        sel_o[n] = tn(hot, out[n]).astype(BF16)


def feed_body(
    info, mixed, normed, middle, out_grad, gain_in, swapped, picks, middle_sel, wo_l, wo_f, wi_l, wi_f, wb_l, wb_f,
    pack_o, act_o, hidden_o, mid_o, carry_o, mixed_o, gain_o, sel_o,
    b_out, b_in, b_back, sems,
):
    step = pl.program_id(0)
    width = middle.shape[1]
    starts = range(0, b_in.shape[1], width)

    @pl.when(step == 0)
    def _():
        fetch(info, wo_l, wo_f, b_out, sems.at[0])
        for n, first in enumerate(starts):
            cols = pl.ds(first, width)
            fetch(info, wi_l.at[:, cols], wi_f.at[:, cols], b_in.at[:, cols], sems.at[1 + 2 * n])
            fetch(info, wb_l.at[cols], wb_f.at[cols], b_back.at[cols], sems.at[2 + 2 * n])
        gain_o[...] = jnp.zeros(gain_o.shape, F32)
        sel_o[0] = jnp.zeros(middle_sel.shape, F32)
        sel_o[1] = middle_sel[...]
        arrived(wo_l, b_out, sems.at[0])

    gain = dense_gain(info, gain_in, swapped, 1)
    pack_o[2] = mixed[...]
    pack_o[3] = normed[...]
    rows = middle[...] + nn(mixed[...], b_out[...])
    scale = mean_square_scale(rows)
    normed_mid = (rows * scale * gain).astype(BF16)
    mid_o[...] = normed_mid
    grad_ffn = out_grad[...]

    def hidden_block(first):
        cols = slice(first, first + width)
        act, slope = gelu_parts(nn(mid_o[...], b_in[:, cols]))
        act_o[:, cols] = act.astype(BF16)
        hidden_o[:, cols] = (nt(out_grad[...], b_back[cols, :]) * slope).astype(BF16)

    @pl.when(step == 0)
    def _():
        for n, first in enumerate(starts):
            cols = pl.ds(first, width)
            arrived(wi_l.at[:, cols], b_in.at[:, cols], sems.at[1 + 2 * n])
            arrived(wb_l.at[cols], b_back.at[cols], sems.at[2 + 2 * n])
            hidden_block(first)

    @pl.when(step > 0)
    def _():
        for first in starts:
            hidden_block(first)

    pack_o[0] = (rows + nn(act_o[...], b_back[...])).astype(BF16)
    grad_mid = nt(hidden_o[...], b_in[...])
    back, gain_sum = norm_back(grad_mid, rows, scale, gain)
    carry = grad_ffn.astype(F32) + back
    carry_o[...] = carry
    grad_attn = carry.astype(BF16)
    pack_o[1] = grad_attn
    mixed_o[...] = nt(grad_attn, b_out[...]).astype(BF16)
    gain_o[3:4, :] += gain_sum
    count, cap = carry.shape[0], middle_sel.shape[0]
    place = step * count + lax.broadcasted_iota(jnp.int32, (count, cap), 0)
    hot = (picks[pl.ds(info[0], 1), :] == place).astype(BF16)
    sel_o[0] += tn(hot, grad_attn) + tn(hot, (carry - grad_attn.astype(F32)).astype(BF16))


def dense_out_body(
    info, packed, carry, middle, gain_in, swapped, w_local, w_far, grad_o, gain_o, b_qkv, sem
):
    step = pl.program_id(0)

    @pl.when(step == 0)
    def _():
        fetch(info, w_local, w_far, b_qkv, sem)
        gain_o[...] = jnp.zeros(gain_o.shape, F32)
        arrived(w_local, b_qkv, sem)

    width = middle.shape[1]
    grad_normed = sum(nt(packed[n], b_qkv[:, n * width : (n + 1) * width]) for n in range(3))
    rows = middle[...]
    gain = dense_gain(info, gain_in, swapped, 0)
    back, gain_sum = norm_back(grad_normed, rows, mean_square_scale(rows), gain)
    gain_o[4:5, :] += gain_sum
    grad_o[...] = (carry[...] + back).astype(BF16)


def ends_body(info, result_block, grad, far_block, far_grad, grad_chosen, picks, out):
    seq = pl.program_id(0)
    step = pl.program_id(1)

    @pl.when(info[0] == 1)
    def _():
        out[...] = jnp.where(seq == 1, result_block[0], far_block[0])

    @pl.when(info[0] == 0)
    def _():
        base = jnp.where(seq == 0, grad[...], far_grad[...]).astype(F32)
        rows = out.shape[0]
        cap = grad_chosen.shape[0]
        place = step * rows + lax.broadcasted_iota(jnp.int32, (rows, cap), 0)
        hot = (picks[pl.ds(seq, 1), :] == place).astype(BF16)
        high = grad_chosen[...].astype(BF16)
        low = (grad_chosen[...] - high.astype(F32)).astype(BF16)
        out[...] = (base + (nn(hot, high) + nn(hot, low))).astype(BF16)


def feed_grad_body(
    info, mid, hidden, act, out_grad, out, mid_b, grad_b, hidden_b, act_b, ring_in, ring_back, in_sems, out_sems
):
    steps, rows, width = hidden_b.shape
    piece = width // PIECES

    def load(source, target, n):
        return pltpu.make_async_copy(source, target, in_sems.at[n])

    mine = pl.ds(pl.multiple_of(info[0] * rows, rows), rows)
    loads = [load(mid, mid_b, 0)]
    loads += [load(hidden.at[:, pl.ds(t * width, width)], hidden_b.at[t], 1 + t) for t in range(steps)]
    loads += [load(out_grad.at[mine], grad_b, 1 + steps)]
    loads += [load(act.at[:, pl.ds(t * width, width)], act_b.at[t], 2 + steps + t) for t in range(steps)]
    for copy in loads:
        copy.start()
    sent = []
    for n in range(2 * steps):
        t = n % steps
        if t == 0:
            loads[0 if n == 0 else 1 + steps].wait()
        loads[1 + t if n < steps else 2 + steps + t].wait()
        product = tn(mid_b[...], hidden_b[t]) if n < steps else tn(act_b[t], grad_b[...])
        ring = ring_in if n < steps else ring_back
        if t >= 2:
            sent[n - 2].wait()
        ring[n % 2] = product.astype(BF16).reshape(ring.shape[1:])
        target = out.at[1, :, :, pl.ds(t * piece, piece)] if n < steps else out.at[0, t]
        sent.append(pltpu.make_async_copy(ring.at[n % 2], target, out_sems.at[n // steps, n % 2]))
        sent[-1].start()
    for n in (steps - 2, steps - 1, 2 * steps - 2, 2 * steps - 1):
        sent[n].wait()


def origin(info, base, place):
    relative = 0
    for stage in range(STAGES):
        if place >> (STAGES - 1 - stage) & 1:
            relative = relative | (1 << info[base + stage])
    return info[1] ^ relative


def put_block(info, outs, product, slot, spot, ring, sems):
    piece = product.shape[0] // PIECES
    ring[spot] = product.astype(BF16)
    half = PIECES // 2
    sent = []
    for place in range(PIECES):
        rows = pl.ds(pl.multiple_of(origin(info, SIDE, place) * piece, piece), piece)
        target = outs[place // half].at[place % half, pl.ds(slot * piece, piece)]
        sent.append(pltpu.make_async_copy(ring.at[spot, rows], target, sems.at[slot, place]))
        sent[-1].start()
    return sent


def side_grad_body(
    info, normed0, packed0, mixed0, attn0,
    p_near, p_far, near, far,
    out_stay, out_go,
    n_buf, p_buf, m_buf, a_buf, ring, sems, out_sems,
):
    outs = (out_stay, out_go)

    def put_all(order, product):
        sent = []
        for n, slot in enumerate(order):
            value = product(slot)
            if n >= 2:
                for copy in sent[n - 2]:
                    copy.wait()
            sent.append(put_block(info, outs, value, slot, n % 2, ring, out_sems))
        for copies in sent[-2:]:
            for copy in copies:
                copy.wait()

    @pl.when(info[0] == 0)
    def _():
        put_all((3, 0, 1, 2), lambda n: tn(normed0[...], packed0[n]) if n < 3 else tn(mixed0[...], attn0[...]))

    @pl.when(info[0] == 1)
    def _():
        sources = [
            (source.at[which], target, n)
            for which, target in ((2, m_buf), (1, a_buf), (3, n_buf))
            for n, source in enumerate((near, far))
        ]
        copies = [
            pltpu.make_async_copy(source, target.at[n], sems.at[k])
            for k, (source, target, n) in enumerate(sources)
        ]
        blocks = [
            pltpu.make_async_copy(source.at[which], p_buf.at[n, which], sems.at[6 + 2 * which + n])
            for which in range(3)
            for n, source in enumerate((p_near, p_far))
        ]
        for copy in copies + blocks:
            copy.start()

        def product(n):
            if n == 3:
                for copy in copies[:4]:
                    copy.wait()
                return tn(m_buf[0], a_buf[0]) + tn(m_buf[1], a_buf[1])
            for copy in (copies[4:] if n == 0 else []) + blocks[2 * n : 2 * n + 2]:
                copy.wait()
            return tn(n_buf[0], p_buf[0, n]) + tn(n_buf[1], p_buf[1, n])

        put_all((3, 0, 1, 2), product)


def quad_grad_body(
    info, stay, from_x, from_y, from_xy, g_own, g_x, g_y, g_xy, w_back, go_o, stay_o,
    b_back, acts, slopes, mids, grads, hidden, held, sems, out_sems,
):
    @pl.when(info[0] == 0)
    def _():
        rows = g_own.shape[0]
        width = grads.shape[1]
        sub = acts.shape[0]
        steps = b_back.shape[0] // width
        piece = sub // QUAD
        count = mids.shape[0] // QUAD
        copies = []

        def load(source, target, n, k):
            copies.append(pltpu.make_async_copy(source, target, sems.at[n, k]))
            copies[-1].start()
            return copies[-1]

        first = [load(g, grads.at[pl.ds(n * rows, rows)], 0, n) for n, g in enumerate((g_own, g_x, g_y, g_xy))]
        parts = (stay, from_x, from_y, from_xy)
        blocks, lefts = [], []
        for t in range(steps):
            at = pl.ds(t * width, width)
            blocks.append([load(w_back.at[at], b_back.at[at], 1 + t, QUAD)])
            for n, source in enumerate(parts):
                here = pl.ds(sub + QUAD * count + t * width, width)
                blocks[t].append(load(source.at[here], slopes.at[at, pl.ds(n * rows, rows)], 1 + t, n))
        for n, source in enumerate(parts):
            to = pl.ds(n * rows, rows)
            lefts.append(load(source.at[pl.ds(0, sub)], acts.at[:, to], 1 + steps, n))
            lefts.append(load(source.at[pl.ds(sub, QUAD * count)], mids.at[:, to], 2 + steps, n))
        for copy in first:
            copy.wait()
        for t in range(steps):
            at = slice(t * width, (t + 1) * width)
            for copy in blocks[t]:
                copy.wait()
            hidden[at, :] = (nt(b_back[at, :], grads[...]) * slopes[at, :].astype(F32)).astype(BF16)
        for copy in lefts:
            copy.wait()
        layer = info[1] >> 2

        def put(z, rows_at, value):
            place = layer ^ z
            place = ((place & 1) << 1) | (place >> 1)

            held[place, rows_at, :] = value

        product = nn(acts[...], grads[...]).astype(BF16)
        for z in range(QUAD):
            put(z, slice(0, piece), product[z * piece : (z + 1) * piece, :])
        for t in range(steps):
            product = nt(mids[...], hidden[t * width : (t + 1) * width, :]).astype(BF16)
            for z in range(QUAD):
                put(z, slice(piece + t * count, piece + (t + 1) * count), product[z * count : (z + 1) * count, :])
        outs = [
            pltpu.make_async_copy(held.at[pl.ds(first, 2)], out, out_sems.at[n])
            for n, (first, out) in enumerate(((2, go_o), (0, stay_o)))
        ]
        for copy in outs:
            copy.start()
        for copy in outs:
            copy.wait()


def feed_grad(info, mid, hidden, act, out_grad):
    depth, width = mid.shape
    steps = hidden.shape[1] // width
    piece = width // PIECES
    return run(
        feed_grad_body,
        info,
        [(v, ANY) for v in (mid, hidden, act, out_grad)],
        [(shape((2, QUAD, QUAD, steps * piece, width), BF16), ANY)],
        (1,),
        [
            pltpu.VMEM((depth, width), BF16),
            pltpu.VMEM((depth, width), BF16),
            pltpu.VMEM((steps, depth, width), BF16),
            pltpu.VMEM((steps, depth, width), BF16),
            pltpu.VMEM((2, QUAD, QUAD, piece, width), BF16),
            pltpu.VMEM((2, QUAD, steps * piece, width), BF16),
            pltpu.SemaphoreType.DMA((2 + 2 * steps,)),
            pltpu.SemaphoreType.DMA((2, 2)),
        ],
        flops=4 * depth * steps * width * width,
        moved=4 * (depth + depth * steps + steps * width) * width,
    )[0]


def side_grad(info, routed, dense):
    _, depth, width = dense[0].shape
    half = PIECES // 2
    piece = width // PIECES

    dims = (half, 4 * piece, width)
    return run(
        side_grad_body,
        info,
        [(v, whole(v.shape)) for v in routed] + [(v, ANY) for v in dense],
        [(shape(dims, BF16), ANY)] * 2,
        (1,),
        [
            pltpu.VMEM((2, depth, width), BF16),
            pltpu.VMEM((2, 3, depth, width), BF16),
            pltpu.VMEM((2, depth, width), BF16),
            pltpu.VMEM((2, depth, width), BF16),
            pltpu.VMEM((2, width, width), BF16),
            pltpu.SemaphoreType.DMA((12,)),
            pltpu.SemaphoreType.DMA((4, PIECES)),
        ],
        flops=16 * depth * width * width,
        moved=24 * depth * width,
    )


def quad_grad(info, parts, grads, w_back):
    hidden, width = w_back.shape
    rows = grads[0].shape[0]
    sub = hidden // QUAD
    dims = (2, 2 * sub // QUAD, width)
    total = QUAD * rows
    return run(
        quad_grad_body,
        info,
        [(v, ANY) for v in parts + grads + [w_back]],
        [(shape(dims, BF16), ANY)] * 2,
        (1,),
        [
            pltpu.VMEM((hidden, width), BF16),
            pltpu.VMEM((sub, total), BF16),
            pltpu.VMEM((hidden, total), BF16),
            pltpu.VMEM((parts[0].shape[0] - sub - hidden, total), BF16),
            pltpu.VMEM((total, width), BF16),
            pltpu.VMEM((hidden, total), BF16),
            pltpu.VMEM((QUAD, *dims[1:]), BF16),
            pltpu.SemaphoreType.DMA((3 + hidden // width, 1 + QUAD)),
            pltpu.SemaphoreType.DMA((2,)),
        ],
        flops=8 * sub * total * width,
        moved=10 * sub * total,
    )


def to_section(value, source):
    return lax.ppermute(value, "section", [(source, 1 - source)])


def swap_section(value):
    return lax.ppermute(value, "section", [(0, 1), (1, 0)])


def after(value, *earlier):
    return lax.optimization_barrier((value, *earlier))[0]


def added_up(parts):
    total = parts[0].astype(F32)
    for part in parts[1:]:
        total = total + part.astype(F32)
    return total


def cross(orders, value, stage):
    count = lax.axis_size("dp")
    low = count // PIECES
    pairs = []
    for section, order in enumerate(orders):
        base = section * count
        flip = low << order[stage]
        pairs += [(base + n, base + (n ^ flip)) for n in range(count)]
    return lax.ppermute(value, ("section", "dp"), pairs)


def cross_first(value, *axes):
    count = lax.axis_size("dp")
    flip = sum((count // PIECES) << axis for axis in axes)
    return lax.ppermute(value, ("section", "dp"), [(n, n ^ flip) for n in range(count)])


def scatter_layers(value):
    stride = QUAD * (lax.axis_size("dp") // PIECES)
    groups = [[base + n * stride for n in range(QUAD)] for base in range(stride)]
    return lax.psum_scatter(value, "dp", scatter_dimension=0, axis_index_groups=groups, tiled=True)


class Exchange:
    def __init__(self, stay, go, swap, stages):
        self.stay, self.go, self.swap = stay, go, swap
        self.stages, self.stage, self.flying = stages, 0, None

    def start(self, info):
        if self.stage:
            half = self.stay[0].shape[0] // 2
            self.go = [part[half:] for part in self.stay]
            self.stay = [part[:half] for part in self.stay]
        send = added_up(self.go).astype(BF16) if len(self.go) > 1 else self.go[0]
        info, send = lax.optimization_barrier((info, send))
        self.flying = self.swap(send, self.stage)
        self.stage += 1
        return info

    def total(self):
        assert self.stage == self.stages
        return added_up(self.stay)[0]


def settle(info, *values):
    arrays = [value.flying if isinstance(value, Exchange) else value for value in values]
    info, *arrays = lax.optimization_barrier((info, *arrays))
    plain = []
    for value, array in zip(values, arrays):
        if isinstance(value, Exchange):
            value.stay = value.stay + [array]
        else:
            plain.append(array)
    return (info, *plain)


def share_out(piece):
    count = lax.axis_size("dp")
    low = count // PIECES
    if low > 1:
        rows, cols = piece.shape
        place = lax.axis_index("dp") % low
        parts = jnp.take(piece.reshape(low, rows // low, cols), jnp.arange(low) ^ place, axis=0)
        while parts.shape[0] > 1:
            half = parts.shape[0] // 2
            far = lax.ppermute(parts[half:], "dp", [(n, n ^ half) for n in range(count)])
            parts = parts[:half] + far
        piece = parts[0]
    return piece[None]


def across(value, flip):
    return lax.ppermute(value, "dp", [(n, n ^ flip) for n in range(lax.axis_size("dp"))])


X, Y, Z, ZZ = 0, 1, 2, 3
ORDERS = ((X, Y, Z, ZZ), (Y, X, Z, ZZ))
SIDE = 2


def shards(inputs, out_grad, picks, valid, router, gain_attn, w_qkv, w_out, gain_mlp, w_in, w_back):
    w_qkv, w_out, w_in, w_back = w_qkv[0], w_out[0], w_in[0], w_back[0]
    seqs, cap = picks.shape
    seq_len = inputs.shape[0] // seqs
    width = inputs.shape[1]
    hidden = w_in.shape[1]
    rows = seqs * cap
    tiles = seq_len // TILE
    section = lax.axis_index("section")
    spot = lax.axis_index("dp") // (lax.axis_size("dp") // PIECES)
    first = section == 0

    table = [(mine, 0) + ORDERS[mine] for mine in (0, 1)]
    facts = jnp.where(first, jnp.array(table[0]), jnp.array(table[1]))
    info = jnp.where(jnp.arange(len(table[0])) == 1, spot, facts).astype(jnp.int32)

    far_qkv = to_section(w_qkv, 1)
    far_out = to_section(w_out, 1)
    far_in = to_section(w_in, 1)

    weight_bufs = [pltpu.VMEM(w.shape, BF16) for w in (w_qkv, w_out, w_in, w_back)]
    weight_bufs.append(pltpu.SemaphoreType.DMA((4,)))
    weight_ins = [(w_qkv, ANY), (w_out, ANY), (w_in, ANY), (w_back, ANY)]

    def full(array):
        return (array, whole(array.shape))

    def made(dims, dtype):
        return (shape(dims, dtype), whole(dims))

    routed_flops = 2 * rows * (4 * width * width + 2 * width * hidden)
    weight_bytes = 2 * (4 * width * width + 2 * width * hidden)
    sub = hidden // QUAD
    kept = [
        shape((rows, width), BF16),
        shape((rows, width), BF16),
        shape((rows, 3 * width), BF16),
        shape((rows, width), BF16),
        shape((rows, width), F32),
        shape((rows, hidden), BF16),
        shape((rows, width), F32),
    ]
    (
        gate0, open0, near, away, chosen, normed0, packed0, mixed0, rows0, slope0, branch0,
        stay0, over_x, over_y, over_xy,
    ) = run(
        routed_forward_body,
        info,
        [(inputs, ANY)] + [full(v) for v in (picks, valid, gain_attn, gain_mlp, router)] + weight_ins,
        [
            made((rows, LANES), F32),
            made((rows, LANES), F32),
            made((cap, width), BF16),
            made((cap + EXTRA, width), BF16),
        ]
        + [(v, ANY) for v in kept]
        + [(shape((sub + width // QUAD + hidden, rows), BF16), ANY)] * QUAD,
        (1,),
        [pltpu.VMEM(v.shape, v.dtype) for v in kept]
        + [pltpu.VMEM(inputs.shape, BF16)]
        + weight_bufs[:4]
        + [pltpu.VMEM((rows, hidden), BF16), pltpu.VMEM((QUAD, sub + width // QUAD, rows), BF16), pltpu.VMEM((hidden, rows), BF16)]
        + weight_bufs[4:]
        + [pltpu.SemaphoreType.DMA((seqs,)), pltpu.SemaphoreType.DMA((len(kept) + 2 * QUAD,))],
        flops=routed_flops,
        moved=weight_bytes,
    )
    info, far_qkv, far_out, far_in, near, away, over_x, over_y, over_xy, w_back_now = settle(
        info, far_qkv, far_out, far_in, near, away, over_x, over_y, over_xy, w_back
    )
    away = swap_section(away)

    def row_tile(dims):
        return pl.BlockSpec(dims, lambda i, info_ref: (i, 0))

    def seq_tile(tile=TILE):
        return pl.BlockSpec((tile, width), lambda i, info_ref: (info_ref[0] * (seq_len // tile) + i, 0))

    def tiled(cols, dtype, tile=TILE):
        return (shape((seq_len, cols), dtype), row_tile((tile, cols)))

    three_tile = pl.BlockSpec((3, WIDE, width), lambda i, info_ref: (0, i, 0))
    three_low = pl.BlockSpec((3, TILE, width), lambda i, info_ref: (0, i, 0))
    three = shape((3, seq_len, width), BF16)

    middle, normed1, packed1, middle_sel = run(
        dense_in_body,
        info,
        [
            (inputs, seq_tile(WIDE)),
            full(near),
            full(away),
            full(picks),
            full(gain_attn),
            (w_qkv, ANY),
            (far_qkv, ANY),
        ],
        [tiled(width, F32, WIDE), tiled(width, BF16, WIDE), (three, three_tile), made((cap, width), F32)],
        (seq_len // WIDE,),
        [pltpu.VMEM(w_qkv.shape, BF16), pltpu.SemaphoreType.DMA],
        flops=6 * seq_len * width * width,
        moved=seq_len * width * 12 + 6 * width * width,
    )

    info, packed1, over_x, over_y, over_xy, w_back_now = settle(
        info, packed1, over_x, over_y, over_xy, w_back_now
    )
    far_back = to_section(w_back_now, 1)
    from_x = cross_first(over_x, X)
    from_y = cross_first(over_y, Y)
    from_xy = cross_first(over_xy, X, Y)

    pair_spec = pl.BlockSpec((3, seq_len, LANES), lambda h, info_ref: (0, 0, h))
    column_spec = pl.BlockSpec((seq_len, LANES), lambda h, info_ref: (0, h))
    logsum_spec = pl.BlockSpec((1, 8, seq_len), lambda h, info_ref: (h, 0, 0))
    attend_flops = 2 * HEADS * seq_len * seq_len * TILE
    mixed1, logsum1 = run(
        attend_forward_body,
        info,
        [(packed1, pair_spec)],
        [
            (shape((seq_len, width), BF16), column_spec),
            (shape((PAIRS, 8, seq_len), F32), logsum_spec),
        ],
        (PAIRS,),
        flops=attend_flops,
        moved=8 * seq_len * width,
    )

    info, mixed1, far_back = settle(info, mixed1, far_back)
    pack1, act1, hidden1, mid1, carry, grad_mixed1, gain_mlp_sum, carried = run(
        feed_body,
        info,
        [
            (mixed1, row_tile((TILE, width))),
            (normed1, row_tile((TILE, width))),
            (middle, row_tile((TILE, width))),
            (out_grad, seq_tile()),
            full(gain_mlp),
            full(away),
            full(picks),
            full(middle_sel),
            (w_out, ANY),
            (far_out, ANY),
            (w_in, ANY),
            (far_in, ANY),
            (w_back, ANY),
            (far_back, ANY),
        ],
        [
            (shape((4, seq_len, width), BF16), pl.BlockSpec((4, TILE, width), lambda i, info_ref: (0, i, 0))),
            tiled(hidden, BF16),
            tiled(hidden, BF16),
            tiled(width, BF16),
            tiled(width, F32),
            tiled(width, BF16),
            made((8, width), F32),
            made((2, cap, width), F32),
        ],
        (tiles,),
        [
            pltpu.VMEM(w_out.shape, BF16),
            pltpu.VMEM(w_in.shape, BF16),
            pltpu.VMEM(w_back.shape, BF16),
            pltpu.SemaphoreType.DMA((1 + 2 * hidden // width,)),
        ],
        flops=2 * seq_len * width * (2 * width + 4 * hidden),
        moved=seq_len * (20 * width + 4 * hidden) + 2 * width * (width + 2 * hidden),
    )
    info, mid1, pack1, carried, from_x, from_y, from_xy = settle(info, mid1, pack1, carried, from_x, from_y, from_xy)
    feed = feed_grad(info, mid1, hidden1, act1, out_grad)
    info, feed = settle(info, feed)
    feed = lax.psum_scatter(feed.reshape(-1, width), "section", scatter_dimension=0, tiled=True)

    def attend_backward(info, start, held):
        def third(rows):
            return pl.BlockSpec((3, rows, LANES), lambda h, info_ref: (0, 0, start + h))

        column = pl.BlockSpec((seq_len, LANES), lambda h, info_ref: (0, start + h))
        logsums = pl.BlockSpec((1, 8, seq_len), lambda h, info_ref: (start + h, 0, 0))
        return run(
            attend_backward_body,
            info,
            [(packed1, third(seq_len)), (grad_mixed1, column), (mixed1, column), (logsum1, logsums), full(picks)]
            + [(v, ANY) for v in held],
            [(three, third(seq_len)), (shape((3, cap, width), BF16), third(cap))],
            (PAIRS // 2,),
            [pltpu.VMEM((seq_len, LANES), F32)],
            flops=5 * attend_flops // 4,
            moved=8 * seq_len * width,
            aliases={6: 0, 7: 1} if held else {},
        )

    held = attend_backward(info, 0, [])
    info, pack1, carried, *held = settle(info, pack1, carried, *held)
    far_pack = to_section(pack1, 0)
    far_carried = to_section(carried, 1)
    info, feed = settle(info, feed)
    feed = scatter_layers(feed)
    packed_grad1, packed_sel = attend_backward(info, PAIRS // 2, held)
    info, packed_grad1, packed_sel, far_pack, far_carried = settle(
        info, packed_grad1, packed_sel, far_pack, far_carried
    )
    far_packed_sel = to_section(packed_sel, 1)
    info, far_packed_sel, packed_grad1 = settle(info, far_packed_sel, packed_grad1)
    far_packed = to_section(packed_grad1, 0)

    made_back = [shape((rows, width), BF16), shape((rows, width), BF16), shape((3, rows, width), BF16)]
    grad_chosen, small0, g_own, attn0, packed_grad0 = run(
        routed_backward_body,
        info,
        [
            full(v)
            for v in (
                packed_sel, far_packed_sel, carried, far_carried,
                chosen, branch0, gate0, valid, gain_attn, gain_mlp, router, away,
            )
        ]
        + [(v, ANY) for v in (packed0, rows0, slope0, far_qkv)]
        + weight_ins,
        [made((rows, width), F32), made((8, width), F32)] + [(v, ANY) for v in made_back],
        (1,),
        weight_bufs[:4]
        + [pltpu.VMEM((rows, hidden), BF16)]
        + [pltpu.VMEM(v.shape, v.dtype) for v in (packed0, rows0, slope0, *made_back)]
        + [pltpu.SemaphoreType.DMA((5,)), pltpu.SemaphoreType.DMA((3,)), pltpu.SemaphoreType.DMA((3,))],
        flops=routed_flops,
        moved=weight_bytes,
    )
    info, small0, packed_grad0, far_packed, g_own = settle(info, small0, packed_grad0, far_packed, g_own)
    g_x = cross_first(g_own, X)
    g_y = cross_first(g_own, Y)
    g_xy = cross_first(g_own, X, Y)

    side_stay, side_go = side_grad(
        info,
        [normed0, packed_grad0, mixed0, attn0],
        [packed_grad1, far_packed, pack1, far_pack],
    )
    info, side_go, g_x, g_y, g_xy = settle(info, side_go, g_x, g_y, g_xy)
    side = Exchange([side_stay], [side_go], functools.partial(cross, ORDERS), STAGES)
    info = side.start(info)

    grad_middle, gain_attn_sum = run(
        dense_out_body,
        info,
        [
            (packed_grad1, three_low),
            (carry, row_tile((TILE, width))),
            (middle, row_tile((TILE, width))),
            full(gain_attn),
            full(away),
            (w_qkv, ANY),
            (far_qkv, ANY),
        ],
        [tiled(width, BF16), made((8, width), F32)],
        (tiles,),
        [pltpu.VMEM(w_qkv.shape, BF16), pltpu.SemaphoreType.DMA],
        flops=6 * seq_len * width * width,
        moved=seq_len * width * 16 + 6 * width * width,
    )
    info, grad_middle, gain_attn_sum = settle(info, grad_middle, gain_attn_sum)
    far_grad = to_section(grad_middle, 1)
    small = jnp.where(first, small0, 0.0) + gain_mlp_sum + gain_attn_sum
    small_far = across(small, 8)
    quad_go, quad_stay = quad_grad(
        info, [stay0, from_x, from_y, from_xy],
        [g_own, g_x, g_y, g_xy], w_back,
    )
    info, quad_go, far_grad, small_far, feed = settle(info, quad_go, far_grad, small_far, feed, side)
    info = side.start(info)
    small = after(small + small_far, info)
    small_far = across(small, 2)
    quad = Exchange([quad_stay], [quad_go], lambda value, stage: cross_first(value, (Z, ZZ)[stage]), 2)
    info = quad.start(info)
    far_places = jnp.where(first, jnp.array([0, 2, 1, 3]), jnp.array([0, 1, 2, 3])) ^ (spot & 3)
    feed = jnp.take(feed.reshape(QUAD, -1, width), far_places, axis=0)
    feed = Exchange([feed[:2]], [feed[2:]], functools.partial(cross, ORDERS), 2)
    info = feed.start(info)

    def end_spec(core, seq, paired):
        def at(s, i, info_ref):
            step = jnp.where((info_ref[0] == core) & (s == seq), i, 0)
            return (0, step, 0) if paired else (step, 0)

        return pl.BlockSpec((1, WIDE, width) if paired else (WIDE, width), at)

    ends = run(
        ends_body,
        info,
        [
            (pack1, end_spec(1, 1, True)),
            (grad_middle, end_spec(0, 0, False)),
            (far_pack, end_spec(1, 0, True)),
            (far_grad, end_spec(0, 1, False)),
            (grad_chosen, pl.BlockSpec((cap, width), lambda s, i, info_ref: (s, 0))),
            (picks, pl.BlockSpec((seqs, cap), lambda s, i, info_ref: (0, 0))),
        ],
        [
            (
                shape((seqs * seq_len, width), BF16),
                pl.BlockSpec((WIDE, width), lambda s, i, info_ref: (s * (seq_len // WIDE) + i, 0)),
            )
        ],
        (seqs, seq_len // WIDE),
        flops=4 * seqs * seq_len * cap * width,
        moved=8 * seqs * seq_len * width,
    )[0]

    info, ends = settle(info, ends, side)
    info = side.start(info)
    info, = settle(info, quad)
    info = quad.start(info)
    info, small_far = settle(info, small_far, feed)
    small = after(small + small_far, info)
    small_far = across(small, 4)
    info = feed.start(info)
    info, small_far = settle(info, small_far, side)
    info = side.start(info)
    small = after(small + small_far, info)
    small_far = across(small, 1)
    info, = settle(info, feed)
    feed1 = feed.total()
    back1 = to_section(feed1.astype(BF16), 0).astype(F32)
    info, small_far, back1 = settle(info, small_far, back1)
    small = small + small_far
    small_far = swap_section(small)
    info, small_far = settle(info, small_far, quad)

    def gain_share(routed_row, dense_row):
        row = jnp.where(first, small[routed_row], small[dense_row])
        return lax.dynamic_slice_in_dim(row, lax.axis_index("dp") * share, share)[None]

    piece = width // PIECES
    small = small + small_far
    flip = PIECES
    while flip < lax.axis_size("dp"):
        small = small + across(small, flip)
        flip *= 2
    share = width // lax.axis_size("dp")
    quad_sum = quad.total()
    back0, in0 = quad_sum[: hidden // PIECES], quad_sum[hidden // PIECES :]
    in0 = in0.reshape(QUAD, piece, width).transpose(1, 0, 2).reshape(piece, hidden)

    in1 = feed1.reshape(QUAD, piece, width).transpose(1, 0, 2).reshape(piece, hidden)
    w_in_out = share_out(jnp.where(first, in0, in1))
    w_back_out = share_out(jnp.where(first, back0, back1))
    gain_attn_out, gain_mlp_out = gain_share(2, 4), gain_share(1, 3)
    info, w_in_out, w_back_out, gain_attn_out, gain_mlp_out, small = settle(
        info, w_in_out, w_back_out, gain_attn_out, gain_mlp_out, small, side
    )
    attend_sum = side.total()
    return (
        ends[None],
        small[0],
        gain_attn_out,
        share_out(jnp.concatenate([attend_sum[n : n + piece] for n in range(0, 3 * piece, piece)], axis=1)),
        share_out(attend_sum[3 * piece :]),
        gain_mlp_out,
        w_in_out,
        w_back_out,
    )


def solution(mesh):
    placed = (
        P("dp", None),
        P("dp", None),
        P("dp", None),
        P("dp", None),
        P(),
        P("section", None),
        P("section", None, None),
        P("section", None, None),
        P("section", None),
        P("section", None, None),
        P("section", None, None),
    )
    return jax.shard_map(
        shards,
        mesh=mesh,
        in_specs=placed,
        out_specs=(
            P("section", "dp", None),
            P(),
            P("section", "dp"),
            P("section", "dp", None),
            P("section", "dp", None),
            P("section", "dp"),
            P("section", "dp", None),
            P("section", "dp", None),
        ),
        check_vma=False,
    )
```

```python
import functools

import jax
import jax.numpy as jnp
from jax import lax
from jax.experimental import pallas as pl
from jax.experimental.pallas import tpu as pltpu
from jax.sharding import PartitionSpec as P

HEADS = 12
HEAD_DIM = 64
LANES = 128
PAIRS = HEADS * HEAD_DIM // LANES
EPS = 1e-06
FACTOR = HEAD_DIM ** (-0.5)
PIECES = 16
STAGES = 4
QUAD = 4
EXTRA = 16
TILE = 256
WIDE = 512
VMEM_BYTES = 56 * 1024 * 1024
BF16 = jnp.bfloat16
F32 = jnp.float32


def nn(a, b):
    return lax.dot_general(a, b, (((1,), (0,)), ((), ())), preferred_element_type=F32)


def nt(a, b):
    return lax.dot_general(a, b, (((1,), (1,)), ((), ())), preferred_element_type=F32)


def tn(a, b):
    return lax.dot_general(a, b, (((0,), (0,)), ((), ())), preferred_element_type=F32)


def shape(dims, dtype):
    return jax.ShapeDtypeStruct(dims, dtype)


def whole(dims):
    zeros = (0,) * len(dims)
    return pl.BlockSpec(dims, lambda *_: zeros)


ANY = pl.BlockSpec(memory_space=pl.ANY)


def run(body, info, ins, outs, grid, scratch=(), flops=0, moved=0, aliases=()):
    arrays, in_specs = zip(*ins)
    shapes, out_specs = zip(*outs)
    return pl.pallas_call(
        body,
        out_shape=shapes,
        input_output_aliases=dict(aliases),
        grid_spec=pltpu.PrefetchScalarGridSpec(
            num_scalar_prefetch=1,
            grid=grid,
            in_specs=in_specs,
            out_specs=out_specs,
            scratch_shapes=scratch,
        ),
        compiler_params=pltpu.CompilerParams(
            vmem_limit_bytes=VMEM_BYTES, dimension_semantics=("arbitrary",) * len(grid)
        ),
        cost_estimate=pl.CostEstimate(flops=flops // 4, bytes_accessed=moved // 4, transcendentals=0),
    )(info, *arrays)


def top_lanes(rows):
    return lax.broadcasted_iota(jnp.int32, (rows, LANES), 1) < HEAD_DIM


def lane_head(rows, which):
    lane = lax.broadcasted_iota(jnp.int32, (rows, LANES), 1)
    return (lane < HEAD_DIM) if which == 0 else (lane >= HEAD_DIM)


def head_only(value, which):
    return jnp.where(lane_head(value.shape[0], which), value, jnp.zeros_like(value))


def mean_square_scale(rows):
    return lax.rsqrt(jnp.mean(rows * rows, axis=-1, keepdims=True) + EPS)


def norm_back(grad, rows, scale, gain):
    hat = rows * scale
    scaled = grad * gain
    back = scale * (scaled - hat * jnp.mean(scaled * hat, axis=-1, keepdims=True))
    return back, jnp.sum(grad * hat, axis=0, keepdims=True)


def gelu_parts(pre):
    root = 0.7978845608028654
    square = pre * pre
    bent = jnp.tanh(root * pre * (1.0 + 0.044715 * square))
    half = 0.5 * (1.0 + bent)
    slope = half + 0.5 * pre * (1.0 - bent * bent) * (root * (1.0 + 0.134145 * square))
    return pre * half, slope


def fetch(info, local, remote, buf, sem):
    @pl.when(info[0] == 1)
    def _():
        pltpu.make_async_copy(local, buf, sem).start()

    @pl.when(info[0] == 0)
    def _():
        pltpu.make_async_copy(remote, buf, sem).start()


def arrived(source, buf, sem):
    pltpu.make_async_copy(source, buf, sem).wait()


def stacked(value):
    return jnp.concatenate([head_only(value, h) for h in range(2)], axis=0)


def unstacked(value):
    half = value.shape[0] // 2
    return jnp.where(top_lanes(half), value[:half], value[half:])


def slot_pieces(packed, seq, pair, cap):
    rows = slice(seq * cap, (seq + 1) * cap)
    width = HEADS * HEAD_DIM
    first = pair * LANES
    queries = stacked(packed[rows, first : first + LANES] * BF16(FACTOR))
    keys = packed[rows, width + first : width + first + LANES]
    values = packed[rows, 2 * width + first : 2 * width + first + LANES]
    return queries, keys, values


def slot_rule(valid_row, cap):
    query = lax.broadcasted_iota(jnp.int32, (cap, cap), 0)
    key = lax.broadcasted_iota(jnp.int32, (cap, cap), 1)
    rule = (key <= query) & ((valid_row > 0) | (key == query))
    return jnp.concatenate([rule, rule], axis=0)


def column_of(row):
    return jnp.transpose(jnp.broadcast_to(row, (row.shape[1], row.shape[1])))


def slot_mask(valid):
    seqs = valid.shape[0]
    return jnp.concatenate([column_of(valid[s : s + 1, :].astype(F32)) for s in range(seqs)], axis=0)[:, 0:1]


def weight_copies(sources, bufs, sems):
    return [pltpu.make_async_copy(a, b, sems.at[n]) for n, (a, b) in enumerate(zip(sources, bufs))]


def routed_forward_body(
    info, x, picks, valid, gain_attn, gain_mlp, router, w_qkv, w_out, w_in, w_back,
    gate_o, open_o, near_o, away_o, chosen_h, normed_h, packed_h, mixed_h, rows_h, slope_h, branch_h,
    stay_o, over_x_o, over_y_o, over_xy_o,
    chosen_o, normed_o, packed_o, mixed_o, rows_o, slope_o, branch_o,
    b_x, b_qkv, b_out, b_in, b_back, act_b, shares, slope_t, sems, x_sems, out_sems,
):
    @pl.when(info[0] == 1)
    def _():
        rest = jnp.concatenate([gain_attn[...], gain_mlp[...]], axis=0)
        count = away_o.shape[0] - EXTRA
        for part in range(3):
            rounded = rest.astype(BF16)
            away_o[count + 2 * part : count + 2 * part + 2, :] = rounded
            rest = rest - rounded.astype(F32)

    @pl.when(info[0] == 0)
    def _():
        copies = weight_copies((w_qkv, w_out, w_in, w_back), (b_qkv, b_out, b_in, b_back), sems)
        seqs, cap = valid.shape
        seq_len = x.shape[0] // seqs
        loads = []
        for seq in range(seqs):
            at = pl.ds(seq * seq_len, seq_len)
            loads.append(pltpu.make_async_copy(x.at[at], b_x.at[at], x_sems.at[seq]))
        for copy in loads + copies:
            copy.start()
        sends = []

        def send(source, target):
            sends.append(pltpu.make_async_copy(source, target, out_sems.at[len(sends)]))
            sends[-1].start()

        parts = []
        for seq in range(seqs):
            place = lax.broadcasted_iota(jnp.int32, (seq_len, cap), 0)
            hot = (picks[seq : seq + 1, :] == place).astype(BF16)
            loads[seq].wait()
            parts.append(tn(hot, b_x[seq * seq_len : (seq + 1) * seq_len, :]))
        chosen = jnp.concatenate(parts, axis=0)
        chosen_o[...] = chosen.astype(BF16)
        send(chosen_o, chosen_h)
        gates = jax.nn.sigmoid(jnp.sum(chosen * router[...].reshape(1, -1), axis=-1, keepdims=True))
        gate_o[...] = jnp.broadcast_to(gates, gate_o.shape)
        normed = (chosen * mean_square_scale(chosen) * gain_attn[...]).astype(BF16)
        normed_o[...] = normed
        send(normed_o, normed_h)
        copies[0].wait()
        packed_o[...] = nn(normed, b_qkv[...]).astype(BF16)
        send(packed_o, packed_h)
        work = [(seq, pair) for seq in range(seqs) for pair in range(PAIRS)]
        allowed = [slot_rule(valid[seq : seq + 1, :], cap) for seq in range(seqs)]
        pieces = [slot_pieces(packed_o, seq, pair, cap) for seq, pair in work]
        scores = [jnp.where(allowed[w[0]], nt(p[0], p[1]), -1e30) for w, p in zip(work, pieces)]
        grown = [jnp.exp(v - jnp.max(v, axis=-1, keepdims=True)).astype(BF16) for v in scores]
        ones = jnp.ones((cap, LANES), BF16)
        outs = [nn(g, jnp.concatenate([p[2], ones], axis=1)) for g, p in zip(grown, pieces)]
        outs = [unstacked(o[:, :LANES] / o[:, LANES:]).astype(BF16) for o in outs]
        mixed = jnp.concatenate(
            [jnp.concatenate(outs[s * PAIRS : (s + 1) * PAIRS], axis=1) for s in range(seqs)], axis=0
        )
        mixed_o[...] = mixed
        send(mixed_o, mixed_h)
        copies[1].wait()
        attn_out = nn(mixed, b_out[...])
        rows = chosen + attn_out
        rows_o[...] = rows
        send(rows_o, rows_h)
        normed_mid = (rows * mean_square_scale(rows) * gain_mlp[...]).astype(BF16)
        member = info[1] & 3
        piece = b_in.shape[1] // PIECES
        mid_turned = jnp.transpose(normed_mid)
        count = mid_turned.shape[0] // PIECES
        sub = piece * QUAD
        for dest in range(PIECES):
            at = sub + dest // QUAD * count
            shares[(dest % QUAD) ^ member, at : at + count, :] = mid_turned[dest * count : (dest + 1) * count, :]
        copies[2].wait()
        step = 768
        for first in range(0, b_in.shape[1], step):
            cols = slice(first, first + step)
            act, slope = gelu_parts(nn(normed_mid, b_in[:, cols]))
            act = act.astype(BF16)
            slope = slope.astype(BF16)
            act_b[:, cols] = act
            slope_o[:, cols] = slope
            chunk = first // step
            slope_t[first : first + step, :] = jnp.transpose(slope)
            turned = jnp.transpose(act)
            for owner in range(QUAD):
                shares[owner ^ member, chunk * piece : (chunk + 1) * piece, :] = turned[
                    owner * piece : (owner + 1) * piece, :
                ]
        send(slope_o, slope_h)
        for n, out in enumerate((stay_o, over_x_o, over_y_o, over_xy_o)):
            send(shares.at[n], out.at[pl.ds(0, shares.shape[1])])
            send(slope_t, out.at[pl.ds(shares.shape[1], slope_t.shape[0])])
        copies[3].wait()
        branch = attn_out + nn(act_b[...], b_back[...])
        branch_o[...] = branch
        send(branch_o, branch_h)
        opened = gates * slot_mask(valid)
        open_o[...] = jnp.broadcast_to(opened, open_o.shape)
        delta = (opened * branch).astype(BF16)
        near_o[...] = delta[:cap]
        away_o[:cap, :] = delta[cap:]
        for copy in sends:
            copy.wait()


def routed_backward_body(
    info, p_near, p_far, r_near, r_far, chosen_i, branch, gate, valid, gain_attn, gain_mlp, router, swapped,
    packed_h, rows_h, slope_h, w_next, w_qkv, w_out, w_in, w_back,
    chosen_o, small_o, ffn_h, attn_h, packed_out,
    b_qkv, b_out, b_in, b_back, hidden_b, packed, rows_i, slope, ffn_o, attn_o, packed_o, sems, in_sems, out_sems,
):
    @pl.when(info[0] == 0)
    def _():
        copies = weight_copies((w_qkv, w_out, w_in, w_back), (b_qkv, b_out, b_in, b_back), sems)
        upper = pltpu.make_async_copy(w_next, b_qkv, sems.at[4])
        upper.start()
        loads = [
            pltpu.make_async_copy(source, target, in_sems.at[n])
            for n, (source, target) in enumerate(((slope_h, slope), (rows_h, rows_i), (packed_h, packed)))
        ]
        for copy in (copies[3], loads[0], copies[2], loads[1], copies[1], loads[2]):
            copy.start()
        sends = []

        def send(source, target):
            sends.append(pltpu.make_async_copy(source, target, out_sems.at[len(sends)]))
            sends[-1].start()

        seqs, cap = valid.shape
        chosen = chosen_i[...].astype(F32)
        width = chosen.shape[1]
        upper.wait()
        upper_gain = dense_gain(info, gain_attn, swapped, 0)
        grad_sel = []
        for dense, carried in ((p_near, r_near), (p_far, r_far)):
            grad_normed = sum(nt(dense[n], b_qkv[:, n * width : (n + 1) * width]) for n in range(3))
            middle = carried[1]
            back, _ = norm_back(grad_normed, middle, mean_square_scale(middle), upper_gain)
            grad_sel.append((carried[0] + back).astype(BF16).astype(F32))
        grad_sel = jnp.concatenate(grad_sel, axis=0)
        copies[0].start()
        gates = gate[:, 0:1]
        mask = slot_mask(valid)
        logit = jnp.sum(grad_sel * branch[...], axis=-1, keepdims=True) * mask * gates * (1.0 - gates)
        grad = grad_sel * (gates * mask)
        grad_ffn = grad.astype(BF16)
        ffn_o[...] = grad_ffn
        send(ffn_o, ffn_h)
        copies[3].wait()
        loads[0].wait()
        step = 768
        for first in range(0, b_in.shape[1], step):
            cols = slice(first, first + step)
            hidden = (nt(grad_ffn, b_back[cols, :]) * slope[:, cols].astype(F32)).astype(BF16)
            hidden_b[:, cols] = hidden
        copies[2].wait()
        grad_mid = nt(hidden_b[...], b_in[...])
        loads[1].wait()
        rows = rows_i[...]
        grad_rows, gain_mlp_sum = norm_back(grad_mid, rows, mean_square_scale(rows), gain_mlp[...])
        grad_attn = (grad + grad_rows).astype(BF16)
        attn_o[...] = grad_attn
        send(attn_o, attn_h)
        copies[1].wait()
        grad_mixed = nt(grad_attn, b_out[...]).astype(BF16)
        loads[2].wait()
        work = [(seq, pair) for seq in range(seqs) for pair in range(PAIRS)]
        allowed = [slot_rule(valid[seq : seq + 1, :], cap) for seq in range(seqs)]
        pieces = [slot_pieces(packed, seq, pair, cap) for seq, pair in work]
        grads = [
            stacked(grad_mixed[seq * cap : (seq + 1) * cap, pair * LANES : (pair + 1) * LANES])
            for seq, pair in work
        ]
        scores = [jnp.where(allowed[w[0]], nt(p[0], p[1]), -1e30) for w, p in zip(work, pieces)]
        grad_probs = [nt(g, p[2]) for g, p in zip(grads, pieces)]
        grown = [jnp.exp(v - jnp.max(v, axis=-1, keepdims=True)) for v in scores]
        probs = [v / jnp.sum(v, axis=-1, keepdims=True) for v in grown]
        lows = [
            (p * (g - jnp.sum(p * g, axis=-1, keepdims=True))).astype(BF16) for p, g in zip(probs, grad_probs)
        ]
        for (seq, pair), piece, grad_head, prob, low in zip(work, pieces, grads, probs, lows):
            at = slice(seq * cap, (seq + 1) * cap)
            cols = slice(pair * LANES, (pair + 1) * LANES)
            packed_o[0, at, cols] = (unstacked(nn(low, piece[1])) * FACTOR).astype(BF16)
            packed_o[1, at, cols] = tn(low, piece[0]).astype(BF16)
            packed_o[2, at, cols] = tn(prob.astype(BF16), grad_head).astype(BF16)
        send(packed_o, packed_out)
        copies[0].wait()
        grad_normed = sum(nt(packed_o[n], b_qkv[:, n * width : (n + 1) * width]) for n in range(3))
        back, gain_attn_sum = norm_back(grad_normed, chosen, mean_square_scale(chosen), gain_attn[...])
        chosen_o[...] = grad_rows + back + logit * router[...].reshape(1, -1)
        small_o[...] = jnp.zeros(small_o.shape, F32)
        small_o[0:1, :] = jnp.sum(logit * chosen, axis=0, keepdims=True)
        small_o[1:2, :] = gain_mlp_sum
        small_o[2:3, :] = gain_attn_sum
        for copy in sends:
            copy.wait()


def dense_gain(info, local, swapped, row):
    first = swapped.shape[0] - EXTRA + row
    far = sum(swapped[first + n : first + n + 1, :].astype(F32) for n in (0, 2, 4))
    return jnp.where(info[0] == 1, local[...], far)


def dense_in_body(
    info, x, near, away, picks, gain, w_local, w_far, middle_o, normed_o, packed_o, sel_o, b_qkv, sem
):
    step = pl.program_id(0)

    @pl.when(step == 0)
    def _():
        fetch(info, w_local, w_far, b_qkv, sem)

    rows, width = x.shape
    cap = near.shape[0]
    delta = jnp.where(info[0] == 0, near[...], away[:cap, :])
    place = step * rows + lax.broadcasted_iota(jnp.int32, (rows, cap), 0)
    hot = (picks[pl.ds(info[0], 1), :] == place).astype(BF16)
    middle = x[...].astype(F32) + nn(hot, delta)
    middle_o[...] = middle

    @pl.when(step == 0)
    def _():
        sel_o[...] = delta.astype(F32)

    sel_o[...] += tn(hot, x[...])
    normed = (middle * mean_square_scale(middle) * dense_gain(info, gain, away, 0)).astype(BF16)
    normed_o[...] = normed

    @pl.when(step == 0)
    def _():
        arrived(w_local, b_qkv, sem)

    for n in range(3):
        packed_o[n] = nn(normed, b_qkv[:, n * width : (n + 1) * width]).astype(BF16)


def attend_forward_body(info, packed, mixed_o, logsum_o):
    seq_len = packed.shape[1]
    tile = 2 * TILE
    queries = packed[0] * BF16(FACTOR)
    keys = packed[1]
    ones = jnp.ones((seq_len, LANES), BF16)
    values = [jnp.concatenate([head_only(packed[2], h), ones], axis=1) for h in range(2)]
    below = lax.broadcasted_iota(jnp.int32, (tile, tile), 1) <= lax.broadcasted_iota(jnp.int32, (tile, tile), 0)
    for first in range(0, seq_len, tile):
        upto = first + tile
        at = slice(first, upto)
        scores = []
        for head in range(2):
            score = nt(head_only(queries[at], head), keys[:upto])
            last = jnp.where(below, score[:, first:], -1e30)
            scores.append(jnp.concatenate([score[:, :first], last], axis=1) if first else last)
        tops = [jnp.max(score, axis=-1, keepdims=True) for score in scores]
        grown = [jnp.exp(score - top).astype(BF16) for score, top in zip(scores, tops)]
        outs = [nn(g, value[:upto]) for g, value in zip(grown, values)]
        mixed = sum(out[:, :LANES] * (1.0 / out[:, LANES:]) for out in outs)
        mixed_o[at, :] = mixed.astype(BF16)
        sums = [top + jnp.log(out[:, LANES:]) for top, out in zip(tops, outs)]
        turned = jnp.transpose(jnp.where(top_lanes(tile), sums[0], sums[1]))
        logsum_o[0, 0:1, at] = turned[0:1]
        logsum_o[0, 1:2, at] = turned[HEAD_DIM : HEAD_DIM + 1]


def attend_backward_body(info, packed, grad, mixed, logsum, picks, *refs):
    out, sel_o, grad_q = refs[-3:]
    seq_len = packed.shape[1]
    queries = packed[0] * BF16(FACTOR)
    queries = [head_only(queries, h) for h in range(2)]
    key_heads = [head_only(packed[1], h) for h in range(2)]
    grads = [head_only(grad[...], h) for h in range(2)]
    product = grad[...].astype(F32) * mixed[...].astype(F32)
    pick_row = lax.broadcasted_iota(jnp.int32, (8, LANES), 0)
    pick_lane = lax.broadcasted_iota(jnp.int32, (8, LANES), 1)
    pick = (pick_row == pick_lane // HEAD_DIM).astype(F32)
    inner = lax.dot_general(
        pick, product, (((1,), (1,)), ((), ())), precision=lax.Precision.HIGHEST, preferred_element_type=F32
    )
    above = lax.broadcasted_iota(jnp.int32, (TILE, TILE), 0) <= lax.broadcasted_iota(
        jnp.int32, (TILE, TILE), 1
    )
    for first in range(0, seq_len, TILE):
        kat = slice(first, first + TILE)
        keys = packed[1, kat, :]
        values = packed[2, kat, :]
        dks, dvs, dqs = [], [], []
        for head in range(2):
            query = queries[head][first:]
            grad_head = grads[head][first:]
            probs = jnp.exp(nt(keys, query) - logsum[0, head : head + 1, first:])
            edge = jnp.where(above, probs[:, :TILE], 0.0)
            probs = jnp.concatenate([edge, probs[:, TILE:]], axis=1) if first + TILE < seq_len else edge
            grad_probs = nt(values, grad_head)
            low = (probs * (grad_probs - inner[head : head + 1, first:])).astype(BF16)
            dvs.append(nn(probs.astype(BF16), grad_head))
            dks.append(nn(low, query))
            dqs.append(tn(low, key_heads[head][kat]))
        if first == 0:
            grad_q[...] = dqs[0] + dqs[1]
        else:
            grad_q[first:, :] += dqs[0] + dqs[1]
        out[1, kat, :] = (dks[0] + dks[1]).astype(BF16)
        out[2, kat, :] = (dvs[0] + dvs[1]).astype(BF16)
    out[0] = (grad_q[...] * FACTOR).astype(BF16)
    cap = picks.shape[1]
    place = lax.broadcasted_iota(jnp.int32, (seq_len, cap), 0)
    hot = (picks[pl.ds(info[0], 1), :] == place).astype(BF16)
    for n in range(3):
        sel_o[n] = tn(hot, out[n]).astype(BF16)


def feed_body(
    info, mixed, normed, middle, out_grad, gain_in, swapped, picks, middle_sel, wo_l, wo_f, wi_l, wi_f, wb_l, wb_f,
    pack_o, act_o, hidden_o, mid_o, carry_o, mixed_o, gain_o, sel_o,
    b_out, b_in, b_back, sems,
):
    step = pl.program_id(0)
    width = middle.shape[1]
    starts = range(0, b_in.shape[1], width)

    @pl.when(step == 0)
    def _():
        fetch(info, wo_l, wo_f, b_out, sems.at[0])
        for n, first in enumerate(starts):
            cols = pl.ds(first, width)
            fetch(info, wi_l.at[:, cols], wi_f.at[:, cols], b_in.at[:, cols], sems.at[1 + 2 * n])
            fetch(info, wb_l.at[cols], wb_f.at[cols], b_back.at[cols], sems.at[2 + 2 * n])
        gain_o[...] = jnp.zeros(gain_o.shape, F32)
        sel_o[0] = jnp.zeros(middle_sel.shape, F32)
        sel_o[1] = middle_sel[...]
        arrived(wo_l, b_out, sems.at[0])

    gain = dense_gain(info, gain_in, swapped, 1)
    pack_o[2] = mixed[...]
    pack_o[3] = normed[...]
    rows = middle[...] + nn(mixed[...], b_out[...])
    scale = mean_square_scale(rows)
    normed_mid = (rows * scale * gain).astype(BF16)
    mid_o[...] = normed_mid
    grad_ffn = out_grad[...]

    def hidden_block(first):
        cols = slice(first, first + width)
        act, slope = gelu_parts(nn(mid_o[...], b_in[:, cols]))
        act_o[:, cols] = act.astype(BF16)
        hidden_o[:, cols] = (nt(out_grad[...], b_back[cols, :]) * slope).astype(BF16)

    @pl.when(step == 0)
    def _():
        for n, first in enumerate(starts):
            cols = pl.ds(first, width)
            arrived(wi_l.at[:, cols], b_in.at[:, cols], sems.at[1 + 2 * n])
            arrived(wb_l.at[cols], b_back.at[cols], sems.at[2 + 2 * n])
            hidden_block(first)

    @pl.when(step > 0)
    def _():
        for first in starts:
            hidden_block(first)

    pack_o[0] = (rows + nn(act_o[...], b_back[...])).astype(BF16)
    grad_mid = nt(hidden_o[...], b_in[...])
    back, gain_sum = norm_back(grad_mid, rows, scale, gain)
    carry = grad_ffn.astype(F32) + back
    carry_o[...] = carry
    grad_attn = carry.astype(BF16)
    pack_o[1] = grad_attn
    mixed_o[...] = nt(grad_attn, b_out[...]).astype(BF16)
    gain_o[3:4, :] += gain_sum
    count, cap = carry.shape[0], middle_sel.shape[0]
    place = step * count + lax.broadcasted_iota(jnp.int32, (count, cap), 0)
    hot = (picks[pl.ds(info[0], 1), :] == place).astype(BF16)
    sel_o[0] += tn(hot, grad_attn) + tn(hot, (carry - grad_attn.astype(F32)).astype(BF16))


def dense_out_body(
    info, packed, carry, middle, gain_in, swapped, w_local, w_far, grad_o, gain_o, b_qkv, sem
):
    step = pl.program_id(0)

    @pl.when(step == 0)
    def _():
        fetch(info, w_local, w_far, b_qkv, sem)
        gain_o[...] = jnp.zeros(gain_o.shape, F32)
        arrived(w_local, b_qkv, sem)

    width = middle.shape[1]
    grad_normed = sum(nt(packed[n], b_qkv[:, n * width : (n + 1) * width]) for n in range(3))
    rows = middle[...]
    gain = dense_gain(info, gain_in, swapped, 0)
    back, gain_sum = norm_back(grad_normed, rows, mean_square_scale(rows), gain)
    gain_o[4:5, :] += gain_sum
    grad_o[...] = (carry[...] + back).astype(BF16)


def ends_body(info, result_block, grad, far_block, far_grad, grad_chosen, picks, out):
    seq = pl.program_id(0)
    step = pl.program_id(1)

    @pl.when(info[0] == 1)
    def _():
        out[...] = jnp.where(seq == 1, result_block[0], far_block[0])

    @pl.when(info[0] == 0)
    def _():
        base = jnp.where(seq == 0, grad[...], far_grad[...]).astype(F32)
        rows = out.shape[0]
        cap = grad_chosen.shape[0]
        place = step * rows + lax.broadcasted_iota(jnp.int32, (rows, cap), 0)
        hot = (picks[pl.ds(seq, 1), :] == place).astype(BF16)
        high = grad_chosen[...].astype(BF16)
        low = (grad_chosen[...] - high.astype(F32)).astype(BF16)
        out[...] = (base + (nn(hot, high) + nn(hot, low))).astype(BF16)


def feed_grad_body(
    info, mid, hidden, act, out_grad, out, mid_b, grad_b, hidden_b, act_b, ring_in, ring_back, in_sems, out_sems
):
    steps, rows, width = hidden_b.shape
    piece = width // PIECES

    def load(source, target, n):
        return pltpu.make_async_copy(source, target, in_sems.at[n])

    mine = pl.ds(pl.multiple_of(info[0] * rows, rows), rows)
    loads = [load(mid, mid_b, 0)]
    loads += [load(hidden.at[:, pl.ds(t * width, width)], hidden_b.at[t], 1 + t) for t in range(steps)]
    loads += [load(out_grad.at[mine], grad_b, 1 + steps)]
    loads += [load(act.at[:, pl.ds(t * width, width)], act_b.at[t], 2 + steps + t) for t in range(steps)]
    for copy in loads:
        copy.start()
    sent = []
    for n in range(2 * steps):
        t = n % steps
        if t == 0:
            loads[0 if n == 0 else 1 + steps].wait()
        loads[1 + t if n < steps else 2 + steps + t].wait()
        product = tn(mid_b[...], hidden_b[t]) if n < steps else tn(act_b[t], grad_b[...])
        ring = ring_in if n < steps else ring_back
        if t >= 2:
            sent[n - 2].wait()
        ring[n % 2] = product.astype(BF16).reshape(ring.shape[1:])
        target = out.at[1, :, :, pl.ds(t * piece, piece)] if n < steps else out.at[0, t]
        sent.append(pltpu.make_async_copy(ring.at[n % 2], target, out_sems.at[n // steps, n % 2]))
        sent[-1].start()
    for n in (steps - 2, steps - 1, 2 * steps - 2, 2 * steps - 1):
        sent[n].wait()


def origin(info, base, place):
    relative = 0
    for stage in range(STAGES):
        if place >> (STAGES - 1 - stage) & 1:
            relative = relative | (1 << info[base + stage])
    return info[1] ^ relative


def put_block(info, outs, product, slot, spot, ring, sems):
    piece = product.shape[0] // PIECES
    ring[spot] = product.astype(BF16)
    half = PIECES // 2
    sent = []
    for place in range(PIECES):
        rows = pl.ds(pl.multiple_of(origin(info, SIDE, place) * piece, piece), piece)
        target = outs[place // half].at[place % half, pl.ds(slot * piece, piece)]
        sent.append(pltpu.make_async_copy(ring.at[spot, rows], target, sems.at[slot, place]))
        sent[-1].start()
    return sent


def side_grad_body(
    info, normed0, packed0, mixed0, attn0,
    p_near, p_far, near, far,
    out_stay, out_go,
    n_buf, p_buf, m_buf, a_buf, ring, sems, out_sems,
):
    outs = (out_stay, out_go)

    def put_all(order, product):
        sent = []
        for n, slot in enumerate(order):
            value = product(slot)
            if n >= 2:
                for copy in sent[n - 2]:
                    copy.wait()
            sent.append(put_block(info, outs, value, slot, n % 2, ring, out_sems))
        for copies in sent[-2:]:
            for copy in copies:
                copy.wait()

    @pl.when(info[0] == 0)
    def _():
        put_all((3, 0, 1, 2), lambda n: tn(normed0[...], packed0[n]) if n < 3 else tn(mixed0[...], attn0[...]))

    @pl.when(info[0] == 1)
    def _():
        sources = [
            (source.at[which], target, n)
            for which, target in ((2, m_buf), (1, a_buf), (3, n_buf))
            for n, source in enumerate((near, far))
        ]
        copies = [
            pltpu.make_async_copy(source, target.at[n], sems.at[k])
            for k, (source, target, n) in enumerate(sources)
        ]
        blocks = [
            pltpu.make_async_copy(source.at[which], p_buf.at[n, which], sems.at[6 + 2 * which + n])
            for which in range(3)
            for n, source in enumerate((p_near, p_far))
        ]
        for copy in copies + blocks:
            copy.start()

        def product(n):
            if n == 3:
                for copy in copies[:4]:
                    copy.wait()
                return tn(m_buf[0], a_buf[0]) + tn(m_buf[1], a_buf[1])
            for copy in (copies[4:] if n == 0 else []) + blocks[2 * n : 2 * n + 2]:
                copy.wait()
            return tn(n_buf[0], p_buf[0, n]) + tn(n_buf[1], p_buf[1, n])

        put_all((3, 0, 1, 2), product)


def quad_grad_body(
    info, stay, from_x, from_y, from_xy, g_own, g_x, g_y, g_xy, w_back, go_o, stay_o,
    b_back, acts, slopes, mids, grads, hidden, held, sems, out_sems,
):
    @pl.when(info[0] == 0)
    def _():
        rows = g_own.shape[0]
        width = grads.shape[1]
        sub = acts.shape[0]
        steps = b_back.shape[0] // width
        piece = sub // QUAD
        count = mids.shape[0] // QUAD
        copies = []

        def load(source, target, n, k):
            copies.append(pltpu.make_async_copy(source, target, sems.at[n, k]))
            copies[-1].start()
            return copies[-1]

        first = [load(g, grads.at[pl.ds(n * rows, rows)], 0, n) for n, g in enumerate((g_own, g_x, g_y, g_xy))]
        parts = (stay, from_x, from_y, from_xy)
        blocks, lefts = [], []
        for t in range(steps):
            at = pl.ds(t * width, width)
            blocks.append([load(w_back.at[at], b_back.at[at], 1 + t, QUAD)])
            for n, source in enumerate(parts):
                here = pl.ds(sub + QUAD * count + t * width, width)
                blocks[t].append(load(source.at[here], slopes.at[at, pl.ds(n * rows, rows)], 1 + t, n))
        for n, source in enumerate(parts):
            to = pl.ds(n * rows, rows)
            lefts.append(load(source.at[pl.ds(0, sub)], acts.at[:, to], 1 + steps, n))
            lefts.append(load(source.at[pl.ds(sub, QUAD * count)], mids.at[:, to], 2 + steps, n))
        for copy in first:
            copy.wait()
        for t in range(steps):
            at = slice(t * width, (t + 1) * width)
            for copy in blocks[t]:
                copy.wait()
            hidden[at, :] = (nt(b_back[at, :], grads[...]) * slopes[at, :].astype(F32)).astype(BF16)
        for copy in lefts:
            copy.wait()
        layer = info[1] >> 2

        def put(z, rows_at, value):
            place = layer ^ z
            place = ((place & 1) << 1) | (place >> 1)

            held[place, rows_at, :] = value

        product = nn(acts[...], grads[...]).astype(BF16)
        for z in range(QUAD):
            put(z, slice(0, piece), product[z * piece : (z + 1) * piece, :])
        for t in range(steps):
            product = nt(mids[...], hidden[t * width : (t + 1) * width, :]).astype(BF16)
            for z in range(QUAD):
                put(z, slice(piece + t * count, piece + (t + 1) * count), product[z * count : (z + 1) * count, :])
        outs = [
            pltpu.make_async_copy(held.at[pl.ds(first, 2)], out, out_sems.at[n])
            for n, (first, out) in enumerate(((2, go_o), (0, stay_o)))
        ]
        for copy in outs:
            copy.start()
        for copy in outs:
            copy.wait()


def feed_grad(info, mid, hidden, act, out_grad):
    depth, width = mid.shape
    steps = hidden.shape[1] // width
    piece = width // PIECES
    return run(
        feed_grad_body,
        info,
        [(v, ANY) for v in (mid, hidden, act, out_grad)],
        [(shape((2, QUAD, QUAD, steps * piece, width), BF16), ANY)],
        (1,),
        [
            pltpu.VMEM((depth, width), BF16),
            pltpu.VMEM((depth, width), BF16),
            pltpu.VMEM((steps, depth, width), BF16),
            pltpu.VMEM((steps, depth, width), BF16),
            pltpu.VMEM((2, QUAD, QUAD, piece, width), BF16),
            pltpu.VMEM((2, QUAD, steps * piece, width), BF16),
            pltpu.SemaphoreType.DMA((2 + 2 * steps,)),
            pltpu.SemaphoreType.DMA((2, 2)),
        ],
        flops=4 * depth * steps * width * width,
        moved=4 * (depth + depth * steps + steps * width) * width,
    )[0]


def side_grad(info, routed, dense):
    _, depth, width = dense[0].shape
    half = PIECES // 2
    piece = width // PIECES

    dims = (half, 4 * piece, width)
    return run(
        side_grad_body,
        info,
        [(v, whole(v.shape)) for v in routed] + [(v, ANY) for v in dense],
        [(shape(dims, BF16), ANY)] * 2,
        (1,),
        [
            pltpu.VMEM((2, depth, width), BF16),
            pltpu.VMEM((2, 3, depth, width), BF16),
            pltpu.VMEM((2, depth, width), BF16),
            pltpu.VMEM((2, depth, width), BF16),
            pltpu.VMEM((2, width, width), BF16),
            pltpu.SemaphoreType.DMA((12,)),
            pltpu.SemaphoreType.DMA((4, PIECES)),
        ],
        flops=16 * depth * width * width,
        moved=24 * depth * width,
    )


def quad_grad(info, parts, grads, w_back):
    hidden, width = w_back.shape
    rows = grads[0].shape[0]
    sub = hidden // QUAD
    dims = (2, 2 * sub // QUAD, width)
    total = QUAD * rows
    return run(
        quad_grad_body,
        info,
        [(v, ANY) for v in parts + grads + [w_back]],
        [(shape(dims, BF16), ANY)] * 2,
        (1,),
        [
            pltpu.VMEM((hidden, width), BF16),
            pltpu.VMEM((sub, total), BF16),
            pltpu.VMEM((hidden, total), BF16),
            pltpu.VMEM((parts[0].shape[0] - sub - hidden, total), BF16),
            pltpu.VMEM((total, width), BF16),
            pltpu.VMEM((hidden, total), BF16),
            pltpu.VMEM((QUAD, *dims[1:]), BF16),
            pltpu.SemaphoreType.DMA((3 + hidden // width, 1 + QUAD)),
            pltpu.SemaphoreType.DMA((2,)),
        ],
        flops=8 * sub * total * width,
        moved=10 * sub * total,
    )


def to_section(value, source):
    return lax.ppermute(value, "section", [(source, 1 - source)])


def swap_section(value):
    return lax.ppermute(value, "section", [(0, 1), (1, 0)])


def after(value, *earlier):
    return lax.optimization_barrier((value, *earlier))[0]


def added_up(parts):
    total = parts[0].astype(F32)
    for part in parts[1:]:
        total = total + part.astype(F32)
    return total


def cross(orders, value, stage):
    count = lax.axis_size("dp")
    low = count // PIECES
    pairs = []
    for section, order in enumerate(orders):
        base = section * count
        flip = low << order[stage]
        pairs += [(base + n, base + (n ^ flip)) for n in range(count)]
    return lax.ppermute(value, ("section", "dp"), pairs)


def cross_first(value, *axes):
    count = lax.axis_size("dp")
    flip = sum((count // PIECES) << axis for axis in axes)
    return lax.ppermute(value, ("section", "dp"), [(n, n ^ flip) for n in range(count)])


def scatter_layers(value):
    stride = QUAD * (lax.axis_size("dp") // PIECES)
    groups = [[base + n * stride for n in range(QUAD)] for base in range(stride)]
    return lax.psum_scatter(value, "dp", scatter_dimension=0, axis_index_groups=groups, tiled=True)


class Exchange:
    def __init__(self, stay, go, swap, stages):
        self.stay, self.go, self.swap = stay, go, swap
        self.stages, self.stage, self.flying = stages, 0, None

    def start(self, info):
        if self.stage:
            half = self.stay[0].shape[0] // 2
            self.go = [part[half:] for part in self.stay]
            self.stay = [part[:half] for part in self.stay]
        send = added_up(self.go).astype(BF16) if len(self.go) > 1 else self.go[0]
        info, send = lax.optimization_barrier((info, send))
        self.flying = self.swap(send, self.stage)
        self.stage += 1
        return info

    def total(self):
        assert self.stage == self.stages
        return added_up(self.stay)[0]


def settle(info, *values):
    arrays = [value.flying if isinstance(value, Exchange) else value for value in values]
    info, *arrays = lax.optimization_barrier((info, *arrays))
    plain = []
    for value, array in zip(values, arrays):
        if isinstance(value, Exchange):
            value.stay = value.stay + [array]
        else:
            plain.append(array)
    return (info, *plain)


def share_out(piece):
    count = lax.axis_size("dp")
    low = count // PIECES
    if low > 1:
        rows, cols = piece.shape
        place = lax.axis_index("dp") % low
        parts = jnp.take(piece.reshape(low, rows // low, cols), jnp.arange(low) ^ place, axis=0)
        while parts.shape[0] > 1:
            half = parts.shape[0] // 2
            far = lax.ppermute(parts[half:], "dp", [(n, n ^ half) for n in range(count)])
            parts = parts[:half] + far
        piece = parts[0]
    return piece[None]


def across(value, flip):
    return lax.ppermute(value, "dp", [(n, n ^ flip) for n in range(lax.axis_size("dp"))])


X, Y, Z, ZZ = 0, 1, 2, 3
ORDERS = ((X, Y, Z, ZZ), (Y, X, Z, ZZ))
SIDE = 2


def shards(inputs, out_grad, picks, valid, router, gain_attn, w_qkv, w_out, gain_mlp, w_in, w_back):
    w_qkv, w_out, w_in, w_back = w_qkv[0], w_out[0], w_in[0], w_back[0]
    seqs, cap = picks.shape
    seq_len = inputs.shape[0] // seqs
    width = inputs.shape[1]
    hidden = w_in.shape[1]
    rows = seqs * cap
    tiles = seq_len // TILE
    section = lax.axis_index("section")
    spot = lax.axis_index("dp") // (lax.axis_size("dp") // PIECES)
    first = section == 0

    table = [(mine, 0) + ORDERS[mine] for mine in (0, 1)]
    facts = jnp.where(first, jnp.array(table[0]), jnp.array(table[1]))
    info = jnp.where(jnp.arange(len(table[0])) == 1, spot, facts).astype(jnp.int32)

    far_qkv = to_section(w_qkv, 1)
    far_out = to_section(w_out, 1)
    far_in = to_section(w_in, 1)

    weight_bufs = [pltpu.VMEM(w.shape, BF16) for w in (w_qkv, w_out, w_in, w_back)]
    weight_bufs.append(pltpu.SemaphoreType.DMA((4,)))
    weight_ins = [(w_qkv, ANY), (w_out, ANY), (w_in, ANY), (w_back, ANY)]

    def full(array):
        return (array, whole(array.shape))

    def made(dims, dtype):
        return (shape(dims, dtype), whole(dims))

    routed_flops = 2 * rows * (4 * width * width + 2 * width * hidden)
    weight_bytes = 2 * (4 * width * width + 2 * width * hidden)
    sub = hidden // QUAD
    kept = [
        shape((rows, width), BF16),
        shape((rows, width), BF16),
        shape((rows, 3 * width), BF16),
        shape((rows, width), BF16),
        shape((rows, width), F32),
        shape((rows, hidden), BF16),
        shape((rows, width), F32),
    ]
    (
        gate0, open0, near, away, chosen, normed0, packed0, mixed0, rows0, slope0, branch0,
        stay0, over_x, over_y, over_xy,
    ) = run(
        routed_forward_body,
        info,
        [(inputs, ANY)] + [full(v) for v in (picks, valid, gain_attn, gain_mlp, router)] + weight_ins,
        [
            made((rows, LANES), F32),
            made((rows, LANES), F32),
            made((cap, width), BF16),
            made((cap + EXTRA, width), BF16),
        ]
        + [(v, ANY) for v in kept]
        + [(shape((sub + width // QUAD + hidden, rows), BF16), ANY)] * QUAD,
        (1,),
        [pltpu.VMEM(v.shape, v.dtype) for v in kept]
        + [pltpu.VMEM(inputs.shape, BF16)]
        + weight_bufs[:4]
        + [pltpu.VMEM((rows, hidden), BF16), pltpu.VMEM((QUAD, sub + width // QUAD, rows), BF16), pltpu.VMEM((hidden, rows), BF16)]
        + weight_bufs[4:]
        + [pltpu.SemaphoreType.DMA((seqs,)), pltpu.SemaphoreType.DMA((len(kept) + 2 * QUAD,))],
        flops=routed_flops,
        moved=weight_bytes,
    )
    info, far_qkv, far_out, far_in, near, away, over_x, over_y, over_xy, w_back_now = settle(
        info, far_qkv, far_out, far_in, near, away, over_x, over_y, over_xy, w_back
    )
    away = swap_section(away)

    def row_tile(dims):
        return pl.BlockSpec(dims, lambda i, info_ref: (i, 0))

    def seq_tile(tile=TILE):
        return pl.BlockSpec((tile, width), lambda i, info_ref: (info_ref[0] * (seq_len // tile) + i, 0))

    def tiled(cols, dtype, tile=TILE):
        return (shape((seq_len, cols), dtype), row_tile((tile, cols)))

    three_tile = pl.BlockSpec((3, WIDE, width), lambda i, info_ref: (0, i, 0))
    three_low = pl.BlockSpec((3, TILE, width), lambda i, info_ref: (0, i, 0))
    three = shape((3, seq_len, width), BF16)

    middle, normed1, packed1, middle_sel = run(
        dense_in_body,
        info,
        [
            (inputs, seq_tile(WIDE)),
            full(near),
            full(away),
            full(picks),
            full(gain_attn),
            (w_qkv, ANY),
            (far_qkv, ANY),
        ],
        [tiled(width, F32, WIDE), tiled(width, BF16, WIDE), (three, three_tile), made((cap, width), F32)],
        (seq_len // WIDE,),
        [pltpu.VMEM(w_qkv.shape, BF16), pltpu.SemaphoreType.DMA],
        flops=6 * seq_len * width * width,
        moved=seq_len * width * 12 + 6 * width * width,
    )

    info, packed1, over_x, over_y, over_xy, w_back_now = settle(
        info, packed1, over_x, over_y, over_xy, w_back_now
    )
    far_back = to_section(w_back_now, 1)
    from_x = cross_first(over_x, X)
    from_y = cross_first(over_y, Y)
    from_xy = cross_first(over_xy, X, Y)

    pair_spec = pl.BlockSpec((3, seq_len, LANES), lambda h, info_ref: (0, 0, h))
    column_spec = pl.BlockSpec((seq_len, LANES), lambda h, info_ref: (0, h))
    logsum_spec = pl.BlockSpec((1, 8, seq_len), lambda h, info_ref: (h, 0, 0))
    attend_flops = 2 * HEADS * seq_len * seq_len * TILE
    mixed1, logsum1 = run(
        attend_forward_body,
        info,
        [(packed1, pair_spec)],
        [
            (shape((seq_len, width), BF16), column_spec),
            (shape((PAIRS, 8, seq_len), F32), logsum_spec),
        ],
        (PAIRS,),
        flops=attend_flops,
        moved=8 * seq_len * width,
    )

    info, mixed1, far_back = settle(info, mixed1, far_back)
    pack1, act1, hidden1, mid1, carry, grad_mixed1, gain_mlp_sum, carried = run(
        feed_body,
        info,
        [
            (mixed1, row_tile((TILE, width))),
            (normed1, row_tile((TILE, width))),
            (middle, row_tile((TILE, width))),
            (out_grad, seq_tile()),
            full(gain_mlp),
            full(away),
            full(picks),
            full(middle_sel),
            (w_out, ANY),
            (far_out, ANY),
            (w_in, ANY),
            (far_in, ANY),
            (w_back, ANY),
            (far_back, ANY),
        ],
        [
            (shape((4, seq_len, width), BF16), pl.BlockSpec((4, TILE, width), lambda i, info_ref: (0, i, 0))),
            tiled(hidden, BF16),
            tiled(hidden, BF16),
            tiled(width, BF16),
            tiled(width, F32),
            tiled(width, BF16),
            made((8, width), F32),
            made((2, cap, width), F32),
        ],
        (tiles,),
        [
            pltpu.VMEM(w_out.shape, BF16),
            pltpu.VMEM(w_in.shape, BF16),
            pltpu.VMEM(w_back.shape, BF16),
            pltpu.SemaphoreType.DMA((1 + 2 * hidden // width,)),
        ],
        flops=2 * seq_len * width * (2 * width + 4 * hidden),
        moved=seq_len * (20 * width + 4 * hidden) + 2 * width * (width + 2 * hidden),
    )
    info, mid1, pack1, carried, from_x, from_y, from_xy = settle(info, mid1, pack1, carried, from_x, from_y, from_xy)
    feed = feed_grad(info, mid1, hidden1, act1, out_grad)
    info, feed = settle(info, feed)
    feed = lax.psum_scatter(feed.reshape(-1, width), "section", scatter_dimension=0, tiled=True)

    def attend_backward(info, start, held):
        def third(rows):
            return pl.BlockSpec((3, rows, LANES), lambda h, info_ref: (0, 0, start + h))

        column = pl.BlockSpec((seq_len, LANES), lambda h, info_ref: (0, start + h))
        logsums = pl.BlockSpec((1, 8, seq_len), lambda h, info_ref: (start + h, 0, 0))
        return run(
            attend_backward_body,
            info,
            [(packed1, third(seq_len)), (grad_mixed1, column), (mixed1, column), (logsum1, logsums), full(picks)]
            + [(v, ANY) for v in held],
            [(three, third(seq_len)), (shape((3, cap, width), BF16), third(cap))],
            (PAIRS // 2,),
            [pltpu.VMEM((seq_len, LANES), F32)],
            flops=5 * attend_flops // 4,
            moved=8 * seq_len * width,
            aliases={6: 0, 7: 1} if held else {},
        )

    held = attend_backward(info, 0, [])
    info, pack1, carried, *held = settle(info, pack1, carried, *held)
    far_pack = to_section(pack1, 0)
    far_carried = to_section(carried, 1)
    info, feed = settle(info, feed)
    feed = scatter_layers(feed)
    packed_grad1, packed_sel = attend_backward(info, PAIRS // 2, held)
    info, packed_grad1, packed_sel, far_pack, far_carried = settle(
        info, packed_grad1, packed_sel, far_pack, far_carried
    )
    far_packed_sel = to_section(packed_sel, 1)
    info, far_packed_sel, packed_grad1 = settle(info, far_packed_sel, packed_grad1)
    far_packed = to_section(packed_grad1, 0)

    made_back = [shape((rows, width), BF16), shape((rows, width), BF16), shape((3, rows, width), BF16)]
    grad_chosen, small0, g_own, attn0, packed_grad0 = run(
        routed_backward_body,
        info,
        [
            full(v)
            for v in (
                packed_sel, far_packed_sel, carried, far_carried,
                chosen, branch0, gate0, valid, gain_attn, gain_mlp, router, away,
            )
        ]
        + [(v, ANY) for v in (packed0, rows0, slope0, far_qkv)]
        + weight_ins,
        [made((rows, width), F32), made((8, width), F32)] + [(v, ANY) for v in made_back],
        (1,),
        weight_bufs[:4]
        + [pltpu.VMEM((rows, hidden), BF16)]
        + [pltpu.VMEM(v.shape, v.dtype) for v in (packed0, rows0, slope0, *made_back)]
        + [pltpu.SemaphoreType.DMA((5,)), pltpu.SemaphoreType.DMA((3,)), pltpu.SemaphoreType.DMA((3,))],
        flops=routed_flops,
        moved=weight_bytes,
    )
    info, small0, packed_grad0, far_packed, g_own = settle(info, small0, packed_grad0, far_packed, g_own)
    g_x = cross_first(g_own, X)
    g_y = cross_first(g_own, Y)
    g_xy = cross_first(g_own, X, Y)

    side_stay, side_go = side_grad(
        info,
        [normed0, packed_grad0, mixed0, attn0],
        [packed_grad1, far_packed, pack1, far_pack],
    )
    info, side_go, g_x, g_y, g_xy = settle(info, side_go, g_x, g_y, g_xy)
    side = Exchange([side_stay], [side_go], functools.partial(cross, ORDERS), STAGES)
    info = side.start(info)

    grad_middle, gain_attn_sum = run(
        dense_out_body,
        info,
        [
            (packed_grad1, three_low),
            (carry, row_tile((TILE, width))),
            (middle, row_tile((TILE, width))),
            full(gain_attn),
            full(away),
            (w_qkv, ANY),
            (far_qkv, ANY),
        ],
        [tiled(width, BF16), made((8, width), F32)],
        (tiles,),
        [pltpu.VMEM(w_qkv.shape, BF16), pltpu.SemaphoreType.DMA],
        flops=6 * seq_len * width * width,
        moved=seq_len * width * 16 + 6 * width * width,
    )
    info, grad_middle, gain_attn_sum = settle(info, grad_middle, gain_attn_sum)
    small = jnp.where(first, small0, 0.0) + gain_mlp_sum + gain_attn_sum
    small_far = across(small, 8)
    quad_go, quad_stay = quad_grad(
        info, [stay0, from_x, from_y, from_xy],
        [g_own, g_x, g_y, g_xy], w_back,
    )
    info, quad_go, small_far, feed, grad_middle = settle(info, quad_go, small_far, feed, grad_middle, side)
    info = side.start(info)
    far_grad = to_section(grad_middle, 1)
    small = after(small + small_far, info)
    small_far = across(small, 2)
    quad = Exchange([quad_stay], [quad_go], lambda value, stage: cross_first(value, (Z, ZZ)[stage]), 2)
    info = quad.start(info)
    far_places = jnp.where(first, jnp.array([0, 2, 1, 3]), jnp.array([0, 1, 2, 3])) ^ (spot & 3)
    feed = jnp.take(feed.reshape(QUAD, -1, width), far_places, axis=0)
    feed = Exchange([feed[:2]], [feed[2:]], functools.partial(cross, ORDERS), 2)
    info = feed.start(info)

    def end_spec(core, seq, paired):
        def at(s, i, info_ref):
            step = jnp.where((info_ref[0] == core) & (s == seq), i, 0)
            return (0, step, 0) if paired else (step, 0)

        return pl.BlockSpec((1, WIDE, width) if paired else (WIDE, width), at)

    ends = run(
        ends_body,
        info,
        [
            (pack1, end_spec(1, 1, True)),
            (grad_middle, end_spec(0, 0, False)),
            (far_pack, end_spec(1, 0, True)),
            (far_grad, end_spec(0, 1, False)),
            (grad_chosen, pl.BlockSpec((cap, width), lambda s, i, info_ref: (s, 0))),
            (picks, pl.BlockSpec((seqs, cap), lambda s, i, info_ref: (0, 0))),
        ],
        [
            (
                shape((seqs * seq_len, width), BF16),
                pl.BlockSpec((WIDE, width), lambda s, i, info_ref: (s * (seq_len // WIDE) + i, 0)),
            )
        ],
        (seqs, seq_len // WIDE),
        flops=4 * seqs * seq_len * cap * width,
        moved=8 * seqs * seq_len * width,
    )[0]

    info, ends = settle(info, ends, side)
    info = side.start(info)
    info, = settle(info, quad)
    info = quad.start(info)
    info, small_far = settle(info, small_far, feed)
    small = after(small + small_far, info)
    small_far = across(small, 4)
    info = feed.start(info)
    info, small_far = settle(info, small_far, side)
    info = side.start(info)
    small = after(small + small_far, info)
    small_far = across(small, 1)
    info, = settle(info, feed)
    feed1 = feed.total()
    back1 = to_section(feed1.astype(BF16), 0).astype(F32)
    info, small_far, back1 = settle(info, small_far, back1)
    small = small + small_far
    small_far = swap_section(small)
    info, small_far = settle(info, small_far, quad)

    def gain_share(routed_row, dense_row):
        row = jnp.where(first, small[routed_row], small[dense_row])
        return lax.dynamic_slice_in_dim(row, lax.axis_index("dp") * share, share)[None]

    piece = width // PIECES
    small = small + small_far
    flip = PIECES
    while flip < lax.axis_size("dp"):
        small = small + across(small, flip)
        flip *= 2
    share = width // lax.axis_size("dp")
    quad_sum = quad.total()
    back0, in0 = quad_sum[: hidden // PIECES], quad_sum[hidden // PIECES :]
    in0 = in0.reshape(QUAD, piece, width).transpose(1, 0, 2).reshape(piece, hidden)

    in1 = feed1.reshape(QUAD, piece, width).transpose(1, 0, 2).reshape(piece, hidden)
    w_in_out = share_out(jnp.where(first, in0, in1))
    w_back_out = share_out(jnp.where(first, back0, back1))
    gain_attn_out, gain_mlp_out = gain_share(2, 4), gain_share(1, 3)
    info, w_in_out, w_back_out, gain_attn_out, gain_mlp_out, small = settle(
        info, w_in_out, w_back_out, gain_attn_out, gain_mlp_out, small, side
    )
    attend_sum = side.total()
    return (
        ends[None],
        small[0],
        gain_attn_out,
        share_out(jnp.concatenate([attend_sum[n : n + piece] for n in range(0, 3 * piece, piece)], axis=1)),
        share_out(attend_sum[3 * piece :]),
        gain_mlp_out,
        w_in_out,
        w_back_out,
    )


def solution(mesh):
    placed = (
        P("dp", None),
        P("dp", None),
        P("dp", None),
        P("dp", None),
        P(),
        P("section", None),
        P("section", None, None),
        P("section", None, None),
        P("section", None),
        P("section", None, None),
        P("section", None, None),
    )
    return jax.shard_map(
        shards,
        mesh=mesh,
        in_specs=placed,
        out_specs=(
            P("section", "dp", None),
            P(),
            P("section", "dp"),
            P("section", "dp", None),
            P("section", "dp", None),
            P("section", "dp"),
            P("section", "dp", None),
            P("section", "dp", None),
        ),
        check_vma=False,
    )
```
